32 devices in a mesh: wide: 8 (over z, y), narrow: 4 (over x, core).
Axes of the slice: x: 2, y: 2, z: 4, core: 2. Of those that a mesh axis runs over, the one named last changes fastest.
Arguments:
- tokens: bfloat16 [4, 4096, 1024], P('narrow', 'wide'), may hold values from -6 to 6
- cotangent: bfloat16 [4, 4096, 1024], P('narrow', 'wide'), may hold values from -6 to 6
- lengths: int32 [4, 16], P('narrow'), may hold values from 0 to 4095, as said below
- decay_rate: float32 [8], replicated, may hold values from 0 to 0.034, as said below
- attn_gain: float32 [1024], replicated, may hold values from 0.1 to 1.9
- w_query: bfloat16 [1024, 1024], replicated, may hold values from -0.1875 to 0.1875
- w_key: bfloat16 [1024, 1024], replicated, may hold values from -0.1875 to 0.1875
- w_value: bfloat16 [1024, 1024], replicated, may hold values from -0.1875 to 0.1875
- w_gate: bfloat16 [1024, 1024], replicated, may hold values from -0.1875 to 0.1875
- w_out: bfloat16 [1024, 1024], replicated, may hold values from -0.1875 to 0.1875
- ffn_gain: float32 [1024], replicated, may hold values from 0.1 to 1.9
- w_left: bfloat16 [1024, 2816], P(None, 'narrow'), may hold values from -0.1875 to 0.1875
- w_right: bfloat16 [1024, 2816], P(None, 'narrow'), may hold values from -0.1875 to 0.1875
- w_down: bfloat16 [2816, 1024], P('narrow'), may hold values from -0.109375 to 0.109375
Outputs:
- output: bfloat16 [4, 4096, 1024], P('narrow', 'wide')
- grad_tokens: float32 [4, 4096, 1024], P('narrow', 'wide')
- grad_w_query: float32 [1024, 1024], replicated
- grad_w_key: float32 [1024, 1024], replicated
- grad_w_value: float32 [1024, 1024], replicated
- grad_w_gate: float32 [1024, 1024], replicated
- grad_w_out: float32 [1024, 1024], replicated
- grad_attn_gain: float32 [1024], replicated
- grad_ffn_gain: float32 [1024], replicated
- grad_w_left: float32 [1024, 2816], P(None, 'narrow')
- grad_w_right: float32 [1024, 2816], P(None, 'narrow')
- grad_w_down: float32 [2816, 1024], P('narrow')
The draws below stay inside these ranges and needn't reach their ends.
Inputs may be any that keep to these rules, and one draw needn't show every extreme that they name: lengths[r] holds the lengths of pack r's sequences in order, then zeros for unused slots; every pack closes with 1 to 255 padding positions; one pack holds a single sequence of 4095 positions. One position's decay of head h is exp(-decay_rate[h]).
All inputs are finite; a program needn't handle non-finite values.
Results may differ from the reference program's by a relative error of at most 0.019.
Values may be sent and summed in bfloat16 or wider, within the bound.
A program may use at most 192 MiB of HBM per device.

```python
import math
import jax
import jax.numpy as jnp
from jax import lax

D = 1024
H = 8
HDIM = 128
FF = 2816
SEQS = 16
TOK_DEV = 512
PACK = 4096
N_NARROW = 4


def draw_lengths(key, part):
    key = jax.random.fold_in(key, 11)
    first_key, second_key, third_key = jax.random.split(key, 3)
    raw_len = jax.random.randint(first_key, (N_NARROW, SEQS), 2 * TOK_DEV, 8 * TOK_DEV + 1)
    pad_len = jax.random.randint(second_key, (N_NARROW,), 1, TOK_DEV // 2)
    chosen = jax.random.randint(third_key, (), 0, N_NARROW)
    is_chosen = jnp.arange(N_NARROW) == chosen
    pad_len = jnp.where(is_chosen, 1, pad_len)
    first_slot = (jnp.arange(SEQS) == 0)[None, :]
    single = jnp.where(first_slot, PACK, 0)
    raw_len = jnp.where(is_chosen[:, None], single, raw_len)
    live_total = PACK - pad_len
    seq_ends = jnp.minimum(jnp.cumsum(raw_len, axis=1), live_total[:, None])
    seq_starts = jnp.concatenate([jnp.zeros((N_NARROW, 1), seq_ends.dtype), seq_ends[:, :-1]], axis=1)
    return (seq_ends - seq_starts).astype(jnp.int32)


def draw_decay_rate(key, part):
    key = jax.random.fold_in(key, 23)
    first_key, second_key, third_key = jax.random.split(key, 3)
    order = jax.random.permutation(first_key, H)
    quick_heads = order < H // 2
    quick_rate = jax.random.uniform(second_key, (H,), jnp.float32, 1.0 / 50.0, 1.0 / 30.0)
    slow_rate = jax.random.uniform(third_key, (H,), jnp.float32, 0.3, 1.0) * (math.log(10.0) / PACK)
    return jnp.where(quick_heads, quick_rate, slow_rate).astype(jnp.float32)


def block_scale(stream_key, extent, cuts, smallest, largest):
    def one(dim, shards_of):
        heights = jax.random.uniform(jax.random.fold_in(jax.random.fold_in(stream_key, 6), dim), (shards_of,), jnp.float32, smallest / len(cuts), largest / len(cuts))
        return jnp.repeat(jnp.exp(heights), extent[dim] // shards_of).reshape((-1,) + (1,) * (len(extent) - dim - 1))

    level = one(*cuts[0])
    for cut in cuts[1:]:
        level = level * one(*cut)
    return level


def bell_draw(stream_key, shape, spread, most, pieces=(), kind=jnp.bfloat16):
    entries = spread * jax.random.normal(stream_key, shape, jnp.float32)
    if pieces:
        entries = entries * block_scale(stream_key, shape, pieces, -0.22, 0.18)
    return jnp.clip(entries, -most, most).astype(kind)


def setup_inputs(seed: int = 0) -> dict:
    streams_of = jax.random.split(jax.random.key(seed), 15)
    tokens = bell_draw(streams_of[0], (N_NARROW, PACK, D), 1.0, 6.0, ((0, 4), (1, 8)))
    cotangent = bell_draw(streams_of[1], (N_NARROW, PACK, D), 1.0, 6.0, ((0, 4), (1, 8)))
    lengths = draw_lengths(jax.random.fold_in(streams_of[14], 71), 0)
    decay_rate = draw_decay_rate(jax.random.fold_in(streams_of[14], 71), 0)
    attn_gain = jnp.clip(1.0 + 0.18 * jax.random.normal(streams_of[4], (D,), jnp.float32), 0.1, 1.9)
    w_query = bell_draw(streams_of[5], (D, D), D ** -0.5, 0.1875)
    w_key = bell_draw(streams_of[6], (D, D), D ** -0.5, 0.1875)
    w_value = bell_draw(streams_of[7], (D, D), D ** -0.5, 0.1875)
    w_gate = bell_draw(streams_of[8], (D, D), D ** -0.5, 0.1875)
    w_out = bell_draw(streams_of[9], (D, D), D ** -0.5, 0.1875)
    ffn_gain = jnp.clip(1.0 + 0.18 * jax.random.normal(streams_of[10], (D,), jnp.float32), 0.1, 1.9)
    w_left = bell_draw(streams_of[11], (D, FF), D ** -0.5, 0.1875, ((1, 4),))
    w_right = bell_draw(streams_of[12], (D, FF), D ** -0.5, 0.1875, ((1, 4),))
    w_down = bell_draw(streams_of[13], (FF, D), FF ** -0.5, 0.109375, ((0, 4),))
    return dict(tokens=tokens, cotangent=cotangent, lengths=lengths, decay_rate=decay_rate, attn_gain=attn_gain, w_query=w_query, w_key=w_key, w_value=w_value, w_gate=w_gate, w_out=w_out, ffn_gain=ffn_gain, w_left=w_left, w_right=w_right, w_down=w_down)


EPS = 1e-06
HIGH = lax.Precision.HIGHEST

@jax.custom_vjp
def low(v):
    return lax.optimization_barrier(v.astype(jnp.bfloat16)).astype(jnp.float32)

@jax.custom_vjp
def low_back(v):
    return v

def low_keep(v):
    return (low(v), None)

def low_pass(kept, grad):
    return (grad,)

def back_keep(v):
    return (v, None)

def back_low(kept, grad):
    return (low(grad),)
low.defvjp(low_keep, low_pass)
low_back.defvjp(back_keep, back_low)

def rms_scale(vector):
    return vector * lax.rsqrt(lax.optimization_barrier(jnp.mean(vector * vector, axis=-1, keepdims=True)) + EPS)

def matmul_hi(left_mat, right_mat):
    return jnp.dot(left_mat, right_mat, precision=HIGH, preferred_element_type=jnp.float32)

def pack_mixer(query, keyed, value, lengths_row, decay_rate):
    seq_ends = jnp.cumsum(lengths_row).astype(jnp.int32)
    places = jnp.arange(PACK).astype(jnp.int32)
    segment = lax.optimization_barrier(jnp.sum((places[:, None] >= seq_ends[None, :]).astype(jnp.int32), axis=1)).astype(jnp.int32)
    is_live = places < seq_ends[-1]
    blocks = PACK // TOK_DEV
    seg_blocks = segment.reshape(blocks, TOK_DEV)
    live_blocks = is_live.reshape(blocks, TOK_DEV)
    seg_before = jnp.concatenate([jnp.full((1,), -1, jnp.int32), segment[TOK_DEV - 1:PACK - 1:TOK_DEV].astype(jnp.int32)])
    local_pos = jnp.arange(TOK_DEV)
    offset = local_pos[:, None] - local_pos[None, :]
    causal = offset >= 0

    def block_step(state, inputs):
        query_blk, keyed_blk, value_blk, seg_blk, live_blk, seg_prev = inputs
        seg_last = seg_blk[TOK_DEV - 1]
        allowed = causal & (seg_blk[:, None] == seg_blk[None, :]) & live_blk[:, None] & live_blk[None, :]
        decay_mask = jnp.exp(-decay_rate[:, None, None] * jnp.where(causal, offset, 0).astype(jnp.float32)[None]) * allowed.astype(jnp.float32)[None]
        gate_in = jnp.exp(-decay_rate[:, None] * (local_pos + 1).astype(jnp.float32)[None]) * ((seg_blk == seg_prev) & live_blk).astype(jnp.float32)[None]
        keep_out = jnp.exp(-decay_rate[:, None] * (TOK_DEV - 1 - local_pos).astype(jnp.float32)[None]) * ((seg_blk == seg_last) & live_blk).astype(jnp.float32)[None]
        pass_on = jnp.exp(-decay_rate * TOK_DEV) * (seg_last == seg_prev).astype(jnp.float32)
        scores = low_back(jnp.einsum('thd,shd->hts', query_blk, keyed_blk, precision=HIGH))
        probs = low(scores * decay_mask)
        intra = jnp.einsum('hts,shd->thd', probs, value_blk, precision=HIGH)
        inter = jnp.einsum('thd,hde->the', query_blk, state, precision=HIGH) * gate_in.T[:, :, None]
        local_state = jnp.einsum('shd,she->hde', keyed_blk * keep_out.T[:, :, None], value_blk, precision=HIGH)
        new_state = pass_on[:, None, None] * state + local_state
        return (new_state, intra + inter)
    shape_blk = (blocks, TOK_DEV, H, HDIM)
    start_state = jnp.zeros((H, HDIM, HDIM), jnp.float32)
    _, outs = lax.scan(jax.checkpoint(block_step), start_state, (query.reshape(shape_blk), keyed.reshape(shape_blk), value.reshape(shape_blk), seg_blocks, live_blocks, seg_before))
    return outs.reshape(PACK, H, HDIM)

def forward(tokens, w_query, w_key, w_value, w_gate, w_out, attn_gain, ffn_gain, w_left, w_right, w_down, lengths, decay_rate):
    results = []
    for pack_idx in range(N_NARROW):
        inputs = tokens[pack_idx]
        normed1 = low(rms_scale(inputs) * attn_gain)
        q_pre = low_back(matmul_hi(normed1, w_query))
        k_pre = low_back(matmul_hi(normed1, w_key))
        query = low(jax.nn.silu(q_pre)).reshape(PACK, H, HDIM)
        keyed = low(jax.nn.silu(k_pre)).reshape(PACK, H, HDIM)
        value = low(low_back(matmul_hi(normed1, w_value))).reshape(PACK, H, HDIM)
        gate_u = low_back(matmul_hi(normed1, w_gate))
        attn_raw = low_back(pack_mixer(query, keyed, value, lengths[pack_idx], decay_rate))
        normed_o = rms_scale(attn_raw).reshape(PACK, D)
        mixed = low(normed_o * gate_u)
        hidden = inputs + low_back(matmul_hi(mixed, w_out))
        normed2 = low(rms_scale(hidden) * ffn_gain)
        left_act = low_back(matmul_hi(normed2, w_left))
        right_act = low_back(matmul_hi(normed2, w_right))
        product = low(left_act * right_act)
        results.append(hidden + low_back(matmul_hi(product, w_down)))
    return jnp.stack(results)

def reference(tokens, cotangent, lengths, decay_rate, attn_gain, w_query, w_key, w_value, w_gate, w_out, ffn_gain, w_left, w_right, w_down):
    primals = (tokens.astype(jnp.float32), w_query.astype(jnp.float32), w_key.astype(jnp.float32), w_value.astype(jnp.float32), w_gate.astype(jnp.float32), w_out.astype(jnp.float32), attn_gain.astype(jnp.float32), ffn_gain.astype(jnp.float32), w_left.astype(jnp.float32), w_right.astype(jnp.float32), w_down.astype(jnp.float32))

    def wrapped(tok, wq, wk, wv, wg, wo, gain_a, gain_f, wl, wr, wd):
        return forward(tok, wq, wk, wv, wg, wo, gain_a, gain_f, wl, wr, wd, lengths, decay_rate)
    result, pullback = jax.vjp(wrapped, *primals)
    grads = pullback(cotangent.astype(jnp.float32))
    return (result.astype(jnp.bfloat16), grads[0], grads[1], grads[2], grads[3], grads[4], grads[5], grads[6], grads[7], grads[8], grads[9], grads[10])
```

```python
import math

import jax
import jax.numpy as jnp
from jax import lax
from jax.experimental import pallas as pl
from jax.experimental.pallas import tpu as pltpu
from jax.sharding import PartitionSpec as P

EPS = 1e-06
HIGH = lax.Precision.HIGHEST

MESH = pl.DeviceIdType.MESH
F32 = jnp.float32
BF16 = jnp.bfloat16
VMEM_BYTES = 62 * 1024 * 1024
ANY = pl.BlockSpec(memory_space=pl.ANY)
IN_VMEM = pl.BlockSpec(memory_space=pltpu.VMEM)
IN_SMEM = pl.BlockSpec(memory_space=pltpu.SMEM)


class Refs:
    def __init__(self, names, refs):
        self.__dict__.update(zip(names, refs, strict=True))


def call_kernel(body, name, number, ins, outs, scratch, cost):
    names = list(ins) + list(outs) + list(scratch)

    def kernel(*refs):
        body(Refs(names, refs))

    results = pl.pallas_call(
        kernel,
        name=name,
        out_shape=list(outs.values()),
        in_specs=[spec for _, spec in ins.values()],
        out_specs=[ANY] * len(outs),
        scratch_shapes=list(scratch.values()),
        cost_estimate=pl.CostEstimate(flops=cost, bytes_accessed=cost // 500, transcendentals=0),
        compiler_params=pltpu.CompilerParams(
            collective_id=number, has_side_effects=True, vmem_limit_bytes=VMEM_BYTES
        ),
    )(*[array for array, _ in ins.values()])
    return dict(zip(outs, results, strict=True))


def nn(left, right):
    return lax.dot_general(left, right, (((1,), (0,)), ((), ())), preferred_element_type=F32)


def nt(left, right):
    return lax.dot_general(left, right, (((1,), (1,)), ((), ())), preferred_element_type=F32)


def tn(left, right):
    return lax.dot_general(left, right, (((0,), (0,)), ((), ())), preferred_element_type=F32)


def part(index, size):
    return pl.ds(pl.multiple_of(index * size, size), size)


def round_up(number, step):
    return -(-number // step) * step


class Place:
    def __init__(self, wide):
        self.wide = wide
        self.lines = wide // 2
        self.w = lax.axis_index("wide")
        self.n = lax.axis_index("narrow")
        self.core = lax.rem(self.n, 2)
        self.xh = lax.div(self.n, 2)
        self.yh = lax.rem(self.w, 2)
        self.zi = lax.div(self.w, 2)
        self.flip_core = (self.w, self.n + 1 - 2 * self.core)
        self.flip_x = (self.w, self.n + 2 - 4 * self.xh)
        self.flip_y = (self.w + 1 - 2 * self.yh, self.n)

    def line(self, step):
        return lax.rem(self.zi + step, self.lines)

    def on_line(self, zi):
        return (2 * zi + self.yh, self.n)

    def on_wide(self, w):
        return (w, self.n)


def greet(partners, place, whole_wide):
    barrier = pltpu.get_barrier_semaphore()
    for partner in partners:
        pl.semaphore_signal(barrier, inc=1, device_id=partner, device_id_type=MESH)
    count = len(partners)
    if whole_wide:

        def one(step, carry):
            pl.semaphore_signal(
                barrier,
                inc=1,
                device_id=place.on_wide(lax.rem(place.w + step, place.wide)),
                device_id_type=MESH,
            )
            return carry

        lax.fori_loop(1, place.wide, one, 0)
        count += place.wide - 1
    pl.semaphore_wait(barrier, count)


def remote(src, dst, send, recv, device):
    return pltpu.make_async_remote_copy(
        src_ref=src, dst_ref=dst, send_sem=send, recv_sem=recv, device_id=device, device_id_type=MESH
    )


def segment_ends(lens):
    ends = []
    total = jnp.int32(0)
    for slot in range(lens.shape[1]):
        total = total + lens[0, slot]
        ends.append(total)
    return ends


def count_ends(ends, spots):
    total = jnp.zeros_like(spots)
    for end in ends:
        total = total + jnp.where(spots >= end, 1, 0)
    return total


def segment_setup(place, ends, rate_row, rows, gate_ref, keep_ref, reach_ref):
    anchor = place.w * rows
    col_local = lax.broadcasted_iota(jnp.int32, (rows, 1), 0)
    row_local = lax.broadcasted_iota(jnp.int32, (1, rows), 1)
    col_seg = count_ends(ends, col_local + anchor)
    row_seg = count_ends(ends, row_local + anchor)
    before = jnp.int32(0)
    last = jnp.int32(0)
    for end in ends:
        before = before + jnp.where(anchor - 1 >= end, 1, 0)
        last = last + jnp.where(anchor + rows - 1 >= end, 1, 0)
    before = jnp.where(place.w > 0, before, -1)
    col_live = (col_local + anchor) < ends[-1]
    row_live = (row_local + anchor) < ends[-1]
    rates = rate_row[...]
    steps = col_local.astype(F32)
    gate_ref[...] = jnp.exp(-(steps + 1.0) * rates) * jnp.where(
        (col_seg == before) & col_live, 1.0, 0.0
    )
    keep_ref[...] = jnp.exp(-(rows - 1.0 - steps) * rates) * jnp.where(
        (col_seg == last) & col_live, 1.0, 0.0
    )
    gap = row_local - col_local
    reaches = (gap >= 0) & (col_seg == row_seg) & row_live
    reach_ref[...] = jnp.where(reaches, gap.astype(F32), -1.0)


def decay_of(reach, rate):
    return jnp.where(reach >= 0.0, jnp.exp(-rate * reach), 0.0)


def scatter_states(place, local, arrived, sends, recvs, chunk):
    def one(step, carry):
        target = lax.rem(place.w + step, place.wide)
        remote(
            local.at[part(target, chunk)],
            arrived.at[place.w],
            sends.at[target],
            recvs.at[place.w],
            place.on_wide(target),
        ).start()
        return carry

    lax.fori_loop(1, place.wide, one, 0)
    arrived[place.w] = local[part(place.w, chunk), :]


def wait_states(place, local, arrived, sends, recvs, chunk):
    def one(step, carry):
        source = lax.rem(place.w + step, place.wide)
        copy = remote(
            local.at[part(source, chunk)],
            arrived.at[source],
            sends.at[source],
            recvs.at[source],
            place.on_wide(source),
        )
        copy.wait_recv()
        copy.wait_send()
        return carry

    lax.fori_loop(1, place.wide, one, 0)


def join_states(place, ends, rate, rows, arrived, joined, backward):
    shape = arrived.shape[1:]
    fade = jnp.exp(jnp.full((1, shape[1]), -1.0 * rows, F32) * rate)

    def one(step, state):
        block = place.wide - 1 - step if backward else step
        joined[block] = state.astype(BF16)
        cuts = jnp.int32(0)
        for end in ends:
            inside = (end >= block * rows) & (end <= block * rows + rows - 1)
            cuts = cuts + jnp.where(inside, 1, 0)
        flag = jnp.where((cuts == 0) & (block > 0), 1.0, 0.0)
        return (fade * flag) * state + arrived[block].astype(F32)

    lax.fori_loop(0, place.wide, one, jnp.zeros(shape, F32))


def return_states(place, joined, entering, sends, recvs, chunk):
    def one(step, carry):
        target = lax.rem(place.w + step, place.wide)
        remote(
            joined.at[target],
            entering.at[part(place.w, chunk)],
            sends.at[target],
            recvs.at[place.w],
            place.on_wide(target),
        ).start()
        return carry

    lax.fori_loop(1, place.wide, one, 0)
    entering[part(place.w, chunk), :] = joined[place.w]


def wait_returned(place, joined, entering, sends, recvs, chunk):
    def one(step, carry):
        source = lax.rem(place.w + step, place.wide)
        copy = remote(
            joined.at[source],
            entering.at[part(source, chunk)],
            sends.at[source],
            recvs.at[source],
            place.on_wide(source),
        )
        copy.wait_recv()
        copy.wait_send()
        return carry

    lax.fori_loop(1, place.wide, one, 0)


class Unit:
    def __init__(self, place, kind, acc, other, xrecv, yrecv, zrecv, out, sems, zsems, index):
        self.place = place
        self.kind = kind
        self.acc = acc
        self.other = other
        self.xrecv = xrecv
        self.yrecv = yrecv
        self.zrecv = zrecv
        self.out = out
        self.sems = sems.at[index]
        self.zsems = zsems.at[index]
        p = place
        rows = out.shape[0]
        if kind == "attn":
            cols = part(p.core, out.shape[1] // 2)
            self.half = rows // 2
            self.quarter = rows // 4
            self.chunk = self.quarter // p.lines
            self.x_region = out.at[part(p.xh, self.half), cols]
            self.core_region = out.at[:, cols]
            y_base = p.xh * self.half + p.yh * self.quarter
            self.y_region = out.at[pl.ds(pl.multiple_of(y_base, self.quarter), self.quarter), cols]
            self.z_base, self.z_cols = y_base, cols
            self.acc_base = y_base
        elif kind == "rows":
            self.half = rows // 2
            self.chunk = self.half // p.lines
            self.y_region = out.at[part(p.yh, self.half), :]
            self.z_base, self.z_cols = p.yh * self.half, slice(None)
            self.acc_base = 0
        else:
            cols = part(p.yh, out.shape[1] // 2)
            self.chunk = rows // p.lines
            self.y_region = out.at[:, cols]
            self.z_base, self.z_cols = 0, cols
            self.acc_base = 0

    def pair(self, step, src, dst, device):
        return remote(src, dst, self.sems.at[2 * step], self.sems.at[2 * step + 1], device)

    def own_rows(self, base, zi):
        start = pl.multiple_of(base + zi * self.chunk, self.chunk)
        return pl.ds(start, self.chunk)

    def x_copy(self):
        src = self.acc.at[part(1 - self.place.xh, self.half)]
        return self.pair(0, src, self.xrecv, self.place.flip_x)

    def x_start(self):
        self.x_copy().start()

    def x_finish(self):
        copy = self.x_copy()
        copy.wait_recv()
        base = self.place.xh * self.half
        add_into(self.acc, base, self.xrecv)
        self.y_start()

    def y_copy(self):
        if self.kind == "attn":
            base = self.place.xh * self.half + (1 - self.place.yh) * self.quarter
            src = self.acc.at[pl.ds(pl.multiple_of(base, self.quarter), self.quarter)]
        else:
            src = self.other
        return self.pair(1, src, self.yrecv, self.place.flip_y)

    def y_start(self):
        self.y_copy().start()

    def y_finish(self):
        self.y_copy().wait_recv()
        add_into(self.acc, self.acc_base, self.yrecv)
        for step in range(1, self.place.lines):
            self.z_copy(step).start()

    def z_copy(self, step):
        zi = self.place.line(step)
        return remote(
            self.acc.at[self.own_rows(self.acc_base, zi)],
            self.zrecv.at[step - 1],
            self.zsems.at[0, step],
            self.zsems.at[1, step],
            self.place.on_line(zi),
        )

    def z_finish(self):
        for step in range(1, self.place.lines):
            self.z_copy(step).wait_recv()
        mine = self.own_rows(self.acc_base, self.place.zi)
        total = self.acc[mine, :].astype(F32)
        for step in range(1, self.place.lines):
            total = total + self.zrecv[step - 1].astype(F32)
        self.acc[mine, :] = total.astype(BF16)
        self.local_copy().start()
        for step in range(1, self.place.lines):
            self.back_copy(step).start()

    def local_copy(self):
        return pltpu.make_async_copy(
            self.acc.at[self.own_rows(self.acc_base, self.place.zi)],
            self.out.at[self.own_rows(self.z_base, self.place.zi), self.z_cols],
            self.zsems.at[2, 0],
        )

    def back_copy(self, step):
        return remote(
            self.acc.at[self.own_rows(self.acc_base, self.place.zi)],
            self.out.at[self.own_rows(self.z_base, self.place.zi), self.z_cols],
            self.zsems.at[2, step],
            self.zsems.at[3, step],
            self.place.on_line(self.place.line(step)),
        )

    def back_y_copy(self):
        return self.pair(2, self.y_region, self.y_region, self.place.flip_y)

    def back_z_finish(self):
        self.local_copy().wait()
        for step in range(1, self.place.lines):
            self.back_copy(step).wait_recv()
        self.back_y_copy().start()

    def back_x_copy(self):
        return self.pair(3, self.x_region, self.x_region, self.place.flip_x)

    def back_y_finish(self):
        self.back_y_copy().wait_recv()
        if self.kind == "attn":
            self.back_x_copy().start()

    def back_core_copy(self):
        return self.pair(4, self.core_region, self.core_region, self.place.flip_core)

    def back_x_finish(self):
        self.back_x_copy().wait_recv()
        self.back_core_copy().start()

    def close(self):
        if self.kind == "attn":
            self.back_core_copy().wait_recv()
            self.x_copy().wait_send()
            self.back_x_copy().wait_send()
            self.back_core_copy().wait_send()
        self.y_copy().wait_send()
        self.back_y_copy().wait_send()
        for step in range(1, self.place.lines):
            self.z_copy(step).wait_send()
            self.back_copy(step).wait_send()


def add_into(acc, base, other):
    rows = other.shape[0]
    tile = math.gcd(rows, 128)

    @pl.loop(0, rows // tile)
    def _(i):
        here = pl.ds(pl.multiple_of(base + i * tile, tile), tile)
        acc[here, :] = acc[here, :] + other[part(i, tile), :]


def backward_body(wide, heads, eps, r):
    p = Place(wide)
    lines = p.lines
    rows, width = r.gn2.shape
    head = width // heads
    half = width // 2
    tile = 128
    chunk = width // wide
    mine = part(p.core, half)
    theirs = part(1 - p.core, half)

    greet([p.flip_core, p.flip_x], p, True)

    names = ("d", "l", "r", "o", "g", "q", "k", "v")
    u = {}
    for i, nm in enumerate(names):
        if nm in "lr":
            src = getattr(r, "p_" + nm).at[part(1 - p.yh, width // 2), :]
            u[nm] = Unit(p, "rows", getattr(r, "acc_" + nm), src, None, getattr(r, "yr_" + nm), getattr(r, "zr_" + nm), getattr(r, "out_" + nm), r.usem, r.zsem, i)
        elif nm == "d":
            src = r.p_d.at[:, part(1 - p.yh, width // 2)]
            u[nm] = Unit(p, "cols", r.acc_d, src, None, r.yr_d, r.zr_d, r.out_d, r.usem, r.zsem, i)
        else:
            k = i - 3
            u[nm] = Unit(p, "attn", r.acc.at[k], None, r.xr.at[k], r.yr.at[k], r.zr.at[k], getattr(r, "out_" + nm), r.usem, r.zsem, i)

    loads = {}

    def load(key, src, dst):
        loads[key] = pltpu.make_async_copy(src, dst, r.lsem.at[len(loads)])
        loads[key].start()

    def need(*keys):
        for key in keys:
            loads[key].wait()

    load("gn2", r.gn2, r.gn2_v)
    load("hidden", r.hidden, r.hid_v)
    load("cot", r.cot, r.cot_v)
    load("wo", r.wo, r.wa)
    load("flat", r.flat, r.flat_v)
    load("gate", r.gate, r.gate_v)
    load("ko", r.ko, r.ko_v)
    load("q", r.q, r.q_v)
    for nm in "dlr":
        u[nm].y_start()
    to_sib = [
        remote(r.mixed, r.mix_v.at[1], r.csem.at[0], r.csem.at[1], p.flip_core),
        remote(r.n1, r.n1_v.at[1], r.csem.at[2], r.csem.at[3], p.flip_core),
    ]
    for copy in to_sib:
        copy.start()
    load("mixed", r.mixed, r.mix_v.at[0])
    load("n1", r.n1, r.n1_v.at[0])
    load("k", r.k, r.k_v)
    load("v", r.v, r.v_v)
    load("sin", r.sin, r.sin_v)
    load("dq", r.dq, r.dq_v)
    load("dk", r.dk, r.dk_v)
    load("accd", r.p_d.at[:, part(p.yh, width // 2)], r.acc_d.at[pl.ds(0, r.p_d.shape[0])])
    load("accl", r.p_l.at[part(p.yh, width // 2), :], r.acc_l)
    load("accr", r.p_r.at[part(p.yh, width // 2), :], r.acc_r)
    load("wk", r.wk, r.wc)
    load("wv", r.wv, r.wd)

    ends = segment_ends(r.lens)
    segment_setup(p, ends, r.rate_row, rows, r.gate_in, r.keep_out, r.reach)

    need("gn2", "hidden", "cot")
    r.gsum[...] = jnp.zeros_like(r.gsum)

    def fold(x):
        return jnp.sum(x.reshape(x.shape[0] // 8, 8, x.shape[1]), axis=0)

    @pl.loop(0, rows // tile)
    def _(i):
        here = part(i, tile)
        hid = r.hid_v[here, :]
        scale = lax.rsqrt(jnp.mean(hid * hid, axis=-1, keepdims=True) + eps)
        unit = hid * scale
        up = r.gn2_v[here, :]
        r.gsum[1] += fold(up * unit)
        up = up * r.fgain[...]
        down = scale * (up - unit * jnp.mean(up * unit, axis=-1, keepdims=True))
        down = down + r.cot_v[here, :].astype(F32)
        r.hid_v[here, :] = down
        r.gb[here, :] = down.astype(BF16)

    load("tok", r.tokens, r.cot_v)
    halves = {}

    def send_half(key, src, slot):
        halves[key] = remote(src.at[:, theirs], r.sib.at[slot], r.csem.at[4 + 2 * slot], r.csem.at[5 + 2 * slot], p.flip_core)
        halves[key].start()

    send_half("o", r.gb, 0)

    need("wo", "flat", "gate", "ko")

    @pl.loop(0, rows // 256)
    def _(i):
        here = part(i, 256)
        gm = nt(r.gb[here, :], r.wa[...])
        flat = r.flat_v[here, :].astype(F32)
        r.gg[here, :] = (gm * flat).astype(BF16)
        gm = gm * r.gate_v[here, :].astype(F32)
        ko = r.ko_v[here, :]
        for h in range(heads):
            cols = slice(h * head, (h + 1) * head)
            up, unit = gm[:, cols], flat[:, cols]
            mean = jnp.mean(up * unit, axis=-1, keepdims=True)
            r.ga[here, cols] = (ko[:, h : h + 1] * (up - unit * mean)).astype(BF16)

    send_half("g", r.gg, 1)
    load("wq", r.wq, r.wa)

    need("q")
    for h in range(heads):
        cols = slice(h * head, (h + 1) * head)
        gated = (r.q_v[:, cols].astype(F32) * r.gate_in[:, h : h + 1]).astype(BF16)
        r.state_a[pl.ds(h * head, head), :] = tn(gated, r.ga[:, cols]).astype(BF16)
    scatter_states(p, r.state_a, r.arrived, r.ssem.at[0], r.ssem.at[1], chunk)

    def weight_unit(nm, slot, left, own):
        acc = r.acc.at["ogqkv".index(nm)]
        other = r.sib.at[slot]
        halves[nm].wait_recv()

        @pl.loop(0, width // 512)
        def _(i):
            here = part(i, 512)
            acc[here, :] = (
                tn(left[0, :, here], own[:, mine]) + tn(left[1, :, here], other[...])
            ).astype(BF16)

        u[nm].x_start()

    need("mixed", "n1")
    for copy in to_sib:
        copy.wait_recv()
    weight_unit("o", 0, r.mix_v, r.gb)
    weight_unit("g", 1, r.n1_v, r.gg)

    need("k", "v", "sin", "dq", "dk")

    def inside(h, carry):
        cols = part(h, head)
        q, k, v, ga = r.q_v[:, cols], r.k_v[:, cols], r.v_v[:, cols], r.ga[:, cols]
        weight = decay_of(r.reach[...], r.rate_s[h])
        probs = (nt(k, q) * weight).astype(BF16)
        r.gv_f[:, cols] = nn(probs, ga)
        scores = (nt(v, ga) * weight).astype(BF16)
        r.gn2_v[:, cols] = nn(scores, q)
        pick = lax.broadcasted_iota(jnp.int32, (1, heads), 1) == h
        gate = jnp.sum(jnp.where(pick, r.gate_in[...], 0.0), axis=1, keepdims=True)
        gq = tn(scores, k) + nt(ga, r.sin_v[cols, :]) * gate
        r.gq[:, cols] = (gq * r.dq_v[:, cols].astype(F32)).astype(BF16)
        return carry

    lax.fori_loop(0, heads // 2, inside, 0)
    need("accd", "accl", "accr")
    u["d"].y_finish()
    wait_states(p, r.state_a, r.arrived, r.ssem.at[0], r.ssem.at[1], chunk)
    join_states(p, ends, r.rate_s[lax.div(p.w * chunk, head)], rows, r.arrived, r.joined, True)
    return_states(p, r.joined, r.state_b, r.ssem.at[2], r.ssem.at[3], chunk)
    u["o"].x_finish()
    lax.fori_loop(heads // 2, heads, inside, 0)
    send_half("q", r.gq, 2)
    u["g"].x_finish()
    u["l"].y_finish()
    weight_unit("q", 2, r.n1_v, r.gq)
    wait_returned(p, r.joined, r.state_b, r.ssem.at[2], r.ssem.at[3], chunk)

    for h in range(heads):
        cols = slice(h * head, (h + 1) * head)
        state = r.state_b[pl.ds(h * head, head), :]
        keep = r.keep_out[:, h : h + 1]
        gk = r.gn2_v[:, cols] + nt(r.v_v[:, cols], state) * keep
        r.flat_v[:, cols] = (gk * r.dk_v[:, cols].astype(F32)).astype(BF16)
        gv = r.gv_f[:, cols] + nn(r.k_v[:, cols], state) * keep
        r.gate_v[:, cols] = gv.astype(BF16)
    send_half("k", r.flat_v, 3)
    send_half("v", r.gate_v, 4)
    weight_unit("k", 3, r.n1_v, r.flat_v)
    weight_unit("v", 4, r.n1_v, r.gate_v)
    to_sib[0].wait_send()
    load("wg0", r.wg.at[pl.ds(0, rows)], r.mix_v.at[0])
    load("wg1", r.wg.at[pl.ds(rows, rows)], r.mix_v.at[1])
    u["d"].z_finish()
    u["r"].y_finish()
    u["o"].y_finish()
    u["g"].y_finish()

    need("wq", "wk", "wv", "wg0", "wg1", "tok")

    @pl.loop(0, rows // tile)
    def _(i):
        here = part(i, tile)
        up = (
            nt(r.gq[here, :], r.wa[...])
            + nt(r.flat_v[here, :], r.wc[...])
            + nt(r.gate_v[here, :], r.wd[...])
            + jnp.concatenate([nt(r.gg[here, :], r.mix_v[i]) for i in range(2)], axis=1)
        )
        tok = r.cot_v[here, :].astype(F32)
        scale = lax.rsqrt(jnp.mean(tok * tok, axis=-1, keepdims=True) + eps)
        unit = tok * scale
        r.gsum[0] += fold(up * unit)
        up = up * r.again[...]
        down = scale * (up - unit * jnp.mean(up * unit, axis=-1, keepdims=True))
        r.hid_v[here, :] += down

    store = pltpu.make_async_copy(r.hid_v, r.gtok, r.osem.at[0])
    store.start()

    r.gains[0] = jnp.zeros_like(r.gains[0])
    for row in range(2):
        r.gains[0, pl.ds(row, 1), :] = jnp.sum(r.gsum[row], axis=0, keepdims=True)

    def gain_copy(step, device):
        return remote(r.gains.at[step], r.grecv.at[step], r.gsem.at[2 * step], r.gsem.at[2 * step + 1], device)

    def gain_line(step):
        return remote(
            r.gains.at[3],
            r.grecv.at[3 + p.zi],
            r.gsem.at[6 + 2 * step],
            r.gsem.at[7 + 2 * step],
            p.on_line(p.line(step)),
        )

    def gain_next(step, device):
        copy = gain_copy(step, device)
        copy.wait_recv()
        r.gains[step + 1] = r.gains[step] + r.grecv[step]

    gain_copy(0, p.flip_core).start()
    u["l"].z_finish()
    u["q"].x_finish()
    gain_next(0, p.flip_core)
    gain_copy(1, p.flip_x).start()
    u["k"].x_finish()
    u["q"].y_finish()
    u["o"].z_finish()
    u["g"].z_finish()
    gain_next(1, p.flip_x)
    gain_copy(2, p.flip_y).start()
    u["d"].back_z_finish()
    u["v"].x_finish()
    u["r"].z_finish()
    u["k"].y_finish()
    u["q"].z_finish()
    gain_next(2, p.flip_y)
    for step in range(1, lines):
        gain_line(step).start()
    u["v"].y_finish()
    u["k"].z_finish()
    u["o"].back_z_finish()
    u["g"].back_z_finish()
    u["l"].back_z_finish()
    u["v"].z_finish()
    u["o"].back_y_finish()
    u["g"].back_y_finish()
    u["q"].back_z_finish()
    u["k"].back_z_finish()
    u["v"].back_z_finish()
    u["r"].back_z_finish()
    for nm in "qkv":
        u[nm].back_y_finish()
    for nm in "ogqkv":
        u[nm].back_x_finish()
    for nm in "dlr":
        u[nm].back_y_finish()
    for step in range(1, lines):
        gain_line(step).wait_recv()
    r.grecv[3 + p.zi] = r.gains[3]
    total = r.grecv[3]
    for zi in range(1, lines):
        total = total + r.grecv[3 + zi]
    r.gains[4] = total
    put = pltpu.make_async_copy(r.gains.at[4], r.out_gain, r.osem.at[1])
    put.start()
    for nm in names:
        u[nm].close()
    put.wait()
    store.wait()
    to_sib[1].wait_send()
    for copy in halves.values():
        copy.wait_send()
    for step, device in enumerate((p.flip_core, p.flip_x, p.flip_y)):
        gain_copy(step, device).wait_send()
    for step in range(1, lines):
        gain_line(step).wait_send()


def backward_call(wide, heads, eps, arrays):
    rows, width = arrays["gn2"].shape
    hidden = arrays["p_l"].shape[1]
    lines = wide // 2
    half, quarter = width // 2, width // 4
    tall = lines * round_up(-(-hidden // lines), 16)
    specs = {"lens": IN_SMEM, "rate_s": IN_SMEM, "rate_row": IN_VMEM, "fgain": IN_VMEM, "again": IN_VMEM}
    ins = {nm: (a, specs.get(nm, ANY)) for nm, a in arrays.items()}
    sds = jax.ShapeDtypeStruct
    outs = {"out_" + nm: sds((width, width), BF16) for nm in "ogqkv"}
    outs["out_l"] = sds((width, hidden), BF16)
    outs["out_r"] = sds((width, hidden), BF16)
    outs["out_d"] = sds((tall, width), BF16)
    outs["gtok"] = sds((rows, width), F32)
    outs["out_gain"] = sds((8, width), F32)
    V = pltpu.VMEM
    dma = pltpu.SemaphoreType.DMA
    scratch = dict(
        gn2_v=V((rows, width), F32),
        hid_v=V((rows, width), F32),
        gv_f=V((rows, width), F32),
        cot_v=V((rows, width), BF16),
        flat_v=V((rows, width), BF16),
        gate_v=V((rows, width), BF16),
        ko_v=V((rows, heads), F32),
        q_v=V((rows, width), BF16),
        k_v=V((rows, width), BF16),
        v_v=V((rows, width), BF16),
        dq_v=V((rows, width), BF16),
        dk_v=V((rows, width), BF16),
        mix_v=V((2, rows, width), BF16),
        n1_v=V((2, rows, width), BF16),
        sin_v=V((width, width // heads), BF16),
        wa=V((width, width), BF16),
        wc=V((width, width), BF16),
        wd=V((width, width), BF16),
        gb=V((rows, width), BF16),
        gg=V((rows, width), BF16),
        ga=V((rows, width), BF16),
        gq=V((rows, width), BF16),
        sib=V((5, rows, half), BF16),
        gate_in=V((rows, heads), F32),
        keep_out=V((rows, heads), F32),
        reach=V((rows, rows), F32),
        state_a=V((width, width // heads), BF16),
        state_b=V((width, width // heads), BF16),
        arrived=V((wide, width // wide, width // heads), BF16),
        joined=V((wide, width // wide, width // heads), BF16),
        acc=V((5, width, half), BF16),
        xr=V((5, half, half), BF16),
        yr=V((5, quarter, half), BF16),
        zr=V((5, lines - 1, quarter // lines, half), BF16),
        acc_d=V((tall, half), BF16),
        acc_l=V((half, hidden), BF16),
        acc_r=V((half, hidden), BF16),
        yr_d=V((hidden, half), BF16),
        yr_l=V((half, hidden), BF16),
        yr_r=V((half, hidden), BF16),
        zr_d=V((lines - 1, tall // lines, half), BF16),
        zr_l=V((lines - 1, half // lines, hidden), BF16),
        zr_r=V((lines - 1, half // lines, hidden), BF16),
        gsum=V((2, 8, width), F32),
        gains=V((5, 8, width), F32),
        grecv=V((3 + lines, 8, width), F32),
        lsem=dma((24,)),
        csem=dma((14,)),
        ssem=dma((4, wide)),
        usem=dma((8, 10)),
        zsem=dma((8, 4, lines)),
        gsem=dma((8 + 2 * lines,)),
        osem=dma((2,)),
    )
    return call_kernel(
        lambda r: backward_body(wide, heads, eps, r), "attention_backward", 3, ins, outs, scratch, 20 * 10**9
    )


def carried_in(array, axis, join, neutral, backward):
    count = lax.axis_size(axis)
    place = lax.axis_index(axis)
    ahead = count - 1 - place if backward else place
    gathered = jax.tree.map(
        lambda a, kind: lax.all_gather(a.astype(kind), axis), array, (jnp.bfloat16, jnp.bfloat16)
    )
    state = jax.tree.map(lambda a, e: jnp.zeros_like(a) + jnp.asarray(e, a.dtype), array, neutral)

    def one(hop, state):
        source = count - 1 - hop if backward else hop
        return join(
            state,
            jax.tree.map(
                lambda a, own: lax.dynamic_index_in_dim(a, source, 0, False).astype(own.dtype),
                gathered,
                array,
            ),
        )

    return lax.fori_loop(0, ahead, one, state)


def rms_scale(vector):
    return vector * lax.rsqrt(jnp.mean(vector * vector, axis=-1, keepdims=True) + EPS)


def scale_norm(vector, gain):
    return rms_scale(vector) * gain


def contract_rows(left_mat, right_mat):
    return lax.dot_general(
        left_mat, right_mat, (((0,), (0,)), ((), ())), preferred_element_type=jnp.float32
    )


def times_transpose(left_mat, right_mat):
    return lax.dot_general(
        left_mat, right_mat, (((1,), (1,)), ((), ())), preferred_element_type=jnp.float32
    )


def combine_affine(earlier, later):
    return (earlier[0] * later[0], later[0][:, None, None] * earlier[1] + later[1])


def body(
    tokens,
    cotangent,
    lengths,
    decay_rate,
    attn_gain,
    w_query,
    w_key,
    w_value,
    w_gate,
    w_out,
    ffn_gain,
    w_left,
    w_right,
    w_down,
):
    rows_dev = tokens.shape[1]
    model_width = tokens.shape[2]
    num_heads = decay_rate.shape[0]
    head_dim = model_width // num_heads
    f32 = jnp.float32
    bf16 = jnp.bfloat16
    inputs = tokens[0].astype(f32)
    anchor = lax.axis_index("wide") * rows_dev
    seq_ends = jnp.cumsum(lengths[0])
    places = anchor + jnp.arange(-1, rows_dev)
    segment_all = jnp.sum((places[:, None] >= seq_ends[None, :]).astype(jnp.int32), axis=1)
    segment = segment_all[1:]
    is_live = places[1:] < seq_ends[-1]
    seg_prev = jnp.where(anchor > 0, segment_all[0], -1)
    seg_last = segment[rows_dev - 1]
    local_pos = jnp.arange(rows_dev)
    offset = local_pos[:, None] - local_pos[None, :]
    causal = offset >= 0
    allowed = causal & (segment[:, None] == segment[None, :]) & is_live[:, None] & is_live[None, :]
    decay_mask = (
        jnp.exp(-decay_rate[:, None, None] * jnp.where(causal, offset, 0).astype(f32)[None])
        * allowed.astype(f32)[None]
    )
    gate_in = (
        jnp.exp(-decay_rate[:, None] * (local_pos + 1).astype(f32)[None])
        * ((segment == seg_prev) & is_live).astype(f32)[None]
    )
    keep_out = (
        jnp.exp(-decay_rate[:, None] * (rows_dev - 1 - local_pos).astype(f32)[None])
        * ((segment == seg_last) & is_live).astype(f32)[None]
    )
    pass_on = jnp.exp(-decay_rate * rows_dev) * (seg_last == seg_prev).astype(f32)
    identity = (jnp.ones((num_heads,), f32), jnp.zeros((num_heads, head_dim, head_dim), f32))
    head_shape = (rows_dev, num_heads, head_dim)
    normed_first, norm_back1 = jax.vjp(scale_norm, inputs, attn_gain)
    normed1 = normed_first.astype(bf16)
    q_pre = jnp.dot(normed1, w_query, preferred_element_type=f32)
    k_pre = jnp.dot(normed1, w_key, preferred_element_type=f32)
    query_full, query_back = jax.vjp(jax.nn.silu, q_pre)
    key_full, key_back = jax.vjp(jax.nn.silu, k_pre)
    query = query_full.astype(bf16).reshape(head_shape)
    keyed = key_full.astype(bf16).reshape(head_shape)
    value = jnp.dot(normed1, w_value, preferred_element_type=f32).astype(bf16).reshape(head_shape)
    gate_u = jnp.dot(normed1, w_gate, preferred_element_type=f32)
    scores = jnp.einsum("thd,shd->hts", query, keyed, preferred_element_type=f32)
    probs = (scores * decay_mask).astype(bf16)
    intra = jnp.einsum("hts,shd->thd", probs, value, preferred_element_type=f32)
    query_wide = query.astype(f32)
    keyed_wide = keyed.astype(f32)
    value_wide = value.astype(f32)
    local_state = jnp.einsum(
        "shd,she->hde", keyed_wide * keep_out.T[:, :, None], value_wide, precision=HIGH
    )
    state_in = carried_in((pass_on, local_state), "wide", combine_affine, identity, False)[1]
    inter = jnp.einsum("thd,hde->the", query_wide, state_in, precision=HIGH) * gate_in.T[:, :, None]
    attn_raw = intra + inter
    normed_o, head_back = jax.vjp(rms_scale, attn_raw)
    flat_o = normed_o.reshape(rows_dev, model_width)
    mixed = (flat_o * gate_u).astype(bf16)
    hidden = inputs + jnp.dot(mixed, w_out, preferred_element_type=f32)
    normed_second, norm_back2 = jax.vjp(scale_norm, hidden, ffn_gain)
    normed2 = normed_second.astype(bf16)
    rows_all = lax.all_gather(normed2, "narrow", axis=0, tiled=True)
    left_act = jnp.dot(rows_all, w_left, preferred_element_type=f32)
    right_act = jnp.dot(rows_all, w_right, preferred_element_type=f32)
    product = (left_act * right_act).astype(bf16)
    ffn_out = lax.psum_scatter(
        jnp.dot(product, w_down, preferred_element_type=f32).astype(jnp.bfloat16),
        "narrow",
        scatter_dimension=0,
        tiled=True,
    ).astype(jnp.float32)
    output = (hidden + ffn_out).astype(bf16)
    grad_out = cotangent[0]
    grad_all = lax.all_gather(grad_out, "narrow", axis=0, tiled=True)
    grad_wdown = contract_rows(product, grad_all)
    grad_prod = times_transpose(grad_all, w_down)
    grad_left = (grad_prod * right_act).astype(bf16)
    grad_right = (grad_prod * left_act).astype(bf16)
    grad_wleft = contract_rows(rows_all, grad_left)
    grad_wright = contract_rows(rows_all, grad_right)
    grad_normed2 = lax.psum_scatter(
        (times_transpose(grad_left, w_left) + times_transpose(grad_right, w_right)).astype(
            jnp.bfloat16
        ),
        "narrow",
        scatter_dimension=0,
        tiled=True,
    ).astype(jnp.float32)
    rows_flat = lambda a: a.reshape(rows_dev, model_width)
    slope = lambda x: jax.nn.sigmoid(x) * (1.0 + x * (1.0 - jax.nn.sigmoid(x)))
    done = backward_call(
        lax.axis_size("wide"),
        num_heads,
        EPS,
        dict(
            gn2=grad_normed2,
            hidden=hidden,
            cot=grad_out,
            wo=w_out,
            flat=flat_o.astype(bf16),
            gate=gate_u.astype(bf16),
            ko=lax.rsqrt(jnp.mean(attn_raw * attn_raw, axis=-1) + EPS),
            q=rows_flat(query),
            k=rows_flat(keyed),
            v=rows_flat(value),
            mixed=mixed,
            n1=normed1,
            sin=state_in.reshape(model_width, head_dim).astype(bf16),
            dq=slope(q_pre).astype(bf16),
            dk=slope(k_pre).astype(bf16),
            p_d=grad_wdown.astype(bf16),
            p_l=grad_wleft.astype(bf16),
            p_r=grad_wright.astype(bf16),
            wq=w_query,
            wk=w_key,
            wv=w_value,
            wg=w_gate,
            tokens=tokens[0],
            lens=lengths,
            rate_s=decay_rate,
            rate_row=decay_rate[None],
            fgain=ffn_gain[None],
            again=attn_gain[None],
        ),
    )
    wide_of = lambda nm: done["out_" + nm].astype(f32)
    return (
        output[None],
        done["gtok"][None],
        wide_of("q"),
        wide_of("k"),
        wide_of("v"),
        wide_of("g"),
        wide_of("o"),
        done["out_gain"][0],
        done["out_gain"][1],
        wide_of("l"),
        wide_of("r"),
        wide_of("d")[: w_down.shape[0]],
    )


def solution(mesh):
    placed = (
        P("narrow", "wide", None),
        P("narrow", "wide", None),
        P("narrow", None),
        P(),
        P(),
        P(),
        P(),
        P(),
        P(),
        P(),
        P(),
        P(None, "narrow"),
        P(None, "narrow"),
        P("narrow", None),
    )
    return jax.shard_map(
        body,
        mesh=mesh,
        in_specs=placed,
        out_specs=(
            P("narrow", "wide", None),
            P("narrow", "wide", None),
            P(),
            P(),
            P(),
            P(),
            P(),
            P(),
            P(),
            P(None, "narrow"),
            P(None, "narrow"),
            P("narrow", None),
        ),
        check_vma=False,
    )
```

```python
import math

import jax
import jax.numpy as jnp
from jax import lax
from jax.experimental import pallas as pl
from jax.experimental.pallas import tpu as pltpu
from jax.sharding import PartitionSpec as P

EPS = 1e-06

MESH = pl.DeviceIdType.MESH
F32 = jnp.float32
BF16 = jnp.bfloat16
VMEM_BYTES = 62 * 1024 * 1024
ANY = pl.BlockSpec(memory_space=pl.ANY)
IN_VMEM = pl.BlockSpec(memory_space=pltpu.VMEM)
IN_SMEM = pl.BlockSpec(memory_space=pltpu.SMEM)


class Refs:
    def __init__(self, names, refs):
        self.recv, self.out_a, self.out_f = {}, {}, {}
        groups = {"r": self.recv, "a": self.out_a, "f": self.out_f}
        for name, ref in zip(names, refs, strict=True):
            if isinstance(name, str):
                setattr(self, name, ref)
            else:
                groups[name[0]][name[1:] if len(name) > 2 else name[1]] = ref


def call_kernel(body, name, number, ins, outs, scratch, cost):
    names = list(ins) + list(outs) + list(scratch)

    def kernel(*refs):
        body(Refs(names, refs))

    results = pl.pallas_call(
        kernel,
        name=name,
        out_shape=list(outs.values()),
        in_specs=[spec for _, spec in ins.values()],
        out_specs=[ANY] * len(outs),
        scratch_shapes=list(scratch.values()),
        cost_estimate=pl.CostEstimate(flops=cost, bytes_accessed=cost // 500, transcendentals=0),
        compiler_params=pltpu.CompilerParams(
            collective_id=number, has_side_effects=True, vmem_limit_bytes=VMEM_BYTES
        ),
    )(*[array for array, _ in ins.values()])
    return dict(zip(outs, results, strict=True))


def nn(left, right):
    return lax.dot_general(left, right, (((1,), (0,)), ((), ())), preferred_element_type=F32)


def nt(left, right):
    return lax.dot_general(left, right, (((1,), (1,)), ((), ())), preferred_element_type=F32)


def tn(left, right):
    return lax.dot_general(left, right, (((0,), (0,)), ((), ())), preferred_element_type=F32)


def part(index, size):
    return pl.ds(pl.multiple_of(index * size, size), size)


def round_up(number, step):
    return -(-number // step) * step


class Place:
    def __init__(self, wide):
        self.wide = wide
        self.w = lax.axis_index("wide")
        self.n = lax.axis_index("narrow")
        self.core = lax.rem(self.n, 2)
        self.xh = lax.div(self.n, 2)
        self.flip_core = (self.w, self.n + 1 - 2 * self.core)
        self.flip_x = (self.w, self.n + 2 - 4 * self.xh)
        self.bits = tuple(range(wide.bit_length() - 1))

    def bit(self, dim):
        return self.xh if dim == X else lax.rem(lax.div(self.w, 2**dim), 2)

    def partner(self, dim):
        if dim == X:
            return self.flip_x
        return (self.w + (1 - 2 * self.bit(dim)) * 2**dim, self.n)

    def on_wide(self, w):
        return (w, self.n)


def greet(partners, place, whole_wide):
    barrier = pltpu.get_barrier_semaphore()
    for partner in partners:
        pl.semaphore_signal(barrier, inc=1, device_id=partner, device_id_type=MESH)
    count = len(partners)
    if whole_wide:

        def one(step, carry):
            pl.semaphore_signal(
                barrier,
                inc=1,
                device_id=place.on_wide(lax.rem(place.w + step, place.wide)),
                device_id_type=MESH,
            )
            return carry

        lax.fori_loop(1, place.wide, one, 0)
        count += place.wide - 1
    pl.semaphore_wait(barrier, count)


def remote(src, dst, send, recv, device):
    return pltpu.make_async_remote_copy(
        src_ref=src, dst_ref=dst, send_sem=send, recv_sem=recv, device_id=device, device_id_type=MESH
    )


def segment_ends(lens):
    ends = []
    total = jnp.int32(0)
    for slot in range(lens.shape[1]):
        total = total + lens[0, slot]
        ends.append(total)
    return ends


def count_ends(ends, spots):
    total = jnp.zeros_like(spots)
    for end in ends:
        total = total + jnp.where(spots >= end, 1, 0)
    return total


def segment_setup(place, ends, rate_row, rows, gate_ref, keep_ref, reach_ref, later_first):
    anchor = place.w * rows
    col_local = lax.broadcasted_iota(jnp.int32, (rows, 1), 0)
    row_local = lax.broadcasted_iota(jnp.int32, (1, rows), 1)
    col_seg = count_ends(ends, col_local + anchor)
    row_seg = count_ends(ends, row_local + anchor)
    before = jnp.int32(0)
    last = jnp.int32(0)
    for end in ends:
        before = before + jnp.where(anchor - 1 >= end, 1, 0)
        last = last + jnp.where(anchor + rows - 1 >= end, 1, 0)
    before = jnp.where(place.w > 0, before, -1)
    col_live = (col_local + anchor) < ends[-1]
    row_live = (row_local + anchor) < ends[-1]
    rates = rate_row[...]
    steps = col_local.astype(F32)
    gate_ref[...] = jnp.exp(-(steps + 1.0) * rates) * jnp.where(
        (col_seg == before) & col_live, 1.0, 0.0
    )
    keep_ref[...] = jnp.exp(-(rows - 1.0 - steps) * rates) * jnp.where(
        (col_seg == last) & col_live, 1.0, 0.0
    )
    gap = col_local - row_local if later_first else row_local - col_local
    reaches = (gap >= 0) & (col_seg == row_seg) & row_live & col_live
    reach_ref[...] = jnp.where(reaches, gap.astype(F32), -1.0)


def decay_of(reach, rate):
    return jnp.where(reach >= 0.0, jnp.exp(-rate * reach), 0.0)


def scatter_states(place, local, arrived, sends, recvs, chunk):
    def one(step, carry):
        target = lax.rem(place.w + step, place.wide)
        remote(
            local.at[part(target, chunk)],
            arrived.at[place.w],
            sends.at[target],
            recvs.at[place.w],
            place.on_wide(target),
        ).start()
        return carry

    lax.fori_loop(1, place.wide, one, 0)
    arrived[place.w] = local[part(place.w, chunk), :]


def wait_states(place, local, arrived, sends, recvs, chunk):
    def one(step, carry):
        source = lax.rem(place.w + step, place.wide)
        copy = remote(
            local.at[part(source, chunk)],
            arrived.at[source],
            sends.at[source],
            recvs.at[source],
            place.on_wide(source),
        )
        copy.wait_recv()
        copy.wait_send()
        return carry

    lax.fori_loop(1, place.wide, one, 0)


def join_states(place, ends, rate, rows, arrived, joined, backward):
    shape = arrived.shape[1:]
    fade = jnp.exp(jnp.full((1, shape[1]), -1.0 * rows, F32) * rate)

    def one(step, state):
        block = place.wide - 1 - step if backward else step
        joined[block] = state.astype(BF16)
        cuts = jnp.int32(0)
        for end in ends:
            inside = (end >= block * rows) & (end <= block * rows + rows - 1)
            cuts = cuts + jnp.where(inside, 1, 0)
        flag = jnp.where((cuts == 0) & (block > 0), 1.0, 0.0)
        return (fade * flag) * state + arrived[block].astype(F32)

    lax.fori_loop(0, place.wide, one, jnp.zeros(shape, F32))


def return_states(place, joined, entering, sends, recvs, chunk):
    def one(step, carry):
        target = lax.rem(place.w + step, place.wide)
        remote(
            joined.at[target],
            entering.at[part(place.w, chunk)],
            sends.at[target],
            recvs.at[place.w],
            place.on_wide(target),
        ).start()
        return carry

    lax.fori_loop(1, place.wide, one, 0)
    entering[part(place.w, chunk), :] = joined[place.w]


def wait_returned(place, joined, entering, sends, recvs, chunk):
    def one(step, carry):
        source = lax.rem(place.w + step, place.wide)
        copy = remote(
            joined.at[source],
            entering.at[part(source, chunk)],
            sends.at[source],
            recvs.at[source],
            place.on_wide(source),
        )
        copy.wait_recv()
        copy.wait_send()
        return carry

    lax.fori_loop(1, place.wide, one, 0)


class Unit:
    def __init__(self, place, dims, acc, out, shift, recvs, sems, is_core, by_columns):
        self.place, self.dims, self.acc, self.out, self.shift = place, dims, acc, out, shift
        self.recvs, self.sems, self.is_core = recvs, sems, is_core
        self.stage = None
        self.count = 2 * len(dims) + is_core
        self.keep, self.give = [], []
        (rows, cols), row, col = acc.shape, 0, 0
        self.whole = (row, rows, col, cols)
        for dim in dims:
            bit = place.bit(dim)
            if dim == by_columns:
                cols //= 2
                self.keep.append((row, rows, col + bit * cols, cols))
                self.give.append((row, rows, col + (1 - bit) * cols, cols))
            else:
                rows //= 2
                self.keep.append((row + bit * rows, rows, col, cols))
                self.give.append((row + (1 - bit) * rows, rows, col, cols))
            row, rows, col, cols = self.keep[-1]

    def at(self, ref, region, shift=0):
        row, rows, col, cols = region
        down = pl.ds(pl.multiple_of(row, rows), rows)
        return ref.at[down, pl.ds(pl.multiple_of(col + shift, cols), cols)]

    def copy(self, stage):
        many = len(self.dims)
        send, recv = self.sems.at[2 * stage], self.sems.at[2 * stage + 1]
        if stage < many:
            src = self.at(self.acc, self.give[stage])
            return remote(src, self.recvs[stage], send, recv, self.place.partner(self.dims[stage]))
        if stage == 2 * many:
            region = self.at(self.out, self.whole, self.shift)
            return remote(region, region, send, recv, self.place.flip_core)
        step = 2 * many - 1 - stage
        dst = self.at(self.out, self.keep[step], self.shift)
        src = self.at(self.acc, self.keep[step]) if stage == many else dst
        return remote(src, dst, send, recv, self.place.partner(self.dims[step]))

    def local(self):
        return pltpu.make_async_copy(
            self.at(self.acc, self.keep[-1]),
            self.at(self.out, self.keep[-1], self.shift),
            self.sems.at[2 * self.count],
        )

    def advance(self):
        many = len(self.dims)
        if self.stage is None:
            self.stage = 0
        elif self.stage < self.count:
            self.copy(self.stage).wait_recv()
            if self.stage < many:
                row, rows, col, cols = self.keep[self.stage]
                add_into(self.acc, row, pl.ds(pl.multiple_of(col, cols), cols), self.recvs[self.stage])
            elif self.stage == many:
                self.local().wait()
            self.stage += 1
        if self.stage < self.count:
            self.copy(self.stage).start()
            if self.stage == many:
                self.local().start()

    def close(self):
        while self.stage < self.count:
            self.advance()
        for stage in range(self.count):
            self.copy(stage).wait_send()


def add_into(acc, base, cols, other):
    rows = other.shape[0]
    tile = math.gcd(rows, 128)

    @pl.loop(0, rows // tile)
    def _(i):
        here = pl.ds(pl.multiple_of(base + i * tile, tile), tile)
        acc[here, cols] = acc[here, cols] + other[part(i, tile), :]


Y, A, B, X = 0, 1, 2, 9
D0, D1, L0, L1, R0, R1, O, G, Q, K, V = range(11)
S1, S2, S3, S5, S6, WO, WG, WQ, WK, WV, INSIDE, JOIN, OUT, OUTX, GAIN = range(20, 35)
DIMS = {
    D0: (A, B, Y),
    D1: (Y, A, B),
    L0: (Y, A, B),
    L1: (Y, A, B),
    R0: (A, Y, B),
    R1: (Y, B, A),
    O: (X, Y, A, B),
    G: (X, Y, A, B),
    Q: (X, Y, A, B),
    K: (X, Y, A, B),
    V: (X, Y, A, B),
}
ORDER = (
    L1, D0, S1, S2, R1, R0, S3, WO, WG, INSIDE, INSIDE, L1, R0, INSIDE, R1, INSIDE, L0, JOIN, INSIDE, R0, O,
    INSIDE, INSIDE, INSIDE, R1, WQ, L0, R1, S5, G, L1, R0, O, WK, WV, R1, D1, S6, G, O, Q, R0, S6, GAIN, G,
    D1, K, O, Q, GAIN, G, R0, R1, O, OUTX, GAIN, K, V, G, R0, R1, GAIN, Q, O, K, V, G, GAIN, Q, K, O, V, OUT,
    GAIN, Q, G, K, V, Q, L1, K, O, V, D0, Q, O, V, L1, K, D1, G, D0, L0, L1, G, D1, L0, D0, Q, D1, L1, Q, D0,
    V, D1, L0, K, D0, K, L0, D1, V, D0, L0, V,
)


def tall_of(wide, hidden):
    return (wide // 2) * round_up(-(-hidden // (wide // 2)), 16)


def dims_of(name, wide):
    return DIMS[name] + tuple(range(3, wide.bit_length() - 1))


def arrivals(name, wide, rows, cols):
    shapes = []
    for dim in dims_of(name, wide):
        if name < O and dim == Y:
            cols //= 2
        else:
            rows //= 2
        shapes.append((rows, cols))
    return shapes


def backward_body(wide, heads, eps, r):
    p = Place(wide)
    rows, width = r.gn2.shape
    head = width // heads
    half = width // 2
    tile = 128
    chunk = width // wide
    mine = part(p.core, half)
    theirs = part(1 - p.core, half)

    greet([p.flip_core, p.flip_x], p, True)

    u = {}
    for name in range(D0, V + 1):
        recvs = [r.recv[name, step] for step in range(len(dims_of(name, wide)))]
        if name < O:
            which, cut = divmod(name - D0, 2)
            acc, out, shift = r.p_v.at[which, :, pl.ds(cut * half, half)], r.out_f[which], cut * half
        else:
            acc, out, shift = r.acc.at[name - O], r.out_a[name - O], p.core * half
        u[name] = Unit(
            p, dims_of(name, wide), acc, out, shift, recvs, r.usem.at[name - D0], name >= O, Y if name < O else None
        )

    loads, landed = {}, set()

    def load(key, src, dst):
        loads[key] = pltpu.make_async_copy(src, dst, r.lsem.at[len(loads)])
        loads[key].start()

    def need(*keys):
        for key in keys:
            if key not in landed:
                loads[key].wait()
                landed.add(key)

    for i, src in enumerate((r.p_d, r.p_l, r.p_r)):
        load(i, src, r.p_v.at[i, pl.ds(0, src.shape[0])])
    load("gn2", r.gn2, r.gn2_v)
    load("hidden", r.hidden, r.hid_v)
    load("cot", r.cot, r.cot_v)
    load("wo", r.wo, r.wa)
    load("flat", r.flat, r.flat_v)
    load("gate", r.gate, r.gate_v)
    load("ko", r.ko, r.ko_v)
    load("q", r.q, r.q_v)
    out_x = remote(r.outx, r.out_rx, r.osem.at[2], r.osem.at[3], p.flip_x)
    to_sib = [
        remote(r.mixed, r.mix_v.at[1], r.csem.at[0], r.csem.at[1], p.flip_core),
        remote(r.n1, r.n1_v.at[1], r.csem.at[2], r.csem.at[3], p.flip_core),
    ]
    for copy in to_sib:
        copy.start()
    load("mixed", r.mixed, r.mix_v.at[0])
    load("n1", r.n1, r.n1_v.at[0])
    load("k", r.k, r.k_v)
    load("v", r.v, r.v_v)
    load("sin", r.sin, r.sin_v)
    load("dq", r.dq, r.dq_v)
    load("dk", r.dk, r.dk_v)
    load("wk", r.wk, r.wc)
    load("wv", r.wv, r.wd)
    ends = segment_ends(r.lens)
    halves = {}

    def send_half(key, src):
        slot = key - O
        halves[key] = remote(
            src.at[:, theirs], r.sib.at[slot], r.csem.at[4 + 2 * slot], r.csem.at[5 + 2 * slot], p.flip_core
        )
        halves[key].start()

    def fold(x):
        return jnp.sum(x.reshape(x.shape[0] // 8, 8, x.shape[1]), axis=0)

    def second_norm():
        r.gsum[...] = jnp.zeros_like(r.gsum)
        need("gn2", "hidden", "cot")

        @pl.loop(0, rows // tile)
        def _(i):
            here = part(i, tile)
            hid = r.hid_v[here, :]
            scale = lax.rsqrt(jnp.mean(hid * hid, axis=-1, keepdims=True) + eps)
            unit = hid * scale
            up = r.gn2_v[here, :]
            r.gsum[1] += fold(up * unit)
            up = up * r.fgain[...]
            down = scale * (up - unit * jnp.mean(up * unit, axis=-1, keepdims=True))
            down = down + r.cot_v[here, :].astype(F32)
            r.hid_v[here, :] = down
            r.gb[here, :] = down.astype(BF16)

        load("tok", r.tokens, r.cot_v)
        send_half(O, r.gb)

    def gates():
        need("wo", "flat", "gate", "ko")

        @pl.loop(0, rows // 256)
        def _(i):
            here = part(i, 256)
            gm = nt(r.gb[here, :], r.wa[...])
            flat = r.flat_v[here, :].astype(F32)
            r.gg[here, :] = (gm * flat).astype(BF16)
            gm = gm * r.gate_v[here, :].astype(F32)
            ko = r.ko_v[here, :]
            for h in range(heads):
                cols = slice(h * head, (h + 1) * head)
                up, unit = gm[:, cols], flat[:, cols]
                mean = jnp.mean(up * unit, axis=-1, keepdims=True)
                r.ga[here, cols] = (ko[:, h : h + 1] * (up - unit * mean)).astype(BF16)

        send_half(G, r.gg)
        load("wq", r.wq, r.wa)

    def states():
        segment_setup(p, ends, r.rate_row, rows, r.gate_in, r.keep_out, r.reach, False)
        need("q")
        for h in range(heads):
            cols = slice(h * head, (h + 1) * head)
            gated = (r.q_v[:, cols].astype(F32) * r.gate_in[:, h : h + 1]).astype(BF16)
            r.state_a[pl.ds(h * head, head), :] = tn(gated, r.ga[:, cols]).astype(BF16)
        scatter_states(p, r.state_a, r.arrived, r.ssem.at[0], r.ssem.at[1], chunk)

    def weight_unit(name, left, own):
        acc = r.acc.at[name - O]
        other = r.sib.at[name - O]
        halves[name].wait_recv()

        @pl.loop(0, width // 512)
        def _(i):
            here = part(i, 512)
            acc[here, :] = (
                tn(left[0, :, here], own[:, mine]) + tn(left[1, :, here], other[...])
            ).astype(BF16)

        u[name].advance()

    def weight_o():
        need("mixed")
        to_sib[0].wait_recv()
        weight_unit(O, r.mix_v, r.gb)

    def weight_g():
        need("n1")
        to_sib[1].wait_recv()
        weight_unit(G, r.n1_v, r.gg)

    turn = [0, 0, 0]

    def inside():
        need("k", "v", "sin", "dq", "dk")
        first = turn[0]
        turn[0] += heads // 8

        def one(h, carry):
            cols = part(h, head)
            q, k, v, ga = r.q_v[:, cols], r.k_v[:, cols], r.v_v[:, cols], r.ga[:, cols]
            weight = decay_of(r.reach[...], r.rate_s[h])
            probs = (nt(k, q) * weight).astype(BF16)
            r.gv_f[:, cols] = nn(probs, ga)
            scores = (nt(v, ga) * weight).astype(BF16)
            r.gn2_v[:, cols] = nn(scores, q)
            pick = lax.broadcasted_iota(jnp.int32, (1, heads), 1) == h
            gate = jnp.sum(jnp.where(pick, r.gate_in[...], 0.0), axis=1, keepdims=True)
            gq = tn(scores, k) + nt(ga, r.sin_v[cols, :]) * gate
            r.gq[:, cols] = (gq * r.dq_v[:, cols].astype(F32)).astype(BF16)
            return carry

        lax.fori_loop(first, turn[0], one, 0)
        if turn[0] == heads:
            send_half(Q, r.gq)

    def join():
        wait_states(p, r.state_a, r.arrived, r.ssem.at[0], r.ssem.at[1], chunk)
        rate = r.rate_s[lax.div(p.w * chunk, head)]
        join_states(p, ends, rate, rows, r.arrived, r.joined, True)
        return_states(p, r.joined, r.state_b, r.ssem.at[2], r.ssem.at[3], chunk)

    def with_states():
        wait_returned(p, r.joined, r.state_b, r.ssem.at[2], r.ssem.at[3], chunk)
        for h in range(heads):
            cols = slice(h * head, (h + 1) * head)
            state = r.state_b[pl.ds(h * head, head), :]
            keep = r.keep_out[:, h : h + 1]
            gk = r.gn2_v[:, cols] + nt(r.v_v[:, cols], state) * keep
            r.flat_v[:, cols] = (gk * r.dk_v[:, cols].astype(F32)).astype(BF16)
            gv = r.gv_f[:, cols] + nn(r.k_v[:, cols], state) * keep
            r.gate_v[:, cols] = gv.astype(BF16)
        send_half(K, r.flat_v)
        send_half(V, r.gate_v)
        load("hidden_again", r.hidden, r.gn2_v)
        load("outown", r.outown, r.q_v)
        to_sib[0].wait_send()
        load("wg0", r.wg.at[pl.ds(0, rows)], r.mix_v.at[0])
        load("wg1", r.wg.at[pl.ds(rows, rows)], r.mix_v.at[1])

    def first_norm():
        need("wq", "wk", "wv", "wg0", "wg1", "tok")
        size = rows // 2
        here = pl.ds(turn[1] * size, size)
        turn[1] += 1
        up = (
            nt(r.gq[here, :], r.wa[...])
            + nt(r.flat_v[here, :], r.wc[...])
            + nt(r.gate_v[here, :], r.wd[...])
            + jnp.concatenate([nt(r.gg[here, :], r.mix_v[i]) for i in range(2)], axis=1)
        )
        tok = r.cot_v[here, :].astype(F32)
        scale = lax.rsqrt(jnp.mean(tok * tok, axis=-1, keepdims=True) + eps)
        unit = tok * scale
        r.gsum[0] += fold(up * unit)
        up = up * r.again[...]
        down = scale * (up - unit * jnp.mean(up * unit, axis=-1, keepdims=True))
        r.hid_v[here, :] += down
        if turn[1] == 2:
            stores["gtok"].start()
            r.gains[0] = jnp.zeros_like(r.gains[0])
            for row in range(2):
                r.gains[0, pl.ds(row, 1), :] = jnp.sum(r.gsum[row], axis=0, keepdims=True)

    stores = {
        "gtok": pltpu.make_async_copy(r.hid_v, r.gtok, r.osem.at[0]),
        "gain": pltpu.make_async_copy(r.gains.at[2 + len(p.bits)], r.out_gain, r.osem.at[1]),
        "out": pltpu.make_async_copy(r.k_v, r.out, r.osem.at[4]),
    }

    def output():
        out_x.wait_recv()
        need("hidden_again", "outown")

        @pl.loop(0, rows // tile)
        def _(i):
            here = part(i, tile)
            total = r.q_v[here, :].astype(F32) + r.out_rx[here, :].astype(F32)
            r.k_v[here, :] = (r.gn2_v[here, :] + total).astype(BF16)

        stores["out"].start()

    gain_to = [p.flip_core, p.flip_x] + [p.partner(bit) for bit in p.bits]
    many = len(gain_to)

    def gain_copy(step):
        return remote(
            r.gains.at[step], r.grecv.at[step], r.gsem.at[2 * step], r.gsem.at[2 * step + 1], gain_to[step]
        )

    def gain():
        step = turn[2]
        turn[2] += 1
        if step:
            gain_copy(step - 1).wait_recv()
            r.gains[step] = r.gains[step - 1] + r.grecv[step - 1]
        if step < many:
            gain_copy(step).start()
        else:
            stores["gain"].start()

    steps = {
        S1: second_norm,
        S2: gates,
        S3: states,
        WO: weight_o,
        WG: weight_g,
        WQ: lambda: weight_unit(Q, r.n1_v, r.gq),
        WK: lambda: weight_unit(K, r.n1_v, r.flat_v),
        WV: lambda: weight_unit(V, r.n1_v, r.gate_v),
        INSIDE: inside,
        JOIN: join,
        S5: with_states,
        S6: first_norm,
        OUT: output,
        OUTX: out_x.start,
        GAIN: gain,
    }
    for step in ORDER:
        if step in u:
            if step < O:
                need((step - D0) // 2)
            u[step].advance()
        else:
            steps[step]()
    while turn[2] <= many:
        gain()
    for one in u.values():
        one.close()
    for copy in stores.values():
        copy.wait()
    out_x.wait_send()
    to_sib[1].wait_send()
    for copy in halves.values():
        copy.wait_send()
    for step in range(many):
        gain_copy(step).wait_send()


def backward_call(wide, heads, eps, arrays):
    rows, width = arrays["gn2"].shape
    hidden = arrays["p_l"].shape[0]
    half = width // 2
    tall = tall_of(wide, hidden)
    bits = wide.bit_length() - 1
    specs = {"lens": IN_SMEM, "rate_s": IN_SMEM, "rate_row": IN_VMEM, "fgain": IN_VMEM, "again": IN_VMEM}
    ins = {nm: (a, specs.get(nm, ANY)) for nm, a in arrays.items()}
    sds = jax.ShapeDtypeStruct
    outs = {("a", i): sds((width, width), BF16) for i in range(5)}
    outs.update({("f", i): sds((tall, width), BF16) for i in range(3)})
    outs["out"] = sds((rows, width), BF16)
    outs["gtok"] = sds((rows, width), F32)
    outs["out_gain"] = sds((8, width), F32)
    VM = pltpu.VMEM
    dma = pltpu.SemaphoreType.DMA
    scratch = dict(
        gn2_v=VM((rows, width), F32),
        hid_v=VM((rows, width), F32),
        gv_f=VM((rows, width), F32),
        cot_v=VM((rows, width), BF16),
        flat_v=VM((rows, width), BF16),
        gate_v=VM((rows, width), BF16),
        ko_v=VM((rows, heads), F32),
        q_v=VM((rows, width), BF16),
        k_v=VM((rows, width), BF16),
        v_v=VM((rows, width), BF16),
        dq_v=VM((rows, width), BF16),
        dk_v=VM((rows, width), BF16),
        mix_v=VM((2, rows, width), BF16),
        n1_v=VM((2, rows, width), BF16),
        sin_v=VM((width, width // heads), BF16),
        wa=VM((width, width), BF16),
        wc=VM((width, width), BF16),
        wd=VM((width, width), BF16),
        gb=VM((rows, width), BF16),
        out_rx=VM((rows, width), BF16),
        gg=VM((rows, width), BF16),
        ga=VM((rows, width), BF16),
        gq=VM((rows, width), BF16),
        sib=VM((5, rows, half), BF16),
        gate_in=VM((rows, heads), F32),
        keep_out=VM((rows, heads), F32),
        reach=VM((rows, rows), F32),
        state_a=VM((width, width // heads), BF16),
        state_b=VM((width, width // heads), BF16),
        arrived=VM((wide, width // wide, width // heads), BF16),
        joined=VM((wide, width // wide, width // heads), BF16),
        acc=VM((5, width, half), BF16),
        p_v=VM((3, tall, width), BF16),
        gsum=VM((2, 8, width), F32),
        gains=VM((3 + bits, 8, width), F32),
        grecv=VM((2 + bits, 8, width), F32),
        lsem=dma((32,)),
        csem=dma((14,)),
        ssem=dma((4, wide)),
        usem=dma((11, 4 * (bits + 1) + 4)),
        gsem=dma((4 + 2 * bits,)),
        osem=dma((5,)),
    )
    for name in range(D0, V + 1):
        for step, shape in enumerate(arrivals(name, wide, tall if name < O else width, half)):
            scratch["r", name, step] = VM(shape, BF16)
    return call_kernel(
        lambda r: backward_body(wide, heads, eps, r), "attention_backward", 3, ins, outs, scratch, 20 * 10**9
    )


PIECES = 4


def forward_body(wide, heads, eps, r):
    p = Place(wide)
    rows, width = r.tokens.shape
    head = width // heads
    tile = 128
    chunk = width // wide
    size = rows // PIECES
    greet([p.flip_core, p.flip_x], p, True)

    def spot(c, second):
        return pl.ds(2 * rows + (2 * c + second) * size, size)

    gather = [
        remote(r.cot.at[pl.ds(c * size, size)], r.cotall.at[spot(c, 0)], r.xsem.at[0, c], r.xsem.at[1, c], p.flip_x)
        for c in range(PIECES)
    ]
    onward = [
        remote(r.cotall.at[spot(c, 0)], r.cotall.at[spot(c, 1)], r.xsem.at[2, c], r.xsem.at[3, c], p.flip_core)
        for c in range(PIECES)
    ]
    across = remote(r.cot, r.cotall.at[pl.ds(rows, rows)], r.xsem.at[4, 0], r.xsem.at[4, 1], p.flip_core)
    for copy in gather:
        copy.start()

    loads = {}

    def load(key, src, dst):
        loads[key] = pltpu.make_async_copy(src, dst, r.lsem.at[len(loads)])
        loads[key].start()

    def need(key):
        loads[key].wait()

    load("tokens", r.tokens, r.tok_v)
    load("wk", r.wk, r.wk_v)
    load("wv", r.wv, r.wv_v)
    load("wq", r.wq, r.wq_v)
    load("wg", r.wg, r.wg_v)
    load("wo", r.wo, r.wo_v)
    load("keep", r.cot, r.cotall.at[pl.ds(0, rows)])
    across.start()
    stores = []

    def store(src, dst):
        copy = pltpu.make_async_copy(src, dst, r.stsem.at[len(stores)])
        copy.start()
        stores.append(copy)

    def pass_on(c):
        gather[c].wait_recv()
        onward[c].start()

    ends = segment_ends(r.lens)
    segment_setup(p, ends, r.rate_row, rows, r.gate_in, r.keep_out, r.reach, True)
    need("tokens")

    @pl.loop(0, rows // tile)
    def _(i):
        here = part(i, tile)
        tok = r.tok_v[here, :].astype(F32)
        scale = lax.rsqrt(jnp.mean(tok * tok, axis=-1, keepdims=True) + eps)
        r.n1_v[here, :] = (tok * scale * r.again[...]).astype(BF16)

    store(r.n1_v, r.n1)

    def silu_rows(weight, act, slope):
        @pl.loop(0, rows // 256)
        def _(i):
            here = part(i, 256)
            pre = nn(r.n1_v[here, :], weight[...])
            gate = lax.logistic(pre)
            act[here, :] = (pre * gate).astype(BF16)
            slope[here, :] = (gate * (1.0 + pre * (1.0 - gate))).astype(BF16)

    def plain_rows(weight, dst):
        @pl.loop(0, rows // 256)
        def _(i):
            here = part(i, 256)
            dst[here, :] = nn(r.n1_v[here, :], weight[...]).astype(BF16)

    need("wk")
    silu_rows(r.wk_v, r.k_v, r.dk_v)
    need("wv")
    plain_rows(r.wv_v, r.v_v)
    for h in range(heads):
        cols = slice(h * head, (h + 1) * head)
        kept = (r.k_v[:, cols].astype(F32) * r.keep_out[:, h : h + 1]).astype(BF16)
        r.state_a[pl.ds(h * head, head), :] = tn(kept, r.v_v[:, cols]).astype(BF16)
    scatter_states(p, r.state_a, r.arrived, r.ssem.at[0], r.ssem.at[1], chunk)
    store(r.k_v, r.k)
    store(r.dk_v, r.dk)
    store(r.v_v, r.v)
    need("wq")
    silu_rows(r.wq_v, r.q_v, r.dq_v)
    store(r.q_v, r.q)
    store(r.dq_v, r.dq)

    def inside(h, carry):
        cols = part(h, head)
        weight = decay_of(r.reach[...], r.rate_s[h])
        probs = (nt(r.q_v[:, cols], r.k_v[:, cols]) * weight).astype(BF16)
        r.raw_f[:, cols] = nn(probs, r.v_v[:, cols])
        return carry

    lax.fori_loop(0, heads // 2, inside, 0)
    pass_on(0)
    wait_states(p, r.state_a, r.arrived, r.ssem.at[0], r.ssem.at[1], chunk)
    join_states(p, ends, r.rate_s[lax.div(p.w * chunk, head)], rows, r.arrived, r.joined, False)
    return_states(p, r.joined, r.state_b, r.ssem.at[2], r.ssem.at[3], chunk)
    need("wg")
    plain_rows(r.wg_v, r.gate_v)
    store(r.gate_v, r.gate)
    lax.fori_loop(heads // 2, heads, inside, 0)
    pass_on(1)
    wait_returned(p, r.joined, r.state_b, r.ssem.at[2], r.ssem.at[3], chunk)
    store(r.state_b, r.sin)
    for h in range(heads):
        cols = slice(h * head, (h + 1) * head)
        state = r.state_b[pl.ds(h * head, head), :]
        raw = r.raw_f[:, cols] + nn(r.q_v[:, cols], state) * r.gate_in[:, h : h + 1]
        scale = lax.rsqrt(jnp.mean(raw * raw, axis=-1, keepdims=True) + eps)
        unit = raw * scale
        r.ko_v[:, h : h + 1] = scale
        r.flat_v[:, cols] = unit.astype(BF16)
        r.mix_v[:, cols] = (unit * r.gate_v[:, cols].astype(F32)).astype(BF16)
    store(r.ko_v, r.ko)
    store(r.flat_v, r.flat)
    store(r.mix_v, r.mixed)
    need("wo")

    @pl.loop(0, rows // 256)
    def _(i):
        here = part(i, 256)
        hid = r.tok_v[here, :].astype(F32) + nn(r.mix_v[here, :], r.wo_v[...])
        scale = lax.rsqrt(jnp.mean(hid * hid, axis=-1, keepdims=True) + eps)
        r.hid_v[here, :] = hid
        r.n2_v[here, :] = (hid * scale * r.fgain[...]).astype(BF16)

    store(r.n2_v, r.n2)
    store(r.hid_v, r.hidden)
    for c in range(2, PIECES):
        pass_on(c)
    across.wait_recv()
    across.wait_send()
    need("keep")
    for copy in onward:
        copy.wait_recv()
    for copy in onward + gather:
        copy.wait_send()
    for copy in stores:
        copy.wait()


def forward_call(wide, heads, eps, arrays):
    rows, width = arrays["tokens"].shape
    specs = {"lens": IN_SMEM, "rate_s": IN_SMEM, "rate_row": IN_VMEM, "fgain": IN_VMEM, "again": IN_VMEM}
    ins = {nm: (a, specs.get(nm, ANY)) for nm, a in arrays.items()}
    sds = jax.ShapeDtypeStruct
    outs = {nm: sds((rows, width), BF16) for nm in ("n1", "q", "k", "v", "dq", "dk", "gate", "flat", "mixed", "n2")}
    outs["ko"] = sds((rows, heads), F32)
    outs["hidden"] = sds((rows, width), F32)
    outs["sin"] = sds((width, width // heads), BF16)
    outs["cotall"] = sds((4 * rows, width), BF16)
    V = pltpu.VMEM
    dma = pltpu.SemaphoreType.DMA
    scratch = {nm + "_v": V((rows, width), BF16) for nm in ("tok", "n1", "q", "k", "v", "dq", "dk", "gate", "flat", "mix", "n2")}
    scratch.update({nm + "_v": V((width, width), BF16) for nm in ("wq", "wk", "wv", "wg", "wo")})
    scratch.update(
        raw_f=V((rows, width), F32),
        hid_v=V((rows, width), F32),
        ko_v=V((rows, heads), F32),
        gate_in=V((rows, heads), F32),
        keep_out=V((rows, heads), F32),
        reach=V((rows, rows), F32),
        state_a=V((width, width // heads), BF16),
        state_b=V((width, width // heads), BF16),
        arrived=V((wide, width // wide, width // heads), BF16),
        joined=V((wide, width // wide, width // heads), BF16),
        lsem=dma((8,)),
        stsem=dma((16,)),
        xsem=dma((5, PIECES)),
        ssem=dma((4, wide)),
    )
    return call_kernel(
        lambda r: forward_body(wide, heads, eps, r), "attention_forward", 1, ins, outs, scratch, 8 * 10**9
    )


def gated_body(wide, r):
    p = Place(wide)
    rows, width = r.n2.shape
    hidden = r.wl.shape[0]
    size = rows // PIECES
    group = 256
    greet([p.flip_core, p.flip_x], p, False)

    def spot(c, second):
        return pl.ds(2 * rows + (2 * c + second) * size, size)

    def remotes(row, src_of, dst_of, device):
        return [
            remote(src_of(c), dst_of(c), r.xsem.at[row, c], r.xsem.at[row + 1, c], device)
            for c in range(PIECES)
        ]

    def piece(ref):
        return lambda c: ref.at[pl.ds(c * size, size)]

    gather = remotes(0, piece(r.n2), lambda c: r.X.at[spot(c, 0)], p.flip_x)
    onward = remotes(2, lambda c: r.X.at[spot(c, 0)], lambda c: r.X.at[spot(c, 1)], p.flip_core)
    across = remote(r.n2, r.X.at[pl.ds(rows, rows)], r.xsem.at[16, 0], r.xsem.at[16, 1], p.flip_core)
    back_core = remotes(4, piece(r.to_core), piece(r.from_core), p.flip_core)
    back_own = remotes(6, piece(r.own_core), piece(r.own_from), p.flip_core)
    back_x = remotes(8, piece(r.to_x), piece(r.from_x), p.flip_x)
    out_core = remotes(10, piece(r.o_to_core), piece(r.o_from_core), p.flip_core)
    out_own = remotes(12, piece(r.o_own_core), piece(r.o_own_from), p.flip_core)

    for copy in gather:
        copy.start()
    across.start()
    loads = {}

    def load(key, src, dst):
        loads[key] = pltpu.make_async_copy(src, dst, r.lsem.at[len(loads)])
        loads[key].start()

    def need(*keys):
        for key in keys:
            loads[key].wait()

    load("x", r.n2, r.X.at[pl.ds(0, rows)])
    load("wl", r.wl, r.wl_v)
    load("wr", r.wr, r.wr_v)
    load("wd", r.wd, r.wd_v)
    load("g", r.cotall, r.G)
    stores = []

    def store(src, dst):
        copy = pltpu.make_async_copy(src, dst, r.stsem.at[len(stores)])
        copy.start()
        stores.append(copy)

    def act(here):
        x = r.X[here, :]
        left = nt(x, r.wl_v[...])
        right = nt(x, r.wr_v[...])
        r.prod[here, :] = (left * right).astype(BF16)
        up = nt(r.G[here, :], r.wd_v[...])
        r.gl[here, :] = (up * right).astype(BF16)
        r.gr[here, :] = (up * left).astype(BF16)
        return nn(r.gl[here, :], r.wl_v[...]) + nn(r.gr[here, :], r.wr_v[...])

    def out_part(here):
        return nn(r.prod[here, :], r.wd_v[...])

    need("x", "wl", "wr", "wd", "g")

    @pl.loop(0, rows // group)
    def _(i):
        r.own[part(i, group), :] = act(part(i, group))

    across.wait_recv()

    @pl.loop(0, rows // group)
    def _(i):
        r.own_core[part(i, group), :] = act(pl.ds(pl.multiple_of(rows + i * group, group), group)).astype(BF16)

    for copy in back_own:
        copy.start()
    gather[0].wait_recv()
    onward[0].start()

    def out_own_rows(i):
        r.o_own[part(i, group), :] = out_part(part(i, group))

    def out_core_rows(i):
        r.o_own_core[part(i, group), :] = out_part(pl.ds(rows + i * group, group)).astype(BF16)

    def far(c):
        here = pl.ds(2 * rows + 2 * c * size, 2 * size)
        got = act(here)
        r.keep[pl.ds(c * size, size), :] = got[:size]
        r.to_core[pl.ds(c * size, size), :] = got[size:].astype(BF16)
        back_core[c].start()

    def far_send(c):
        back_core[c].wait_recv()
        here = pl.ds(c * size, size)
        r.to_x[here, :] = (r.keep[here, :] + r.from_core[here, :].astype(F32)).astype(BF16)
        back_x[c].start()

    fill = [
        lambda: out_own_rows(0),
        lambda: out_own_rows(1),
        lambda: out_core_rows(0),
        lambda: out_core_rows(1),
    ]
    for c in range(PIECES):
        fill[c]()
        onward[c].wait_recv()
        far(c)
        if c + 1 < PIECES:
            if c:
                far_send(c - 1)
            gather[c + 1].wait_recv()
            onward[c + 1].start()
    for copy in out_own:
        copy.start()
    far_send(PIECES - 2)

    def out_far(c):
        got = out_part(pl.ds(2 * rows + 2 * c * size, 2 * size))
        r.o_keep[pl.ds(c * size, size), :] = got[:size]
        r.o_to_core[pl.ds(c * size, size), :] = got[size:].astype(BF16)
        out_core[c].start()

    out_far(0)
    out_far(1)
    far_send(PIECES - 1)
    out_far(2)
    out_far(3)

    def weight(left, right, dst, out):
        cut = 384 if hidden > 384 else hidden
        for base, extent in ((0, cut), (cut, hidden - cut)):
            if extent:
                here = pl.ds(base, extent)
                dst[here, :] = tn(left[:, here], right[...]).astype(BF16)
        store(dst, out)

    weight(r.prod, r.G, r.pd_v, r.p_d)
    weight(r.gl, r.X, r.pl_v, r.p_l)
    weight(r.gr, r.X, r.pr_v, r.p_r)

    for c in range(PIECES):
        out_core[c].wait_recv()
        out_own[c].wait_recv()
        here = pl.ds(c * size, size)
        r.o_x[here, :] = (r.o_keep[here, :] + r.o_from_core[here, :].astype(F32)).astype(BF16)
        r.o_sum[here, :] = (r.o_own[here, :] + r.o_own_from[here, :].astype(F32)).astype(BF16)
    store(r.o_x, r.outx)
    store(r.o_sum, r.outown)
    for c in range(PIECES):
        back_own[c].wait_recv()
        back_x[c].wait_recv()
        here = pl.ds(c * size, size)
        r.own[here, :] += r.own_from[here, :].astype(F32) + r.from_x[here, :].astype(F32)
    store(r.own, r.gn2)
    across.wait_send()
    for copies in (gather, onward, back_core, back_own, back_x, out_core, out_own):
        for copy in copies:
            copy.wait_send()
    for copy in stores:
        copy.wait()


def gated_call(wide, arrays):
    rows, width = arrays["n2"].shape
    hidden = arrays["wl"].shape[0]
    ins = {nm: (a, ANY) for nm, a in arrays.items()}
    sds = jax.ShapeDtypeStruct
    outs = dict(
        gn2=sds((rows, width), F32),
        outx=sds((rows, width), BF16),
        outown=sds((rows, width), BF16),
        p_d=sds((hidden, width), BF16),
        p_l=sds((hidden, width), BF16),
        p_r=sds((hidden, width), BF16),
    )
    V = pltpu.VMEM
    dma = pltpu.SemaphoreType.DMA
    few = ("to_core", "from_core", "own_core", "own_from", "to_x", "from_x")
    few += ("o_to_core", "o_from_core", "o_own_core", "o_own_from", "o_x", "o_sum")
    scratch = {nm: V((rows, width), BF16) for nm in few}
    scratch.update({nm: V((rows, width), F32) for nm in ("own", "keep", "o_own", "o_keep")})
    scratch.update({nm: V((4 * rows, hidden), BF16) for nm in ("prod", "gl", "gr")})
    scratch.update(
        X=V((4 * rows, width), BF16),
        G=V((4 * rows, width), BF16),
        wl_v=V((hidden, width), BF16),
        wr_v=V((hidden, width), BF16),
        wd_v=V((hidden, width), BF16),
        pl_v=V((hidden, width), BF16),
        pr_v=V((hidden, width), BF16),
        pd_v=V((hidden, width), BF16),
        xsem=dma((17, PIECES)),
        lsem=dma((5,)),
        stsem=dma((6,)),
    )
    return call_kernel(lambda r: gated_body(wide, r), "gated_unit", 2, ins, outs, scratch, 27 * 10**9)


def body(
    tokens,
    cotangent,
    lengths,
    decay_rate,
    attn_gain,
    w_query,
    w_key,
    w_value,
    w_gate,
    w_out,
    ffn_gain,
    w_left,
    w_right,
    w_down,
):
    wide = lax.axis_size("wide")
    heads = decay_rate.shape[0]
    hidden = w_down.shape[0]
    shared = dict(
        lens=lengths,
        rate_s=decay_rate,
        rate_row=decay_rate[None],
        fgain=ffn_gain[None],
        again=attn_gain[None],
        wq=w_query,
        wk=w_key,
        wv=w_value,
        wg=w_gate,
        wo=w_out,
        tokens=tokens[0],
        cot=cotangent[0],
    )
    first = forward_call(wide, heads, EPS, shared)
    second = gated_call(
        wide, dict(n2=first.pop("n2"), cotall=first.pop("cotall"), wl=w_left.T, wr=w_right.T, wd=w_down)
    )
    done = backward_call(wide, heads, EPS, {**shared, **first, **second})

    def full(name):
        key = ("a", name - O) if name >= O else ("f", (name - D0) // 2)
        return done[key].astype(F32)

    return (
        done["out"][None],
        done["gtok"][None],
        full(Q),
        full(K),
        full(V),
        full(G),
        full(O),
        done["out_gain"][0],
        done["out_gain"][1],
        full(L0)[:hidden].T,
        full(R0)[:hidden].T,
        full(D0)[:hidden],
    )


def solution(mesh):
    placed = (
        P("narrow", "wide", None),
        P("narrow", "wide", None),
        P("narrow", None),
        P(),
        P(),
        P(),
        P(),
        P(),
        P(),
        P(),
        P(),
        P(None, "narrow"),
        P(None, "narrow"),
        P("narrow", None),
    )
    return jax.shard_map(
        body,
        mesh=mesh,
        in_specs=placed,
        out_specs=(
            P("narrow", "wide", None),
            P("narrow", "wide", None),
            P(),
            P(),
            P(),
            P(),
            P(),
            P(),
            P(),
            P(None, "narrow"),
            P(None, "narrow"),
            P("narrow", None),
        ),
        check_vma=False,
    )
```

```python
import math

import jax
import jax.numpy as jnp
from jax import lax
from jax.experimental import pallas as pl
from jax.experimental.pallas import tpu as pltpu
from jax.sharding import PartitionSpec as P

EPS = 1e-06

MESH = pl.DeviceIdType.MESH
F32 = jnp.float32
BF16 = jnp.bfloat16
VMEM_BYTES = 62 * 1024 * 1024
ANY = pl.BlockSpec(memory_space=pl.ANY)
IN_VMEM = pl.BlockSpec(memory_space=pltpu.VMEM)
IN_SMEM = pl.BlockSpec(memory_space=pltpu.SMEM)


class Refs:
    def __init__(self, names, refs):
        self.recv, self.out_a, self.out_f = {}, {}, {}
        groups = {"r": self.recv, "a": self.out_a, "f": self.out_f}
        for name, ref in zip(names, refs, strict=True):
            if isinstance(name, str):
                setattr(self, name, ref)
            else:
                groups[name[0]][name[1:] if len(name) > 2 else name[1]] = ref


def call_kernel(body, name, number, ins, outs, scratch, cost):
    names = list(ins) + list(outs) + list(scratch)

    def kernel(*refs):
        body(Refs(names, refs))

    results = pl.pallas_call(
        kernel,
        name=name,
        out_shape=list(outs.values()),
        in_specs=[spec for _, spec in ins.values()],
        out_specs=[ANY] * len(outs),
        scratch_shapes=list(scratch.values()),
        cost_estimate=pl.CostEstimate(flops=cost, bytes_accessed=cost // 500, transcendentals=0),
        compiler_params=pltpu.CompilerParams(
            collective_id=number, has_side_effects=True, vmem_limit_bytes=VMEM_BYTES
        ),
    )(*[array for array, _ in ins.values()])
    return dict(zip(outs, results, strict=True))


def nn(left, right):
    return lax.dot_general(left, right, (((1,), (0,)), ((), ())), preferred_element_type=F32)


def nt(left, right):
    return lax.dot_general(left, right, (((1,), (1,)), ((), ())), preferred_element_type=F32)


def tn(left, right):
    return lax.dot_general(left, right, (((0,), (0,)), ((), ())), preferred_element_type=F32)


def part(index, size):
    return pl.ds(pl.multiple_of(index * size, size), size)


def round_up(number, step):
    return -(-number // step) * step


class Place:
    def __init__(self, wide):
        self.wide = wide
        self.w = lax.axis_index("wide")
        self.n = lax.axis_index("narrow")
        self.core = lax.rem(self.n, 2)
        self.xh = lax.div(self.n, 2)
        self.flip_core = (self.w, self.n + 1 - 2 * self.core)
        self.flip_x = (self.w, self.n + 2 - 4 * self.xh)
        self.bits = tuple(range(wide.bit_length() - 1))

    def bit(self, dim):
        return self.xh if dim == X else lax.rem(lax.div(self.w, 2**dim), 2)

    def partner(self, dim):
        if dim == X:
            return self.flip_x
        return (self.w + (1 - 2 * self.bit(dim)) * 2**dim, self.n)

    def on_wide(self, w):
        return (w, self.n)


def greet(partners, place, whole_wide):
    barrier = pltpu.get_barrier_semaphore()
    for partner in partners:
        pl.semaphore_signal(barrier, inc=1, device_id=partner, device_id_type=MESH)
    count = len(partners)
    if whole_wide:

        def one(step, carry):
            pl.semaphore_signal(
                barrier,
                inc=1,
                device_id=place.on_wide(lax.rem(place.w + step, place.wide)),
                device_id_type=MESH,
            )
            return carry

        lax.fori_loop(1, place.wide, one, 0)
        count += place.wide - 1
    pl.semaphore_wait(barrier, count)


def remote(src, dst, send, recv, device):
    return pltpu.make_async_remote_copy(
        src_ref=src, dst_ref=dst, send_sem=send, recv_sem=recv, device_id=device, device_id_type=MESH
    )


def segment_ends(lens):
    ends = []
    total = jnp.int32(0)
    for slot in range(lens.shape[1]):
        total = total + lens[0, slot]
        ends.append(total)
    return ends


def count_ends(ends, spots):
    total = jnp.zeros_like(spots)
    for end in ends:
        total = total + jnp.where(spots >= end, 1, 0)
    return total


def segment_setup(place, ends, rate_row, rows, gate_ref, keep_ref, reach_ref, later_first):
    anchor = place.w * rows
    col_local = lax.broadcasted_iota(jnp.int32, (rows, 1), 0)
    row_local = lax.broadcasted_iota(jnp.int32, (1, rows), 1)
    col_seg = count_ends(ends, col_local + anchor)
    row_seg = count_ends(ends, row_local + anchor)
    before = jnp.int32(0)
    last = jnp.int32(0)
    for end in ends:
        before = before + jnp.where(anchor - 1 >= end, 1, 0)
        last = last + jnp.where(anchor + rows - 1 >= end, 1, 0)
    before = jnp.where(place.w > 0, before, -1)
    col_live = (col_local + anchor) < ends[-1]
    row_live = (row_local + anchor) < ends[-1]
    rates = rate_row[...]
    steps = col_local.astype(F32)
    gate_ref[...] = jnp.exp(-(steps + 1.0) * rates) * jnp.where(
        (col_seg == before) & col_live, 1.0, 0.0
    )
    keep_ref[...] = jnp.exp(-(rows - 1.0 - steps) * rates) * jnp.where(
        (col_seg == last) & col_live, 1.0, 0.0
    )
    gap = col_local - row_local if later_first else row_local - col_local
    reaches = (gap >= 0) & (col_seg == row_seg) & row_live & col_live
    reach_ref[...] = jnp.where(reaches, gap.astype(F32), -1.0)


def decay_of(reach, rate):
    return jnp.where(reach >= 0.0, jnp.exp(-rate * reach), 0.0)


def scatter_states(place, local, arrived, sends, recvs, chunk):
    def one(step, carry):
        target = lax.rem(place.w + step, place.wide)
        remote(
            local.at[part(target, chunk)],
            arrived.at[place.w],
            sends.at[target],
            recvs.at[place.w],
            place.on_wide(target),
        ).start()
        return carry

    lax.fori_loop(1, place.wide, one, 0)
    arrived[place.w] = local[part(place.w, chunk), :]


def wait_states(place, local, arrived, sends, recvs, chunk):
    def one(step, carry):
        source = lax.rem(place.w + step, place.wide)
        copy = remote(
            local.at[part(source, chunk)],
            arrived.at[source],
            sends.at[source],
            recvs.at[source],
            place.on_wide(source),
        )
        copy.wait_recv()
        copy.wait_send()
        return carry

    lax.fori_loop(1, place.wide, one, 0)


def join_states(place, ends, rate, rows, arrived, joined, backward):
    shape = arrived.shape[1:]
    fade = jnp.exp(jnp.full((1, shape[1]), -1.0 * rows, F32) * rate)

    def one(step, state):
        block = place.wide - 1 - step if backward else step
        joined[block] = state.astype(BF16)
        cuts = jnp.int32(0)
        for end in ends:
            inside = (end >= block * rows) & (end <= block * rows + rows - 1)
            cuts = cuts + jnp.where(inside, 1, 0)
        flag = jnp.where((cuts == 0) & (block > 0), 1.0, 0.0)
        return (fade * flag) * state + arrived[block].astype(F32)

    lax.fori_loop(0, place.wide, one, jnp.zeros(shape, F32))


def return_states(place, joined, entering, sends, recvs, chunk):
    def one(step, carry):
        target = lax.rem(place.w + step, place.wide)
        remote(
            joined.at[target],
            entering.at[part(place.w, chunk)],
            sends.at[target],
            recvs.at[place.w],
            place.on_wide(target),
        ).start()
        return carry

    lax.fori_loop(1, place.wide, one, 0)
    entering[part(place.w, chunk), :] = joined[place.w]


def wait_returned(place, joined, entering, sends, recvs, chunk):
    def one(step, carry):
        source = lax.rem(place.w + step, place.wide)
        copy = remote(
            joined.at[source],
            entering.at[part(source, chunk)],
            sends.at[source],
            recvs.at[source],
            place.on_wide(source),
        )
        copy.wait_recv()
        copy.wait_send()
        return carry

    lax.fori_loop(1, place.wide, one, 0)


class Unit:
    def __init__(self, place, dims, acc, out, shift, recvs, sems, is_core, by_columns, first=0):
        self.place, self.dims, self.acc, self.out, self.shift = place, dims, acc, out, shift
        self.recvs, self.sems, self.is_core = recvs, sems, is_core
        self.first, self.stage = first, None
        self.count = 2 * len(dims) + is_core
        self.keep, self.give = [], []
        (rows, cols), row, col = acc.shape, 0, 0
        self.whole = (row, rows, col, cols)
        for dim in dims:
            bit = place.bit(dim)
            if dim == by_columns:
                cols //= 2
                self.keep.append((row, rows, col + bit * cols, cols))
                self.give.append((row, rows, col + (1 - bit) * cols, cols))
            else:
                rows //= 2
                self.keep.append((row + bit * rows, rows, col, cols))
                self.give.append((row + (1 - bit) * rows, rows, col, cols))
            row, rows, col, cols = self.keep[-1]

    def at(self, ref, region, shift=0):
        row, rows, col, cols = region
        down = pl.ds(pl.multiple_of(row, rows), rows)
        return ref.at[down, pl.ds(pl.multiple_of(col + shift, cols), cols)]

    def copy(self, stage):
        many = len(self.dims)
        send, recv = self.sems.at[2 * stage], self.sems.at[2 * stage + 1]
        if stage < many:
            src = self.at(self.acc, self.give[stage])
            return remote(src, self.recvs[stage], send, recv, self.place.partner(self.dims[stage]))
        if stage == 2 * many:
            region = self.at(self.out, self.whole, self.shift)
            return remote(region, region, send, recv, self.place.flip_core)
        step = 2 * many - 1 - stage
        dst = self.at(self.out, self.keep[step], self.shift)
        src = self.at(self.acc, self.keep[step]) if stage == many else dst
        return remote(src, dst, send, recv, self.place.partner(self.dims[step]))

    def local(self):
        return pltpu.make_async_copy(
            self.at(self.acc, self.keep[-1]),
            self.at(self.out, self.keep[-1], self.shift),
            self.sems.at[2 * self.count],
        )

    def take(self, stage):
        many = len(self.dims)
        self.copy(stage).wait_recv()
        if stage < many:
            row, rows, col, cols = self.keep[stage]
            add_into(self.acc, row, pl.ds(pl.multiple_of(col, cols), cols), self.recvs[stage])
        elif stage == many:
            self.local().wait()

    def advance(self):
        if self.stage is None:
            self.stage = self.first
        elif self.stage < self.count:
            self.take(self.stage)
            self.stage += 1
        if self.stage < self.count:
            self.copy(self.stage).start()
            if self.stage == len(self.dims):
                self.local().start()

    def close(self):
        while self.stage < self.count:
            self.advance()
        for stage in range(self.first, self.count):
            self.copy(stage).wait_send()


def add_into(acc, base, cols, other):
    rows = other.shape[0]
    tile = math.gcd(rows, 128)

    @pl.loop(0, rows // tile)
    def _(i):
        here = pl.ds(pl.multiple_of(base + i * tile, tile), tile)
        acc[here, cols] = acc[here, cols] + other[part(i, tile), :]


Y, A, B, X = 0, 1, 2, 9
D0, D1, L0, L1, R0, R1, O, G, Q, K, V = range(11)
S1, S2, S3, S5, S6, WO, WG, WQ, WK, WV, INSIDE, JOIN, OUT, OUTX, GAIN = range(20, 35)
EARLY = (D0, D1, L0, L1)
DIMS = {
    D0: (Y, A, B),
    D1: (A, Y, B),
    L0: (Y, B, A),
    L1: (A, Y, B),
    R0: (Y, A, B),
    R1: (A, Y, B),
    O: (X, A, Y, B),
    G: (Y, X, A, B),
    Q: (Y, X, A, B),
    K: (X, Y, A, B),
    V: (X, Y, A, B),
}
ORDER = (
    OUTX, D1, R0, L1, D0, R1, L0, S1, S2, D1, D0, S3, WO, R0, WG, INSIDE, INSIDE, D1, INSIDE, D0, INSIDE,
    JOIN, INSIDE, INSIDE, R0, INSIDE, D1, INSIDE, G, D0, WQ, O, S5, D1, WK, R0, D0, WV, S6, O, G, S6, GAIN,
    D1, OUT, R0, K, D0, GAIN, G, Q, O, L0, R0, GAIN, G, K, O, V, G, GAIN, K, Q, O, R0, G, GAIN, L1, K, R1, V,
    Q, GAIN, O, G, V, K, Q, O, V, G, L1, K, Q, V, G, L1, R1, Q, K, O, L0, V, L1, O, Q, V, R1, L1, L0, R1, K,
    Q, K, L0, R1, Q, V, V, L0, R1,
)


def tall_of(wide, hidden):
    return (wide // 2) * round_up(-(-hidden // (wide // 2)), 16)


def dims_of(name, wide):
    return DIMS[name] + tuple(range(3, wide.bit_length() - 1))


def arrivals(name, wide, rows, cols):
    shapes = []
    for dim in dims_of(name, wide):
        if name < O and dim == Y:
            cols //= 2
        else:
            rows //= 2
        shapes.append((rows, cols))
    return shapes


def backward_body(wide, heads, eps, r):
    p = Place(wide)
    rows, width = r.gn2.shape
    head = width // heads
    half = width // 2
    tile = 128
    chunk = width // wide
    mine = part(p.core, half)
    theirs = part(1 - p.core, half)

    greet([p.flip_core, p.flip_x], p, True)

    u = {}
    for name in range(D0, V + 1):
        first = 1 if name in EARLY else 0
        recvs = [r.recv.get((name, step)) for step in range(len(dims_of(name, wide)))]
        if name < O:
            which, cut = divmod(name - D0, 2)
            acc, out, shift = r.p_v.at[which, :, pl.ds(cut * half, half)], r.out_f[which], cut * half
        else:
            acc, out, shift = r.acc.at[name - O], r.out_a[name - O], p.core * half
        u[name] = Unit(
            p,
            dims_of(name, wide),
            acc,
            out,
            shift,
            recvs,
            r.usem.at[name - D0],
            name >= O,
            Y if name < O else None,
            first,
        )

    loads, landed = {}, set()

    def load(key, src, dst):
        loads[key] = pltpu.make_async_copy(src, dst, r.lsem.at[len(loads)])
        loads[key].start()

    def need(*keys):
        for key in keys:
            if key not in landed:
                loads[key].wait()
                landed.add(key)

    for i in range(3):
        load(i, r.p.at[i], r.p_v.at[i])
    load("gn2", r.gn2, r.gn2_v)
    load("hidden", r.hidden, r.hid_v)
    load("cot", r.cot, r.cot_v)
    load("wo", r.wo, r.wa)
    load("flat", r.flat, r.flat_v)
    load("gate", r.gate, r.gate_v)
    load("ko", r.ko, r.ko_v)
    load("q", r.q, r.q_v)
    out_x = remote(r.outx, r.out_rx, r.osem.at[2], r.osem.at[3], p.flip_x)
    to_sib = [
        remote(r.mixed, r.mix_v.at[1], r.csem.at[0], r.csem.at[1], p.flip_core),
        remote(r.n1, r.n1_v.at[1], r.csem.at[2], r.csem.at[3], p.flip_core),
    ]
    for copy in to_sib:
        copy.start()
    load("mixed", r.mixed, r.mix_v.at[0])
    load("n1", r.n1, r.n1_v.at[0])
    load("k", r.k, r.k_v)
    load("v", r.v, r.v_v)
    load("sin", r.sin, r.sin_v)
    load("dq", r.dq, r.dq_v)
    load("dk", r.dk, r.dk_v)
    load("wk", r.wk, r.wc)
    load("wv", r.wv, r.wd)
    ends = segment_ends(r.lens)
    halves = {}

    def send_half(key, src):
        slot = key - O
        halves[key] = remote(
            src.at[:, theirs], r.sib.at[slot], r.csem.at[4 + 2 * slot], r.csem.at[5 + 2 * slot], p.flip_core
        )
        halves[key].start()

    def fold(x):
        return jnp.sum(x.reshape(x.shape[0] // 8, 8, x.shape[1]), axis=0)

    def second_norm():
        r.gsum[...] = jnp.zeros_like(r.gsum)
        need("gn2", "hidden", "cot")

        @pl.loop(0, rows // tile)
        def _(i):
            here = part(i, tile)
            hid = r.hid_v[here, :]
            scale = lax.rsqrt(jnp.mean(hid * hid, axis=-1, keepdims=True) + eps)
            unit = hid * scale
            up = r.gn2_v[here, :]
            r.gsum[1] += fold(up * unit)
            up = up * r.fgain[...]
            down = scale * (up - unit * jnp.mean(up * unit, axis=-1, keepdims=True))
            down = down + r.cot_v[here, :].astype(F32)
            r.hid_v[here, :] = down
            r.gb[here, :] = down.astype(BF16)

        load("tok", r.tokens, r.cot_v)
        send_half(O, r.gb)

    def gates():
        need("wo", "flat", "gate", "ko")

        @pl.loop(0, rows // 256)
        def _(i):
            here = part(i, 256)
            gm = nt(r.gb[here, :], r.wa[...])
            flat = r.flat_v[here, :].astype(F32)
            r.gg[here, :] = (gm * flat).astype(BF16)
            gm = gm * r.gate_v[here, :].astype(F32)
            ko = r.ko_v[here, :]
            for h in range(heads):
                cols = slice(h * head, (h + 1) * head)
                up, unit = gm[:, cols], flat[:, cols]
                mean = jnp.mean(up * unit, axis=-1, keepdims=True)
                r.ga[here, cols] = (ko[:, h : h + 1] * (up - unit * mean)).astype(BF16)

        send_half(G, r.gg)
        load("wq", r.wq, r.wa)

    def states():
        segment_setup(p, ends, r.rate_row, rows, r.gate_in, r.keep_out, r.reach, False)
        need("q")
        for h in range(heads):
            cols = slice(h * head, (h + 1) * head)
            gated = (r.q_v[:, cols].astype(F32) * r.gate_in[:, h : h + 1]).astype(BF16)
            r.state_a[pl.ds(h * head, head), :] = tn(gated, r.ga[:, cols]).astype(BF16)
        scatter_states(p, r.state_a, r.arrived, r.ssem.at[0], r.ssem.at[1], chunk)

    def weight_unit(name, left, own):
        acc = r.acc.at[name - O]
        other = r.sib.at[name - O]
        halves[name].wait_recv()

        @pl.loop(0, width // 512)
        def _(i):
            here = part(i, 512)
            acc[here, :] = (
                tn(left[0, :, here], own[:, mine]) + tn(left[1, :, here], other[...])
            ).astype(BF16)

        u[name].advance()

    def weight_o():
        need("mixed")
        to_sib[0].wait_recv()
        weight_unit(O, r.mix_v, r.gb)

    def weight_g():
        need("n1")
        to_sib[1].wait_recv()
        weight_unit(G, r.n1_v, r.gg)

    turn = [0, 0, 0]

    def inside():
        need("k", "v", "sin", "dq", "dk")
        first = turn[0]
        turn[0] += heads // 8

        def one(h, carry):
            cols = part(h, head)
            q, k, v, ga = r.q_v[:, cols], r.k_v[:, cols], r.v_v[:, cols], r.ga[:, cols]
            weight = decay_of(r.reach[...], r.rate_s[h])
            probs = (nt(k, q) * weight).astype(BF16)
            r.gv_f[:, cols] = nn(probs, ga)
            scores = (nt(v, ga) * weight).astype(BF16)
            r.gn2_v[:, cols] = nn(scores, q)
            pick = lax.broadcasted_iota(jnp.int32, (1, heads), 1) == h
            gate = jnp.sum(jnp.where(pick, r.gate_in[...], 0.0), axis=1, keepdims=True)
            gq = tn(scores, k) + nt(ga, r.sin_v[cols, :]) * gate
            r.gq[:, cols] = (gq * r.dq_v[:, cols].astype(F32)).astype(BF16)
            return carry

        lax.fori_loop(first, turn[0], one, 0)
        if turn[0] == heads:
            send_half(Q, r.gq)

    def join():
        wait_states(p, r.state_a, r.arrived, r.ssem.at[0], r.ssem.at[1], chunk)
        rate = r.rate_s[lax.div(p.w * chunk, head)]
        join_states(p, ends, rate, rows, r.arrived, r.joined, True)
        return_states(p, r.joined, r.state_b, r.ssem.at[2], r.ssem.at[3], chunk)

    def with_states():
        wait_returned(p, r.joined, r.state_b, r.ssem.at[2], r.ssem.at[3], chunk)
        for h in range(heads):
            cols = slice(h * head, (h + 1) * head)
            state = r.state_b[pl.ds(h * head, head), :]
            keep = r.keep_out[:, h : h + 1]
            gk = r.gn2_v[:, cols] + nt(r.v_v[:, cols], state) * keep
            r.flat_v[:, cols] = (gk * r.dk_v[:, cols].astype(F32)).astype(BF16)
            gv = r.gv_f[:, cols] + nn(r.k_v[:, cols], state) * keep
            r.gate_v[:, cols] = gv.astype(BF16)
        send_half(K, r.flat_v)
        send_half(V, r.gate_v)
        load("hidden_again", r.hidden, r.gn2_v)
        load("outown", r.outown, r.q_v)
        to_sib[0].wait_send()
        load("wg0", r.wg.at[pl.ds(0, rows)], r.mix_v.at[0])
        load("wg1", r.wg.at[pl.ds(rows, rows)], r.mix_v.at[1])

    def first_norm():
        need("wq", "wk", "wv", "wg0", "wg1", "tok")
        size = rows // 2
        here = pl.ds(turn[1] * size, size)
        turn[1] += 1
        up = (
            nt(r.gq[here, :], r.wa[...])
            + nt(r.flat_v[here, :], r.wc[...])
            + nt(r.gate_v[here, :], r.wd[...])
            + jnp.concatenate([nt(r.gg[here, :], r.mix_v[i]) for i in range(2)], axis=1)
        )
        tok = r.cot_v[here, :].astype(F32)
        scale = lax.rsqrt(jnp.mean(tok * tok, axis=-1, keepdims=True) + eps)
        unit = tok * scale
        r.gsum[0] += fold(up * unit)
        up = up * r.again[...]
        down = scale * (up - unit * jnp.mean(up * unit, axis=-1, keepdims=True))
        r.hid_v[here, :] += down
        if turn[1] == 2:
            stores["gtok"].start()
            r.gains[0] = jnp.zeros_like(r.gains[0])
            for row in range(2):
                r.gains[0, pl.ds(row, 1), :] = jnp.sum(r.gsum[row], axis=0, keepdims=True)

    stores = {
        "gtok": pltpu.make_async_copy(r.hid_v, r.gtok, r.osem.at[0]),
        "gain": pltpu.make_async_copy(r.gains.at[2 + len(p.bits)], r.out_gain, r.osem.at[1]),
        "out": pltpu.make_async_copy(r.k_v, r.out, r.osem.at[4]),
    }

    def output():
        out_x.wait_recv()
        need("hidden_again", "outown")

        @pl.loop(0, rows // tile)
        def _(i):
            here = part(i, tile)
            total = r.q_v[here, :].astype(F32) + r.out_rx[here, :].astype(F32)
            r.k_v[here, :] = (r.gn2_v[here, :] + total).astype(BF16)

        stores["out"].start()

    gain_to = [p.flip_core, p.flip_x] + [p.partner(bit) for bit in p.bits]
    many = len(gain_to)

    def gain_copy(step):
        return remote(
            r.gains.at[step], r.grecv.at[step], r.gsem.at[2 * step], r.gsem.at[2 * step + 1], gain_to[step]
        )

    def gain():
        step = turn[2]
        turn[2] += 1
        if step:
            gain_copy(step - 1).wait_recv()
            r.gains[step] = r.gains[step - 1] + r.grecv[step - 1]
        if step < many:
            gain_copy(step).start()
        else:
            stores["gain"].start()

    steps = {
        S1: second_norm,
        S2: gates,
        S3: states,
        WO: weight_o,
        WG: weight_g,
        WQ: lambda: weight_unit(Q, r.n1_v, r.gq),
        WK: lambda: weight_unit(K, r.n1_v, r.flat_v),
        WV: lambda: weight_unit(V, r.n1_v, r.gate_v),
        INSIDE: inside,
        JOIN: join,
        S5: with_states,
        S6: first_norm,
        OUT: output,
        OUTX: out_x.start,
        GAIN: gain,
    }
    for step in ORDER:
        if step in u:
            if step < O:
                need((step - D0) // 2)
            u[step].advance()
        else:
            steps[step]()
    while turn[2] <= many:
        gain()
    for one in u.values():
        one.close()
    for copy in stores.values():
        copy.wait()
    out_x.wait_send()
    to_sib[1].wait_send()
    for copy in halves.values():
        copy.wait_send()
    for step in range(many):
        gain_copy(step).wait_send()


def backward_call(wide, heads, eps, arrays):
    rows, width = arrays["gn2"].shape
    tall = arrays["p"].shape[1]
    half = width // 2
    bits = wide.bit_length() - 1
    specs = {"lens": IN_SMEM, "rate_s": IN_SMEM, "rate_row": IN_VMEM, "fgain": IN_VMEM, "again": IN_VMEM}
    ins = {nm: (a, specs.get(nm, ANY)) for nm, a in arrays.items()}
    sds = jax.ShapeDtypeStruct
    outs = {("a", i): sds((width, width), BF16) for i in range(5)}
    outs.update({("f", i): sds((tall, width), BF16) for i in range(3)})
    outs["out"] = sds((rows, width), BF16)
    outs["gtok"] = sds((rows, width), F32)
    outs["out_gain"] = sds((8, width), F32)
    VM = pltpu.VMEM
    dma = pltpu.SemaphoreType.DMA
    scratch = dict(
        gn2_v=VM((rows, width), F32),
        hid_v=VM((rows, width), F32),
        gv_f=VM((rows, width), F32),
        cot_v=VM((rows, width), BF16),
        flat_v=VM((rows, width), BF16),
        gate_v=VM((rows, width), BF16),
        ko_v=VM((rows, heads), F32),
        q_v=VM((rows, width), BF16),
        k_v=VM((rows, width), BF16),
        v_v=VM((rows, width), BF16),
        dq_v=VM((rows, width), BF16),
        dk_v=VM((rows, width), BF16),
        mix_v=VM((2, rows, width), BF16),
        n1_v=VM((2, rows, width), BF16),
        sin_v=VM((width, width // heads), BF16),
        wa=VM((width, width), BF16),
        wc=VM((width, width), BF16),
        wd=VM((width, width), BF16),
        gb=VM((rows, width), BF16),
        out_rx=VM((rows, width), BF16),
        gg=VM((rows, width), BF16),
        ga=VM((rows, width), BF16),
        gq=VM((rows, width), BF16),
        sib=VM((5, rows, half), BF16),
        gate_in=VM((rows, heads), F32),
        keep_out=VM((rows, heads), F32),
        reach=VM((rows, rows), F32),
        state_a=VM((width, width // heads), BF16),
        state_b=VM((width, width // heads), BF16),
        arrived=VM((wide, width // wide, width // heads), BF16),
        joined=VM((wide, width // wide, width // heads), BF16),
        acc=VM((5, width, half), BF16),
        p_v=VM((3, tall, width), BF16),
        gsum=VM((2, 8, width), F32),
        gains=VM((3 + bits, 8, width), F32),
        grecv=VM((2 + bits, 8, width), F32),
        lsem=dma((32,)),
        csem=dma((14,)),
        ssem=dma((4, wide)),
        usem=dma((11, 4 * (bits + 1) + 4)),
        gsem=dma((4 + 2 * bits,)),
        osem=dma((5,)),
    )
    for name in range(D0, V + 1):
        for step, shape in enumerate(arrivals(name, wide, tall if name < O else width, half)):
            if step or name not in EARLY:
                scratch["r", name, step] = VM(shape, BF16)
    return call_kernel(
        lambda r: backward_body(wide, heads, eps, r), "attention_backward", 3, ins, outs, scratch, 20 * 10**9
    )


PIECES = 4


def forward_body(wide, heads, eps, r):
    p = Place(wide)
    rows, width = r.tokens.shape
    head = width // heads
    tile = 128
    chunk = width // wide
    size = rows // PIECES
    greet([p.flip_core, p.flip_x], p, True)

    def spot(c, second):
        return pl.ds(2 * rows + (2 * c + second) * size, size)

    gather = [
        remote(r.cot.at[pl.ds(c * size, size)], r.cotall.at[spot(c, 0)], r.xsem.at[0, c], r.xsem.at[1, c], p.flip_x)
        for c in range(PIECES)
    ]
    onward = [
        remote(r.cotall.at[spot(c, 0)], r.cotall.at[spot(c, 1)], r.xsem.at[2, c], r.xsem.at[3, c], p.flip_core)
        for c in range(PIECES)
    ]
    across = remote(r.cot, r.cotall.at[pl.ds(rows, rows)], r.xsem.at[4, 0], r.xsem.at[4, 1], p.flip_core)
    for copy in gather:
        copy.start()

    loads = {}

    def load(key, src, dst):
        loads[key] = pltpu.make_async_copy(src, dst, r.lsem.at[len(loads)])
        loads[key].start()

    def need(key):
        loads[key].wait()

    load("tokens", r.tokens, r.tok_v)
    load("wk", r.wk, r.wk_v)
    load("wv", r.wv, r.wv_v)
    load("wq", r.wq, r.wq_v)
    load("wg", r.wg, r.wg_v)
    load("wo", r.wo, r.wo_v)
    load("keep", r.cot, r.cotall.at[pl.ds(0, rows)])
    across.start()
    stores = []

    def store(src, dst):
        copy = pltpu.make_async_copy(src, dst, r.stsem.at[len(stores)])
        copy.start()
        stores.append(copy)

    def pass_on(c):
        gather[c].wait_recv()
        onward[c].start()

    ends = segment_ends(r.lens)
    segment_setup(p, ends, r.rate_row, rows, r.gate_in, r.keep_out, r.reach, True)
    need("tokens")

    @pl.loop(0, rows // tile)
    def _(i):
        here = part(i, tile)
        tok = r.tok_v[here, :].astype(F32)
        scale = lax.rsqrt(jnp.mean(tok * tok, axis=-1, keepdims=True) + eps)
        r.n1_v[here, :] = (tok * scale * r.again[...]).astype(BF16)

    store(r.n1_v, r.n1)

    def silu_rows(weight, act, slope):
        @pl.loop(0, rows // 256)
        def _(i):
            here = part(i, 256)
            pre = nn(r.n1_v[here, :], weight[...])
            gate = lax.logistic(pre)
            act[here, :] = (pre * gate).astype(BF16)
            slope[here, :] = (gate * (1.0 + pre * (1.0 - gate))).astype(BF16)

    def plain_rows(weight, dst):
        @pl.loop(0, rows // 256)
        def _(i):
            here = part(i, 256)
            dst[here, :] = nn(r.n1_v[here, :], weight[...]).astype(BF16)

    need("wk")
    silu_rows(r.wk_v, r.k_v, r.dk_v)
    need("wv")
    plain_rows(r.wv_v, r.v_v)
    for h in range(heads):
        cols = slice(h * head, (h + 1) * head)
        kept = (r.k_v[:, cols].astype(F32) * r.keep_out[:, h : h + 1]).astype(BF16)
        r.state_a[pl.ds(h * head, head), :] = tn(kept, r.v_v[:, cols]).astype(BF16)
    scatter_states(p, r.state_a, r.arrived, r.ssem.at[0], r.ssem.at[1], chunk)
    store(r.k_v, r.k)
    store(r.dk_v, r.dk)
    store(r.v_v, r.v)
    need("wq")
    silu_rows(r.wq_v, r.q_v, r.dq_v)
    store(r.q_v, r.q)
    store(r.dq_v, r.dq)

    def inside(h, carry):
        cols = part(h, head)
        weight = decay_of(r.reach[...], r.rate_s[h])
        probs = (nt(r.q_v[:, cols], r.k_v[:, cols]) * weight).astype(BF16)
        r.raw_f[:, cols] = nn(probs, r.v_v[:, cols])
        return carry

    lax.fori_loop(0, heads // 2, inside, 0)
    pass_on(0)
    wait_states(p, r.state_a, r.arrived, r.ssem.at[0], r.ssem.at[1], chunk)
    join_states(p, ends, r.rate_s[lax.div(p.w * chunk, head)], rows, r.arrived, r.joined, False)
    return_states(p, r.joined, r.state_b, r.ssem.at[2], r.ssem.at[3], chunk)
    need("wg")
    plain_rows(r.wg_v, r.gate_v)
    store(r.gate_v, r.gate)
    lax.fori_loop(heads // 2, heads, inside, 0)
    pass_on(1)
    wait_returned(p, r.joined, r.state_b, r.ssem.at[2], r.ssem.at[3], chunk)
    store(r.state_b, r.sin)
    for h in range(heads):
        cols = slice(h * head, (h + 1) * head)
        state = r.state_b[pl.ds(h * head, head), :]
        raw = r.raw_f[:, cols] + nn(r.q_v[:, cols], state) * r.gate_in[:, h : h + 1]
        scale = lax.rsqrt(jnp.mean(raw * raw, axis=-1, keepdims=True) + eps)
        unit = raw * scale
        r.ko_v[:, h : h + 1] = scale
        r.flat_v[:, cols] = unit.astype(BF16)
        r.mix_v[:, cols] = (unit * r.gate_v[:, cols].astype(F32)).astype(BF16)
    store(r.ko_v, r.ko)
    store(r.flat_v, r.flat)
    store(r.mix_v, r.mixed)
    need("wo")

    @pl.loop(0, rows // 256)
    def _(i):
        here = part(i, 256)
        hid = r.tok_v[here, :].astype(F32) + nn(r.mix_v[here, :], r.wo_v[...])
        scale = lax.rsqrt(jnp.mean(hid * hid, axis=-1, keepdims=True) + eps)
        r.hid_v[here, :] = hid
        r.n2_v[here, :] = (hid * scale * r.fgain[...]).astype(BF16)

    store(r.n2_v, r.n2)
    store(r.hid_v, r.hidden)
    for c in range(2, PIECES):
        pass_on(c)
    across.wait_recv()
    across.wait_send()
    need("keep")
    for copy in onward:
        copy.wait_recv()
    for copy in onward + gather:
        copy.wait_send()
    for copy in stores:
        copy.wait()


def forward_call(wide, heads, eps, arrays):
    rows, width = arrays["tokens"].shape
    specs = {"lens": IN_SMEM, "rate_s": IN_SMEM, "rate_row": IN_VMEM, "fgain": IN_VMEM, "again": IN_VMEM}
    ins = {nm: (a, specs.get(nm, ANY)) for nm, a in arrays.items()}
    sds = jax.ShapeDtypeStruct
    outs = {nm: sds((rows, width), BF16) for nm in ("n1", "q", "k", "v", "dq", "dk", "gate", "flat", "mixed", "n2")}
    outs["ko"] = sds((rows, heads), F32)
    outs["hidden"] = sds((rows, width), F32)
    outs["sin"] = sds((width, width // heads), BF16)
    outs["cotall"] = sds((4 * rows, width), BF16)
    V = pltpu.VMEM
    dma = pltpu.SemaphoreType.DMA
    scratch = {nm + "_v": V((rows, width), BF16) for nm in ("tok", "n1", "q", "k", "v", "dq", "dk", "gate", "flat", "mix", "n2")}
    scratch.update({nm + "_v": V((width, width), BF16) for nm in ("wq", "wk", "wv", "wg", "wo")})
    scratch.update(
        raw_f=V((rows, width), F32),
        hid_v=V((rows, width), F32),
        ko_v=V((rows, heads), F32),
        gate_in=V((rows, heads), F32),
        keep_out=V((rows, heads), F32),
        reach=V((rows, rows), F32),
        state_a=V((width, width // heads), BF16),
        state_b=V((width, width // heads), BF16),
        arrived=V((wide, width // wide, width // heads), BF16),
        joined=V((wide, width // wide, width // heads), BF16),
        lsem=dma((8,)),
        stsem=dma((16,)),
        xsem=dma((5, PIECES)),
        ssem=dma((4, wide)),
    )
    return call_kernel(
        lambda r: forward_body(wide, heads, eps, r), "attention_forward", 1, ins, outs, scratch, 8 * 10**9
    )


def gated_body(wide, r):
    p = Place(wide)
    rows, width = r.n2.shape
    hidden = r.wl.shape[0]
    size = rows // PIECES
    group = 256
    greet([p.flip_core, p.flip_x, p.partner(Y), p.partner(A)], p, False)

    def spot(c, second):
        return pl.ds(2 * rows + (2 * c + second) * size, size)

    def remotes(row, src_of, dst_of, device):
        return [
            remote(src_of(c), dst_of(c), r.xsem.at[row, c], r.xsem.at[row + 1, c], device)
            for c in range(PIECES)
        ]

    def piece(ref):
        return lambda c: ref.at[pl.ds(c * size, size)]

    gather = remotes(0, piece(r.n2), lambda c: r.X.at[spot(c, 0)], p.flip_x)
    onward = remotes(2, lambda c: r.X.at[spot(c, 0)], lambda c: r.X.at[spot(c, 1)], p.flip_core)
    across = remote(r.n2, r.X.at[pl.ds(rows, rows)], r.xsem.at[16, 0], r.xsem.at[16, 1], p.flip_core)
    back_core = remotes(4, piece(r.to_core), piece(r.from_core), p.flip_core)
    back_own = remotes(6, piece(r.own_core), piece(r.own_from), p.flip_core)
    back_x = remotes(8, piece(r.to_x), piece(r.from_x), p.flip_x)
    out_core = remotes(10, piece(r.o_to_core), piece(r.o_from_core), p.flip_core)
    out_own = remotes(12, piece(r.o_own_core), piece(r.o_own_from), p.flip_core)

    for copy in gather:
        copy.start()
    across.start()
    loads = {}

    def load(key, src, dst):
        loads[key] = pltpu.make_async_copy(src, dst, r.lsem.at[len(loads)])
        loads[key].start()

    def need(*keys):
        for key in keys:
            loads[key].wait()

    load("x", r.n2, r.X.at[pl.ds(0, rows)])
    load("wl", r.wl, r.wl_v)
    load("wr", r.wr, r.wr_v)
    load("wd", r.wd, r.wd_v)
    load("g", r.cotall, r.G)
    stores = []

    def store(src, dst):
        copy = pltpu.make_async_copy(src, dst, r.stsem.at[len(stores)])
        copy.start()
        stores.append(copy)

    def act(here):
        x = r.X[here, :]
        left = nt(x, r.wl_v[...])
        right = nt(x, r.wr_v[...])
        r.prod[here, :] = (left * right).astype(BF16)
        up = nt(r.G[here, :], r.wd_v[...])
        r.gl[here, :] = (up * right).astype(BF16)
        r.gr[here, :] = (up * left).astype(BF16)
        return nn(r.gl[here, :], r.wl_v[...]) + nn(r.gr[here, :], r.wr_v[...])

    def out_part(here):
        return nn(r.prod[here, :], r.wd_v[...])

    need("x", "wl", "wr", "wd", "g")

    @pl.loop(0, rows // group)
    def _(i):
        r.own[part(i, group), :] = act(part(i, group))

    across.wait_recv()

    @pl.loop(0, rows // group)
    def _(i):
        r.own_core[part(i, group), :] = act(pl.ds(pl.multiple_of(rows + i * group, group), group)).astype(BF16)

    for copy in back_own:
        copy.start()
    gather[0].wait_recv()
    onward[0].start()

    def out_own_rows(i):
        r.o_own[part(i, group), :] = out_part(part(i, group))

    def out_core_rows(i):
        r.o_own_core[part(i, group), :] = out_part(pl.ds(rows + i * group, group)).astype(BF16)

    def far(c):
        here = pl.ds(2 * rows + 2 * c * size, 2 * size)
        got = act(here)
        r.keep[pl.ds(c * size, size), :] = got[:size]
        r.to_core[pl.ds(c * size, size), :] = got[size:].astype(BF16)
        back_core[c].start()

    def far_send(c):
        back_core[c].wait_recv()
        here = pl.ds(c * size, size)
        r.to_x[here, :] = (r.keep[here, :] + r.from_core[here, :].astype(F32)).astype(BF16)
        back_x[c].start()

    fill = [
        lambda: out_own_rows(0),
        lambda: out_own_rows(1),
        lambda: out_core_rows(0),
        lambda: out_core_rows(1),
    ]
    for c in range(PIECES):
        fill[c]()
        onward[c].wait_recv()
        far(c)
        if c + 1 < PIECES:
            if c:
                far_send(c - 1)
            gather[c + 1].wait_recv()
            onward[c + 1].start()
    for copy in out_own:
        copy.start()
    far_send(PIECES - 2)

    def out_far(c):
        got = out_part(pl.ds(2 * rows + 2 * c * size, 2 * size))
        r.o_keep[pl.ds(c * size, size), :] = got[:size]
        r.o_to_core[pl.ds(c * size, size), :] = got[size:].astype(BF16)
        out_core[c].start()

    def weight(which, left, right):
        cut = 384 if hidden > 384 else hidden
        for base, extent in ((0, cut), (cut, hidden - cut)):
            if extent:
                here = pl.ds(base, extent)
                r.p_v[which, here, :] = tn(left[:, here], right[...]).astype(BF16)

    half = width // 2
    sums = {}
    for name in EARLY:
        which, cut = divmod(name - D0, 2)
        acc = r.p_v.at[which, :, pl.ds(cut * half, half)]
        sems = r.usem.at[name - D0]
        sums[name] = Unit(p, dims_of(name, wide), acc, None, 0, [r.recv[name, 0]], sems, 0, Y)

    def begin(names):
        for name in names:
            sums[name].copy(0).start()

    def finish(names):
        for name in names:
            sums[name].take(0)

    out_far(0)
    far_send(PIECES - 1)
    weight(0, r.prod, r.G)
    begin(EARLY[:2])
    weight(1, r.gl, r.X)
    begin(EARLY[2:])
    out_far(1)
    out_far(2)
    out_far(3)
    weight(2, r.gr, r.X)
    store(r.p_v.at[2], r.p.at[2])
    finish(EARLY[:2])
    store(r.p_v.at[0], r.p.at[0])
    for c in range(PIECES):
        out_core[c].wait_recv()
        out_own[c].wait_recv()
        here = pl.ds(c * size, size)
        r.o_x[here, :] = (r.o_keep[here, :] + r.o_from_core[here, :].astype(F32)).astype(BF16)
        r.o_sum[here, :] = (r.o_own[here, :] + r.o_own_from[here, :].astype(F32)).astype(BF16)
    store(r.o_x, r.outx)
    store(r.o_sum, r.outown)
    finish(EARLY[2:])
    store(r.p_v.at[1], r.p.at[1])
    for c in range(PIECES):
        back_own[c].wait_recv()
        back_x[c].wait_recv()
        here = pl.ds(c * size, size)
        r.own[here, :] += r.own_from[here, :].astype(F32) + r.from_x[here, :].astype(F32)
    store(r.own, r.gn2)
    across.wait_send()
    for copies in (gather, onward, back_core, back_own, back_x, out_core, out_own):
        for copy in copies:
            copy.wait_send()
    for copy in stores:
        copy.wait()
    for one in sums.values():
        one.copy(0).wait_send()


def gated_call(wide, arrays):
    rows, width = arrays["n2"].shape
    hidden = arrays["wl"].shape[0]
    ins = {nm: (a, ANY) for nm, a in arrays.items()}
    sds = jax.ShapeDtypeStruct
    outs = dict(
        gn2=sds((rows, width), F32),
        outx=sds((rows, width), BF16),
        outown=sds((rows, width), BF16),
        p=sds((3, tall_of(wide, hidden), width), BF16),
    )
    V = pltpu.VMEM
    dma = pltpu.SemaphoreType.DMA
    few = ("to_core", "from_core", "own_core", "own_from", "to_x", "from_x")
    few += ("o_to_core", "o_from_core", "o_own_core", "o_own_from", "o_x", "o_sum")
    scratch = {nm: V((rows, width), BF16) for nm in few}
    scratch.update({nm: V((rows, width), F32) for nm in ("own", "keep", "o_own", "o_keep")})
    scratch.update({nm: V((4 * rows, hidden), BF16) for nm in ("prod", "gl", "gr")})
    scratch.update(
        X=V((4 * rows, width), BF16),
        G=V((4 * rows, width), BF16),
        wl_v=V((hidden, width), BF16),
        wr_v=V((hidden, width), BF16),
        wd_v=V((hidden, width), BF16),
        p_v=V((3, tall_of(wide, hidden), width), BF16),
        usem=dma((6, 2)),
        xsem=dma((17, PIECES)),
        lsem=dma((5,)),
        stsem=dma((6,)),
    )
    for name in EARLY:
        scratch["r", name, 0] = V(arrivals(name, wide, tall_of(wide, hidden), width // 2)[0], BF16)
    return call_kernel(lambda r: gated_body(wide, r), "gated_unit", 2, ins, outs, scratch, 27 * 10**9)


def widen_body(*refs):
    many = len(refs) // 2
    for src, dst in zip(refs[:many], refs[many:], strict=True):
        dst[...] = src[...].astype(dst.dtype)


def widen(arrays, rows, types, steps, name):
    def block(count, width):
        return pl.BlockSpec((count // steps, width), lambda i: (i, 0))

    width = arrays[0].shape[1]
    specs = [block(count, width) for count in rows]
    return pl.pallas_call(
        widen_body,
        name=name,
        grid=(steps,),
        in_specs=specs,
        out_specs=specs,
        out_shape=[jax.ShapeDtypeStruct((n, width), kind) for n, kind in zip(rows, types, strict=True)],
        compiler_params=pltpu.CompilerParams(vmem_limit_bytes=VMEM_BYTES // 2),
    )(*arrays)


def body(
    tokens,
    cotangent,
    lengths,
    decay_rate,
    attn_gain,
    w_query,
    w_key,
    w_value,
    w_gate,
    w_out,
    ffn_gain,
    w_left,
    w_right,
    w_down,
):
    wide = lax.axis_size("wide")
    heads = decay_rate.shape[0]
    hidden = w_down.shape[0]
    shared = dict(
        lens=lengths,
        rate_s=decay_rate,
        rate_row=decay_rate[None],
        fgain=ffn_gain[None],
        again=attn_gain[None],
        wq=w_query,
        wk=w_key,
        wv=w_value,
        wg=w_gate,
        wo=w_out,
        tokens=tokens[0],
        cot=cotangent[0],
    )
    first = forward_call(wide, heads, EPS, shared)
    second = gated_call(
        wide, dict(n2=first.pop("n2"), cotall=first.pop("cotall"), wl=w_left.T, wr=w_right.T, wd=w_down)
    )
    done = backward_call(wide, heads, EPS, {**shared, **first, **second})

    rows, width = tokens.shape[1:]
    attn = [done["a", i] for i in range(5)] + [done["gtok"], done["out"]]
    g_o, g_g, g_q, g_k, g_v, gtok, out = widen(
        attn, [width] * 5 + [rows] * 2, [F32] * 6 + [BF16], 8, "widen_attention"
    )
    g_d, g_l, g_r = widen([done["f", i] for i in range(3)], [hidden] * 3, [F32] * 3, 4, "widen_gated")
    gains = done["out_gain"]
    return (out[None], gtok[None], g_q, g_k, g_v, g_g, g_o, gains[0], gains[1], g_l.T, g_r.T, g_d)


def solution(mesh):
    placed = (
        P("narrow", "wide", None),
        P("narrow", "wide", None),
        P("narrow", None),
        P(),
        P(),
        P(),
        P(),
        P(),
        P(),
        P(),
        P(),
        P(None, "narrow"),
        P(None, "narrow"),
        P("narrow", None),
    )
    return jax.shard_map(
        body,
        mesh=mesh,
        in_specs=placed,
        out_specs=(
            P("narrow", "wide", None),
            P("narrow", "wide", None),
            P(),
            P(),
            P(),
            P(),
            P(),
            P(),
            P(),
            P(None, "narrow"),
            P(None, "narrow"),
            P("narrow", None),
        ),
        check_vma=False,
    )
```

```python
import math

import jax
import jax.numpy as jnp
from jax import lax
from jax.experimental import pallas as pl
from jax.experimental.pallas import tpu as pltpu
from jax.sharding import PartitionSpec as P

EPS = 1e-06

MESH = pl.DeviceIdType.MESH
F32 = jnp.float32
BF16 = jnp.bfloat16
VMEM_BYTES = 62 * 1024 * 1024
ANY = pl.BlockSpec(memory_space=pl.ANY)
IN_VMEM = pl.BlockSpec(memory_space=pltpu.VMEM)
IN_SMEM = pl.BlockSpec(memory_space=pltpu.SMEM)


class Refs:
    def __init__(self, names, refs):
        self.recv, self.out_a, self.out_f = {}, {}, {}
        self.src, self.dst, self.wide_v, self.narrow_v = {}, {}, {}, {}
        groups = {"r": self.recv, "a": self.out_a, "f": self.out_f}
        groups.update(s=self.src, d=self.dst, w=self.wide_v, n=self.narrow_v)
        for name, ref in zip(names, refs, strict=True):
            if isinstance(name, str):
                setattr(self, name, ref)
            else:
                groups[name[0]][name[1:] if len(name) > 2 else name[1]] = ref


def call_kernel(body, name, number, ins, outs, scratch, cost):
    names = list(ins) + list(outs) + list(scratch)

    def kernel(*refs):
        body(Refs(names, refs))

    results = pl.pallas_call(
        kernel,
        name=name,
        out_shape=list(outs.values()),
        in_specs=[spec for _, spec in ins.values()],
        out_specs=[ANY] * len(outs),
        scratch_shapes=list(scratch.values()),
        cost_estimate=pl.CostEstimate(flops=cost, bytes_accessed=cost // 500, transcendentals=0),
        compiler_params=pltpu.CompilerParams(
            collective_id=number, has_side_effects=True, vmem_limit_bytes=VMEM_BYTES
        ),
    )(*[array for array, _ in ins.values()])
    return dict(zip(outs, results, strict=True))


def nn(left, right):
    return lax.dot_general(left, right, (((1,), (0,)), ((), ())), preferred_element_type=F32)


def nt(left, right):
    return lax.dot_general(left, right, (((1,), (1,)), ((), ())), preferred_element_type=F32)


def tn(left, right):
    return lax.dot_general(left, right, (((0,), (0,)), ((), ())), preferred_element_type=F32)


def part(index, size):
    return pl.ds(pl.multiple_of(index * size, size), size)


def round_up(number, step):
    return -(-number // step) * step


class Place:
    def __init__(self, wide):
        self.wide = wide
        self.w = lax.axis_index("wide")
        self.n = lax.axis_index("narrow")
        self.core = lax.rem(self.n, 2)
        self.xh = lax.div(self.n, 2)
        self.flip_core = (self.w, self.n + 1 - 2 * self.core)
        self.flip_x = (self.w, self.n + 2 - 4 * self.xh)
        self.bits = tuple(range(wide.bit_length() - 1))

    def bit(self, dim):
        return self.xh if dim == X else lax.rem(lax.div(self.w, 2**dim), 2)

    def partner(self, dim):
        if dim == X:
            return self.flip_x
        return (self.w + (1 - 2 * self.bit(dim)) * 2**dim, self.n)

    def on_wide(self, w):
        return (w, self.n)


def greet(partners, place, whole_wide):
    barrier = pltpu.get_barrier_semaphore()
    for partner in partners:
        pl.semaphore_signal(barrier, inc=1, device_id=partner, device_id_type=MESH)
    count = len(partners)
    if whole_wide:

        def one(step, carry):
            pl.semaphore_signal(
                barrier,
                inc=1,
                device_id=place.on_wide(lax.rem(place.w + step, place.wide)),
                device_id_type=MESH,
            )
            return carry

        lax.fori_loop(1, place.wide, one, 0)
        count += place.wide - 1
    pl.semaphore_wait(barrier, count)


def remote(src, dst, send, recv, device):
    return pltpu.make_async_remote_copy(
        src_ref=src, dst_ref=dst, send_sem=send, recv_sem=recv, device_id=device, device_id_type=MESH
    )


def segment_ends(lens):
    ends = []
    total = jnp.int32(0)
    for slot in range(lens.shape[1]):
        total = total + lens[0, slot]
        ends.append(total)
    return ends


def count_ends(ends, spots):
    total = jnp.zeros_like(spots)
    for end in ends:
        total = total + jnp.where(spots >= end, 1, 0)
    return total


def segment_setup(place, ends, rate_row, rows, gate_ref, keep_ref, reach_ref, later_first):
    anchor = place.w * rows
    col_local = lax.broadcasted_iota(jnp.int32, (rows, 1), 0)
    row_local = lax.broadcasted_iota(jnp.int32, (1, rows), 1)
    col_seg = count_ends(ends, col_local + anchor)
    row_seg = count_ends(ends, row_local + anchor)
    before = jnp.int32(0)
    last = jnp.int32(0)
    for end in ends:
        before = before + jnp.where(anchor - 1 >= end, 1, 0)
        last = last + jnp.where(anchor + rows - 1 >= end, 1, 0)
    before = jnp.where(place.w > 0, before, -1)
    col_live = (col_local + anchor) < ends[-1]
    row_live = (row_local + anchor) < ends[-1]
    rates = rate_row[...]
    steps = col_local.astype(F32)
    gate_ref[...] = jnp.exp(-(steps + 1.0) * rates) * jnp.where(
        (col_seg == before) & col_live, 1.0, 0.0
    )
    keep_ref[...] = jnp.exp(-(rows - 1.0 - steps) * rates) * jnp.where(
        (col_seg == last) & col_live, 1.0, 0.0
    )
    gap = col_local - row_local if later_first else row_local - col_local
    reaches = (gap >= 0) & (col_seg == row_seg) & row_live & col_live
    reach_ref[...] = jnp.where(reaches, gap.astype(F32), -1.0)


def decay_of(reach, rate):
    return jnp.where(reach >= 0.0, jnp.exp(-rate * reach), 0.0)


def scatter_states(place, local, arrived, sends, recvs, chunk):
    def one(step, carry):
        target = lax.rem(place.w + step, place.wide)
        remote(
            local.at[part(target, chunk)],
            arrived.at[place.w],
            sends.at[target],
            recvs.at[place.w],
            place.on_wide(target),
        ).start()
        return carry

    lax.fori_loop(1, place.wide, one, 0)
    arrived[place.w] = local[part(place.w, chunk), :]


def wait_states(place, local, arrived, sends, recvs, chunk):
    def one(step, carry):
        source = lax.rem(place.w + step, place.wide)
        copy = remote(
            local.at[part(source, chunk)],
            arrived.at[source],
            sends.at[source],
            recvs.at[source],
            place.on_wide(source),
        )
        copy.wait_recv()
        copy.wait_send()
        return carry

    lax.fori_loop(1, place.wide, one, 0)


def join_states(place, ends, rate, rows, arrived, joined, backward):
    shape = arrived.shape[1:]
    fade = jnp.exp(jnp.full((1, shape[1]), -1.0 * rows, F32) * rate)

    def one(step, state):
        block = place.wide - 1 - step if backward else step
        joined[block] = state.astype(BF16)
        cuts = jnp.int32(0)
        for end in ends:
            inside = (end >= block * rows) & (end <= block * rows + rows - 1)
            cuts = cuts + jnp.where(inside, 1, 0)
        flag = jnp.where((cuts == 0) & (block > 0), 1.0, 0.0)
        return (fade * flag) * state + arrived[block].astype(F32)

    lax.fori_loop(0, place.wide, one, jnp.zeros(shape, F32))


def return_states(place, joined, entering, sends, recvs, chunk):
    def one(step, carry):
        target = lax.rem(place.w + step, place.wide)
        remote(
            joined.at[target],
            entering.at[part(place.w, chunk)],
            sends.at[target],
            recvs.at[place.w],
            place.on_wide(target),
        ).start()
        return carry

    lax.fori_loop(1, place.wide, one, 0)
    entering[part(place.w, chunk), :] = joined[place.w]


def wait_returned(place, joined, entering, sends, recvs, chunk):
    def one(step, carry):
        source = lax.rem(place.w + step, place.wide)
        copy = remote(
            joined.at[source],
            entering.at[part(source, chunk)],
            sends.at[source],
            recvs.at[source],
            place.on_wide(source),
        )
        copy.wait_recv()
        copy.wait_send()
        return carry

    lax.fori_loop(1, place.wide, one, 0)


class Unit:
    def __init__(self, place, dims, acc, out, shift, recvs, sems, is_core, by_columns, first=0):
        self.place, self.dims, self.acc, self.out, self.shift = place, dims, acc, out, shift
        self.recvs, self.sems, self.is_core = recvs, sems, is_core
        self.first, self.stage = first, None
        self.count = 2 * len(dims) + is_core
        self.keep, self.give = [], []
        (rows, cols), row, col = acc.shape, 0, 0
        self.whole = (row, rows, col, cols)
        for dim in dims:
            bit = place.bit(dim)
            if dim == by_columns:
                cols //= 2
                self.keep.append((row, rows, col + bit * cols, cols))
                self.give.append((row, rows, col + (1 - bit) * cols, cols))
            else:
                rows //= 2
                self.keep.append((row + bit * rows, rows, col, cols))
                self.give.append((row + (1 - bit) * rows, rows, col, cols))
            row, rows, col, cols = self.keep[-1]

    def at(self, ref, region, shift=0):
        row, rows, col, cols = region
        down = pl.ds(pl.multiple_of(row, rows), rows)
        return ref.at[down, pl.ds(pl.multiple_of(col + shift, cols), cols)]

    def copy(self, stage):
        many = len(self.dims)
        send, recv = self.sems.at[2 * stage], self.sems.at[2 * stage + 1]
        if stage < many:
            src = self.at(self.acc, self.give[stage])
            return remote(src, self.recvs[stage], send, recv, self.place.partner(self.dims[stage]))
        if stage == 2 * many:
            region = self.at(self.out, self.whole, self.shift)
            return remote(region, region, send, recv, self.place.flip_core)
        step = 2 * many - 1 - stage
        dst = self.at(self.out, self.keep[step], self.shift)
        src = self.at(self.acc, self.keep[step]) if stage == many else dst
        return remote(src, dst, send, recv, self.place.partner(self.dims[step]))

    def local(self):
        return pltpu.make_async_copy(
            self.at(self.acc, self.keep[-1]),
            self.at(self.out, self.keep[-1], self.shift),
            self.sems.at[2 * self.count],
        )

    def take(self, stage):
        many = len(self.dims)
        self.copy(stage).wait_recv()
        if stage < many:
            row, rows, col, cols = self.keep[stage]
            add_into(self.acc, row, pl.ds(pl.multiple_of(col, cols), cols), self.recvs[stage])
        elif stage == many:
            self.local().wait()

    def advance(self):
        if self.stage is None:
            self.stage = self.first
        elif self.stage < self.count:
            self.take(self.stage)
            self.stage += 1
        if self.stage < self.count:
            self.copy(self.stage).start()
            if self.stage == len(self.dims):
                self.local().start()

    def close(self):
        while self.stage < self.count:
            self.advance()
        for stage in range(self.first, self.count):
            self.copy(stage).wait_send()


def add_into(acc, base, cols, other):
    rows = other.shape[0]
    tile = math.gcd(rows, 128)

    @pl.loop(0, rows // tile)
    def _(i):
        here = pl.ds(pl.multiple_of(base + i * tile, tile), tile)
        acc[here, cols] = acc[here, cols] + other[part(i, tile), :]


PIECES = 4


def forward_body(wide, heads, eps, r):
    p = Place(wide)
    rows, width = r.tokens.shape
    head = width // heads
    tile = 128
    chunk = width // wide
    size = rows // PIECES
    greet([p.flip_core, p.flip_x], p, True)

    def spot(c, second):
        return pl.ds(rows + (2 * c + second) * size, size)

    gather = [
        remote(r.cot.at[pl.ds(c * size, size)], r.cotall.at[spot(c, 0)], r.xsem.at[0, c], r.xsem.at[1, c], p.flip_x)
        for c in range(PIECES)
    ]
    onward = [
        remote(r.cotall.at[spot(c, 0)], r.cotall.at[spot(c, 1)], r.xsem.at[2, c], r.xsem.at[3, c], p.flip_core)
        for c in range(PIECES)
    ]
    across = remote(r.cot, r.cotall.at[pl.ds(0, rows)], r.xsem.at[4, 0], r.xsem.at[4, 1], p.flip_core)
    for copy in gather:
        copy.start()

    loads = {}

    def load(key, src, dst):
        loads[key] = pltpu.make_async_copy(src, dst, r.lsem.at[len(loads)])
        loads[key].start()

    def need(key):
        loads[key].wait()

    load("tokens", r.tokens, r.tok_v)
    load("wk", r.wk, r.wk_v)
    load("wv", r.wv, r.wv_v)
    load("wq", r.wq, r.wq_v)
    load("wg", r.wg, r.wg_v)
    load("wo", r.wo, r.wo_v)
    across.start()
    stores = []

    def store(src, dst):
        copy = pltpu.make_async_copy(src, dst, r.stsem.at[len(stores)])
        copy.start()
        stores.append(copy)

    def pass_on(c):
        gather[c].wait_recv()
        onward[c].start()

    ends = segment_ends(r.lens)
    segment_setup(p, ends, r.rate_row, rows, r.gate_in, r.keep_out, r.reach, True)
    need("tokens")

    @pl.loop(0, rows // tile)
    def _(i):
        here = part(i, tile)
        tok = r.tok_v[here, :].astype(F32)
        scale = lax.rsqrt(jnp.mean(tok * tok, axis=-1, keepdims=True) + eps)
        r.n1_v[here, :] = (tok * scale * r.again[...]).astype(BF16)

    store(r.n1_v, r.n1)

    def silu_rows(weight, act, slope):
        @pl.loop(0, rows // 256)
        def _(i):
            here = part(i, 256)
            pre = nn(r.n1_v[here, :], weight[...])
            gate = lax.logistic(pre)
            act[here, :] = (pre * gate).astype(BF16)
            slope[here, :] = (gate * (1.0 + pre * (1.0 - gate))).astype(BF16)

    def plain_rows(weight, dst):
        @pl.loop(0, rows // 256)
        def _(i):
            here = part(i, 256)
            dst[here, :] = nn(r.n1_v[here, :], weight[...]).astype(BF16)

    need("wk")
    silu_rows(r.wk_v, r.k_v, r.dk_v)
    need("wv")
    plain_rows(r.wv_v, r.v_v)
    for h in range(heads):
        cols = slice(h * head, (h + 1) * head)
        kept = (r.k_v[:, cols].astype(F32) * r.keep_out[:, h : h + 1]).astype(BF16)
        r.state_a[pl.ds(h * head, head), :] = tn(kept, r.v_v[:, cols]).astype(BF16)
    scatter_states(p, r.state_a, r.arrived, r.ssem.at[0], r.ssem.at[1], chunk)
    store(r.k_v, r.k)
    store(r.dk_v, r.dk)
    store(r.v_v, r.v)
    need("wq")
    silu_rows(r.wq_v, r.q_v, r.dq_v)
    store(r.q_v, r.q)
    store(r.dq_v, r.dq)

    def inside(h, carry):
        cols = part(h, head)
        weight = decay_of(r.reach[...], r.rate_s[h])
        probs = (nt(r.q_v[:, cols], r.k_v[:, cols]) * weight).astype(BF16)
        r.raw_f[:, cols] = nn(probs, r.v_v[:, cols])
        return carry

    lax.fori_loop(0, heads // 2, inside, 0)
    pass_on(0)
    wait_states(p, r.state_a, r.arrived, r.ssem.at[0], r.ssem.at[1], chunk)
    join_states(p, ends, r.rate_s[lax.div(p.w * chunk, head)], rows, r.arrived, r.joined, False)
    return_states(p, r.joined, r.state_b, r.ssem.at[2], r.ssem.at[3], chunk)
    need("wg")
    plain_rows(r.wg_v, r.gate_v)
    store(r.gate_v, r.gate)
    lax.fori_loop(heads // 2, heads, inside, 0)
    pass_on(1)
    wait_returned(p, r.joined, r.state_b, r.ssem.at[2], r.ssem.at[3], chunk)
    store(r.state_b, r.sin)
    for h in range(heads):
        cols = slice(h * head, (h + 1) * head)
        state = r.state_b[pl.ds(h * head, head), :]
        raw = r.raw_f[:, cols] + nn(r.q_v[:, cols], state) * r.gate_in[:, h : h + 1]
        scale = lax.rsqrt(jnp.mean(raw * raw, axis=-1, keepdims=True) + eps)
        unit = raw * scale
        r.ko_v[:, h : h + 1] = scale
        r.flat_v[:, cols] = unit.astype(BF16)
        r.mix_v[:, cols] = (unit * r.gate_v[:, cols].astype(F32)).astype(BF16)
    store(r.ko_v, r.ko)
    store(r.flat_v, r.flat)
    store(r.mix_v, r.mixed)
    need("wo")

    @pl.loop(0, rows // 256)
    def _(i):
        here = part(i, 256)
        hid = r.tok_v[here, :].astype(F32) + nn(r.mix_v[here, :], r.wo_v[...])
        scale = lax.rsqrt(jnp.mean(hid * hid, axis=-1, keepdims=True) + eps)
        r.hid_v[here, :] = hid
        r.n2_v[here, :] = (hid * scale * r.fgain[...]).astype(BF16)

    store(r.n2_v, r.n2)
    store(r.hid_v, r.hidden)
    for c in range(2, PIECES):
        pass_on(c)
    across.wait_recv()
    across.wait_send()
    for copy in onward:
        copy.wait_recv()
    for copy in onward + gather:
        copy.wait_send()
    for copy in stores:
        copy.wait()


def forward_call(wide, heads, eps, arrays):
    rows, width = arrays["tokens"].shape
    specs = {"lens": IN_SMEM, "rate_s": IN_SMEM, "rate_row": IN_VMEM, "fgain": IN_VMEM, "again": IN_VMEM}
    ins = {nm: (a, specs.get(nm, ANY)) for nm, a in arrays.items()}
    sds = jax.ShapeDtypeStruct
    outs = {nm: sds((rows, width), BF16) for nm in ("n1", "q", "k", "v", "dq", "dk", "gate", "flat", "mixed", "n2")}
    outs["ko"] = sds((rows, heads), F32)
    outs["hidden"] = sds((rows, width), F32)
    outs["sin"] = sds((width, width // heads), BF16)
    outs["cotall"] = sds((3 * rows, width), BF16)
    V = pltpu.VMEM
    dma = pltpu.SemaphoreType.DMA
    scratch = {nm + "_v": V((rows, width), BF16) for nm in ("tok", "n1", "q", "k", "v", "dq", "dk", "gate", "flat", "mix", "n2")}
    scratch.update({nm + "_v": V((width, width), BF16) for nm in ("wq", "wk", "wv", "wg", "wo")})
    scratch.update(
        raw_f=V((rows, width), F32),
        hid_v=V((rows, width), F32),
        ko_v=V((rows, heads), F32),
        gate_in=V((rows, heads), F32),
        keep_out=V((rows, heads), F32),
        reach=V((rows, rows), F32),
        state_a=V((width, width // heads), BF16),
        state_b=V((width, width // heads), BF16),
        arrived=V((wide, width // wide, width // heads), BF16),
        joined=V((wide, width // wide, width // heads), BF16),
        lsem=dma((8,)),
        stsem=dma((16,)),
        xsem=dma((5, PIECES)),
        ssem=dma((4, wide)),
    )
    return call_kernel(
        lambda r: forward_body(wide, heads, eps, r), "attention_forward", 1, ins, outs, scratch, 8 * 10**9
    )


Y, A, B, X = 0, 1, 2, 9
D0, D1, L0, L1, R0, R1, O, G, Q, K, V = range(11)
S1, S2, S3, S5, S6, WO, WG, WQ, WK, WV, INSIDE, JOIN, OUT, OUTX, GAIN, WD, WL, WR, OUTFAR, OUTSUM = range(20, 40)
DIMS = {
    D0: (A, Y, B),
    D1: (Y, A, B),
    L0: (Y, A, B),
    L1: (A, B, Y),
    R0: (Y, A, B),
    R1: (Y, A, B),
    O: (X, Y, A, B),
    G: (X, Y, A, B),
    Q: (X, Y, A, B),
    K: (Y, X, A, B),
    V: (X, Y, A, B),
}
ORDER = (
    WD, D1, D0, OUTFAR, OUTFAR, OUTFAR, OUTSUM, WL, L0, L1, WR, R0, R1, D1, S1, S2, L0, S3, WO, WG, D1,
    INSIDE, INSIDE, L0, R0, INSIDE, INSIDE, D1, D0, R1, O, JOIN, INSIDE, L0, INSIDE, INSIDE, INSIDE, WQ, D1,
    R0, O, G, S5, L0, WK, WV, R0, S6, O, G, Q, S6, GAIN, R0, O, L0, G, K, GAIN, L1, O, Q, G, OUTX, GAIN, R0,
    O, L0, K, Q, GAIN, G, K, Q, R0, V, GAIN, G, D0, O, Q, K, GAIN, OUT, V, D1, Q, D0, K, V, G, R1, O, V, D1,
    O, R1, L1, D0, V, K, Q, G, L1, R1, V, D0, G, K, L1, V, D0, Q, R1, Q, L1, K, K, V, R1, L1, V,
)


def tall_of(wide, hidden):
    return (wide // 2) * round_up(-(-hidden // (wide // 2)), 16)


def dims_of(name, wide):
    return DIMS[name] + tuple(range(3, wide.bit_length() - 1))


def arrivals(name, wide, rows, cols):
    shapes = []
    for dim in dims_of(name, wide):
        if name < O and dim == Y:
            cols //= 2
        else:
            rows //= 2
        shapes.append((rows, cols))
    return shapes


def main_body(wide, heads, eps, r):
    p = Place(wide)
    rows, width = r.n2.shape
    hidden = r.wl.shape[0]
    size = rows // PIECES
    group = 256
    head = width // heads
    half = width // 2
    tile = 128
    chunk = width // wide
    mine = part(p.core, half)
    turn = [0, 0, 0, 1]
    theirs = part(1 - p.core, half)

    greet([p.flip_core, p.flip_x], p, True)

    def rows_of(ref, i):
        return ref.at[pl.ds(i * rows, rows)]

    wl_v, wr_v, wd_v = [r.wf.at[pl.ds(i * hidden, hidden)] for i in range(3)]
    wa, wc = r.wf.at[pl.ds(0, width)], r.wf.at[pl.ds(width, width)]
    wv_v, wg_v = r.X.at[pl.ds(0, width)], r.X.at[pl.ds(width, width)]
    q_v, k_v, v_v, dq_v = [rows_of(r.X, i) for i in range(4)]
    cot_v, dk_v, mix_v, n1_v = [rows_of(r.G, i) for i in range(4)]
    flat_v, gate_v, gb, gg, ga_v, gq_v = r.to_core, r.own_core, r.from_core, r.to_x, r.own_from, r.from_x
    gn2_v, hid_v, out_v, gv_v = r.own, r.keep, dk_v, r.o_own_from
    accs = [
        buf.at[pl.ds((i % 2) * width, width), pl.ds(0, half)]
        for i, buf in enumerate((r.gl, r.gl, r.gr, r.gr, r.prod))
    ]

    u = {}
    for name in range(D0, V + 1):
        first = 0
        recvs = [r.recv.get((name, step)) for step in range(len(dims_of(name, wide)))]
        if name < O:
            which, cut = divmod(name - D0, 2)
            acc, out, shift = r.p_v.at[which, :, pl.ds(cut * half, half)], r.out_f[which], cut * half
        else:
            acc, out, shift = accs[name - O], r.out_a[name - O], p.core * half
        u[name] = Unit(
            p,
            dims_of(name, wide),
            acc,
            out,
            shift,
            recvs,
            r.usem.at[name - D0],
            name >= O,
            Y if name < O else None,
            first,
        )

    loads, landed = {}, set()

    def load(key, src, dst):
        loads[key] = pltpu.make_async_copy(src, dst, r.lsem.at[len(loads)])
        loads[key].start()

    def need(*keys):
        for key in keys:
            if key not in landed:
                loads[key].wait()
                landed.add(key)

    def spot(c, second):
        return pl.ds(2 * rows + (2 * c + second) * size, size)

    def remotes(row, src_of, dst_of, device):
        return [
            remote(src_of(c), dst_of(c), r.xsem.at[row, c], r.xsem.at[row + 1, c], device)
            for c in range(PIECES)
        ]

    def piece(ref):
        return lambda c: ref.at[pl.ds(c * size, size)]

    gather = remotes(0, piece(r.n2), lambda c: r.X.at[spot(c, 0)], p.flip_x)
    onward = remotes(2, lambda c: r.X.at[spot(c, 0)], lambda c: r.X.at[spot(c, 1)], p.flip_core)
    across = remote(r.n2, r.X.at[pl.ds(rows, rows)], r.xsem.at[16, 0], r.xsem.at[16, 1], p.flip_core)
    back_core = remotes(4, piece(r.to_core), piece(r.from_core), p.flip_core)
    back_own = remotes(6, piece(r.own_core), piece(r.own_from), p.flip_core)
    back_x = remotes(8, piece(r.to_x), piece(r.from_x), p.flip_x)
    out_core = remotes(10, piece(r.to_core), piece(r.o_from_core), p.flip_core)
    out_own = remotes(12, piece(r.own_core), piece(r.o_own_from), p.flip_core)

    for copy in gather:
        copy.start()
    across.start()
    load("x", r.n2, r.X.at[pl.ds(0, rows)])
    load("wl", r.wl, wl_v)
    load("wr", r.wr, wr_v)
    load("wd", r.wd, wd_v)
    load("g", r.cot, r.G.at[pl.ds(0, rows)])
    load("g_far", r.cotall, r.G.at[pl.ds(rows, 3 * rows)])

    def act(here):
        x = r.X[here, :]
        left = nt(x, wl_v[...])
        right = nt(x, wr_v[...])
        r.prod[here, :] = (left * right).astype(BF16)
        up = nt(r.G[here, :], wd_v[...])
        r.gl[here, :] = (up * right).astype(BF16)
        r.gr[here, :] = (up * left).astype(BF16)
        return nn(r.gl[here, :], wl_v[...]) + nn(r.gr[here, :], wr_v[...])

    def out_part(here):
        return nn(r.prod[here, :], wd_v[...])

    need("x", "wl", "wr", "wd", "g")

    @pl.loop(0, rows // group)
    def _(i):
        r.own[part(i, group), :] = act(part(i, group))

    across.wait_recv()
    need("g_far")

    @pl.loop(0, rows // group)
    def _(i):
        r.own_core[part(i, group), :] = act(pl.ds(pl.multiple_of(rows + i * group, group), group)).astype(BF16)

    for copy in back_own:
        copy.start()
    gather[0].wait_recv()
    onward[0].start()

    def out_own_rows(i):
        r.o_sum[part(i, group), :] = out_part(part(i, group)).astype(BF16)

    def out_core_rows(i):
        if i == 0:
            for copy in back_own:
                copy.wait_send()
        r.own_core[part(i, group), :] = out_part(pl.ds(rows + i * group, group)).astype(BF16)

    def far(c):
        here = pl.ds(2 * rows + 2 * c * size, 2 * size)
        got = act(here)
        r.keep[pl.ds(c * size, size), :] = got[:size]
        r.to_core[pl.ds(c * size, size), :] = got[size:].astype(BF16)
        back_core[c].start()

    def far_send(c):
        back_core[c].wait_recv()
        here = pl.ds(c * size, size)
        r.to_x[here, :] = (r.keep[here, :] + r.from_core[here, :].astype(F32)).astype(BF16)
        back_x[c].start()

    fill = [
        lambda: out_own_rows(0),
        lambda: out_own_rows(1),
        lambda: out_core_rows(0),
        lambda: out_core_rows(1),
    ]
    for c in range(PIECES):
        fill[c]()
        onward[c].wait_recv()
        far(c)
        if c + 1 < PIECES:
            if c:
                far_send(c - 1)
            gather[c + 1].wait_recv()
            onward[c + 1].start()
    for copy in out_own:
        copy.start()
    far_send(PIECES - 2)

    def out_far(c):
        got = out_part(pl.ds(2 * rows + 2 * c * size, 2 * size)).astype(BF16)
        here = pl.ds(c * size, size)
        r.o_x[here, :] = got[:size]
        back_core[c].wait_send()
        r.to_core[here, :] = got[size:]
        out_core[c].start()

    out_far(0)
    far_send(PIECES - 1)
    load("hidden", r.hidden, hid_v)
    load("wo", r.wo, wa)
    load("ko", r.ko, r.ko_v)
    load("sin", r.sin, r.sin_v)
    out_x = remote(r.o_x, r.out_rx, r.osem.at[2], r.osem.at[3], p.flip_x)
    to_sib = [
        remote(r.mixed, r.mix_sib, r.csem.at[0], r.csem.at[1], p.flip_core),
        remote(r.n1, r.n1_sib, r.csem.at[2], r.csem.at[3], p.flip_core),
    ]
    for copy in to_sib:
        copy.start()

    def out_far_next():
        out_far(turn[3])
        turn[3] += 1

    def out_sums():
        for c in range(PIECES):
            out_core[c].wait_recv()
            out_own[c].wait_recv()
            here = pl.ds(c * size, size)
            r.o_x[here, :] = r.o_x[here, :] + r.o_from_core[here, :]
            r.o_sum[here, :] = r.o_sum[here, :] + r.o_own_from[here, :]
        for copy in out_core + out_own:
            copy.wait_send()
        load("flat", r.flat, flat_v)
        load("gate", r.gate, gate_v)
        load("wk", r.wk, wc)

    def weight(which, left, right):
        cut = 384 if hidden > 384 else hidden
        for base, extent in ((0, cut), (cut, hidden - cut)):
            if extent:
                here = pl.ds(base, extent)
                r.p_v[which, here, :] = tn(left[:, here], right[...]).astype(BF16)

    def weight_last():
        weight(2, r.gr, r.X)
        for copy in onward:
            copy.wait_send()
        load("q", r.q, q_v)
        load("mixed", r.mixed, mix_v)
        load("n1", r.n1, n1_v)
        load("k", r.k, k_v)
        load("v", r.v, v_v)
        load("dq", r.dq, dq_v)
        load("dk", r.dk, dk_v)

    ends = segment_ends(r.lens)
    halves = {}

    def send_half(key, src):
        slot = key - O
        halves[key] = remote(
            src.at[:, theirs], r.sib.at[slot], r.csem.at[4 + 2 * slot], r.csem.at[5 + 2 * slot], p.flip_core
        )
        halves[key].start()

    def fold(x):
        return jnp.sum(x.reshape(x.shape[0] // 8, 8, x.shape[1]), axis=0)

    def second_norm():
        r.gsum[...] = jnp.zeros_like(r.gsum)
        for c in range(PIECES):
            back_own[c].wait_recv()
            back_x[c].wait_recv()
        need("hidden")

        @pl.loop(0, rows // tile)
        def _(i):
            here = part(i, tile)
            hid = hid_v[here, :]
            scale = lax.rsqrt(jnp.mean(hid * hid, axis=-1, keepdims=True) + eps)
            unit = hid * scale
            up = gn2_v[here, :] + r.own_from[here, :].astype(F32) + r.from_x[here, :].astype(F32)
            r.gsum[1] += fold(up * unit)
            up = up * r.fgain[...]
            down = scale * (up - unit * jnp.mean(up * unit, axis=-1, keepdims=True))
            down = down + cot_v[here, :].astype(F32)
            hid_v[here, :] = down
            gb[here, :] = down.astype(BF16)

        load("tok", r.tokens, cot_v)
        send_half(O, gb)

    def gates():
        for copy in back_x:
            copy.wait_send()
        need("wo", "flat", "gate", "ko")

        @pl.loop(0, rows // 256)
        def _(i):
            here = part(i, 256)
            gm = nt(gb[here, :], wa[...])
            flat = flat_v[here, :].astype(F32)
            gg[here, :] = (gm * flat).astype(BF16)
            gm = gm * gate_v[here, :].astype(F32)
            ko = r.ko_v[here, :]
            for h in range(heads):
                cols = slice(h * head, (h + 1) * head)
                up, unit = gm[:, cols], flat[:, cols]
                mean = jnp.mean(up * unit, axis=-1, keepdims=True)
                ga_v[here, cols] = (ko[:, h : h + 1] * (up - unit * mean)).astype(BF16)

        send_half(G, gg)
        load("wq", r.wq, wa)

    def states():
        segment_setup(p, ends, r.rate_row, rows, r.gate_in, r.keep_out, r.reach, False)
        need("q")
        for h in range(heads):
            cols = slice(h * head, (h + 1) * head)
            gated = (q_v[:, cols].astype(F32) * r.gate_in[:, h : h + 1]).astype(BF16)
            r.state_a[pl.ds(h * head, head), :] = tn(gated, ga_v[:, cols]).astype(BF16)
        scatter_states(p, r.state_a, r.arrived, r.ssem.at[0], r.ssem.at[1], chunk)

    def weight_unit(name, left, own):
        acc = accs[name - O]
        other = r.sib.at[name - O]
        halves[name].wait_recv()

        @pl.loop(0, width // 512)
        def _(i):
            here = part(i, 512)
            acc[here, :] = (
                tn(left[0][:, here], own[:, mine]) + tn(left[1][:, here], other[...])
            ).astype(BF16)

        u[name].advance()

    def weight_o():
        need("mixed")
        to_sib[0].wait_recv()
        weight_unit(O, (mix_v, r.mix_sib), gb)

    def weight_g():
        need("n1")
        to_sib[1].wait_recv()
        weight_unit(G, (n1_v, r.n1_sib), gg)


    def inside():
        need("k", "v", "sin", "dq", "dk")
        first = turn[0]
        turn[0] += heads // 8

        def one(h, carry):
            cols = part(h, head)
            q, k, v, ga = q_v[:, cols], k_v[:, cols], v_v[:, cols], ga_v[:, cols]
            weight = decay_of(r.reach[...], r.rate_s[h])
            probs = (nt(k, q) * weight).astype(BF16)
            gv_v[:, cols] = nn(probs, ga).astype(BF16)
            scores = (nt(v, ga) * weight).astype(BF16)
            gn2_v[:, cols] = nn(scores, q)
            pick = lax.broadcasted_iota(jnp.int32, (1, heads), 1) == h
            gate = jnp.sum(jnp.where(pick, r.gate_in[...], 0.0), axis=1, keepdims=True)
            gq = tn(scores, k) + nt(ga, r.sin_v[cols, :]) * gate
            gq_v[:, cols] = (gq * dq_v[:, cols].astype(F32)).astype(BF16)
            return carry

        lax.fori_loop(first, turn[0], one, 0)
        if turn[0] == heads:
            send_half(Q, gq_v)

    def join():
        wait_states(p, r.state_a, r.arrived, r.ssem.at[0], r.ssem.at[1], chunk)
        rate = r.rate_s[lax.div(p.w * chunk, head)]
        join_states(p, ends, rate, rows, r.arrived, r.joined, True)
        return_states(p, r.joined, r.state_b, r.ssem.at[2], r.ssem.at[3], chunk)

    def with_states():
        wait_returned(p, r.joined, r.state_b, r.ssem.at[2], r.ssem.at[3], chunk)
        for h in range(heads):
            cols = slice(h * head, (h + 1) * head)
            state = r.state_b[pl.ds(h * head, head), :]
            keep = r.keep_out[:, h : h + 1]
            gk = gn2_v[:, cols] + nt(v_v[:, cols], state) * keep
            flat_v[:, cols] = (gk * dk_v[:, cols].astype(F32)).astype(BF16)
            gv = gv_v[:, cols].astype(F32) + nn(k_v[:, cols], state) * keep
            gate_v[:, cols] = gv.astype(BF16)
        send_half(K, flat_v)
        send_half(V, gate_v)
        load("hidden_again", r.hidden, gn2_v)
        load("wv", r.wv, wv_v)
        load("wg", r.wg, wg_v)

    def first_norm():
        need("wq", "wk", "wv", "wg", "tok")
        size = rows // 2
        here = pl.ds(turn[1] * size, size)
        turn[1] += 1
        up = (
            nt(gq_v[here, :], wa[...])
            + nt(flat_v[here, :], wc[...])
            + nt(gate_v[here, :], wv_v[...])
            + nt(gg[here, :], wg_v[...])
        )
        tok = cot_v[here, :].astype(F32)
        scale = lax.rsqrt(jnp.mean(tok * tok, axis=-1, keepdims=True) + eps)
        unit = tok * scale
        r.gsum[0] += fold(up * unit)
        up = up * r.again[...]
        down = scale * (up - unit * jnp.mean(up * unit, axis=-1, keepdims=True))
        hid_v[here, :] += down
        if turn[1] == 2:
            stores["gtok"].start()
            r.gains[0] = jnp.zeros_like(r.gains[0])
            for row in range(2):
                r.gains[0, pl.ds(row, 1), :] = jnp.sum(r.gsum[row], axis=0, keepdims=True)

    stores = {
        "gtok": pltpu.make_async_copy(hid_v, r.gtok, r.osem.at[0]),
        "gain": pltpu.make_async_copy(r.gains.at[2 + len(p.bits)], r.out_gain, r.osem.at[1]),
        "out": pltpu.make_async_copy(out_v, r.out, r.osem.at[4]),
    }

    def output():
        out_x.wait_recv()
        need("hidden_again")

        @pl.loop(0, rows // tile)
        def _(i):
            here = part(i, tile)
            total = r.o_sum[here, :].astype(F32) + r.out_rx[here, :].astype(F32)
            out_v[here, :] = (gn2_v[here, :] + total).astype(BF16)

        stores["out"].start()

    gain_to = [p.flip_core, p.flip_x] + [p.partner(bit) for bit in p.bits]
    many = len(gain_to)

    def gain_copy(step):
        return remote(
            r.gains.at[step], r.grecv.at[step], r.gsem.at[2 * step], r.gsem.at[2 * step + 1], gain_to[step]
        )

    def gain():
        step = turn[2]
        turn[2] += 1
        if step:
            gain_copy(step - 1).wait_recv()
            r.gains[step] = r.gains[step - 1] + r.grecv[step - 1]
        if step < many:
            gain_copy(step).start()
        else:
            stores["gain"].start()

    steps = {
        S1: second_norm,
        S2: gates,
        S3: states,
        WO: weight_o,
        WG: weight_g,
        WQ: lambda: weight_unit(Q, (n1_v, r.n1_sib), gq_v),
        WK: lambda: weight_unit(K, (n1_v, r.n1_sib), flat_v),
        WV: lambda: weight_unit(V, (n1_v, r.n1_sib), gate_v),
        INSIDE: inside,
        JOIN: join,
        S5: with_states,
        S6: first_norm,
        OUT: output,
        OUTX: out_x.start,
        WD: lambda: weight(0, r.prod, r.G),
        WL: lambda: weight(1, r.gl, r.X),
        WR: weight_last,
        OUTFAR: out_far_next,
        OUTSUM: out_sums,
        GAIN: gain,
    }
    for step in ORDER:
        if step in u:
            u[step].advance()
        else:
            steps[step]()
    while turn[2] <= many:
        gain()
    for one in u.values():
        one.close()
    for copy in stores.values():
        copy.wait()
    out_x.wait_send()
    for copy in to_sib + [across]:
        copy.wait_send()
    for copy in gather:
        copy.wait_send()
    for copy in halves.values():
        copy.wait_send()
    for step in range(many):
        gain_copy(step).wait_send()


def main_call(wide, heads, eps, arrays):
    rows, width = arrays["n2"].shape
    hidden = arrays["wl"].shape[0]
    half = width // 2
    bits = wide.bit_length() - 1
    tall = tall_of(wide, hidden)
    specs = {"lens": IN_SMEM, "rate_s": IN_SMEM, "rate_row": IN_VMEM, "fgain": IN_VMEM, "again": IN_VMEM}
    ins = {nm: (a, specs.get(nm, ANY)) for nm, a in arrays.items()}
    sds = jax.ShapeDtypeStruct
    outs = {("a", i): sds((width, width), BF16) for i in range(5)}
    outs.update({("f", i): sds((tall, width), BF16) for i in range(3)})
    outs["out"] = sds((rows, width), BF16)
    outs["gtok"] = sds((rows, width), F32)
    outs["out_gain"] = sds((8, width), F32)
    VM = pltpu.VMEM
    dma = pltpu.SemaphoreType.DMA
    few = ("to_core", "from_core", "own_core", "own_from", "to_x", "from_x")
    few += ("o_sum", "o_x", "o_from_core", "o_own_from", "out_rx", "mix_sib", "n1_sib")
    scratch = {nm: VM((rows, width), BF16) for nm in few}
    scratch.update({nm: VM((rows, width), F32) for nm in ("own", "keep")})
    scratch.update({nm: VM((4 * rows, hidden), BF16) for nm in ("prod", "gl", "gr")})
    scratch.update({nm: VM((4 * rows, width), BF16) for nm in ("X", "G")})
    scratch.update({nm: VM((rows, heads), F32) for nm in ("ko_v", "gate_in", "keep_out")})
    scratch.update({nm: VM((width, width // heads), BF16) for nm in ("sin_v", "state_a", "state_b")})
    scratch.update({nm: VM((wide, width // wide, width // heads), BF16) for nm in ("arrived", "joined")})
    scratch.update(
        wf=VM((3 * hidden, width), BF16),
        p_v=VM((3, tall, width), BF16),
        sib=VM((5, rows, half), BF16),
        reach=VM((rows, rows), F32),
        gsum=VM((2, 8, width), F32),
        gains=VM((3 + bits, 8, width), F32),
        grecv=VM((2 + bits, 8, width), F32),
        lsem=dma((32,)),
        csem=dma((14,)),
        ssem=dma((4, wide)),
        xsem=dma((17, PIECES)),
        usem=dma((11, 4 * (bits + 1) + 4)),
        gsem=dma((4 + 2 * bits,)),
        osem=dma((5,)),
    )
    for name in range(D0, V + 1):
        for step, shape in enumerate(arrivals(name, wide, tall if name < O else width, half)):
            scratch["r", name, step] = VM(shape, BF16)
    return call_kernel(lambda r: main_body(wide, heads, eps, r), "whole_block", 3, ins, outs, scratch, 40 * 10**9)


def widen_body(r):
    jobs = []
    for key, src in r.src.items():
        dst, wide_v, narrow_v = r.dst[key], r.wide_v[key], r.narrow_v[key]
        rows = dst.shape[0]
        size = rows // 4 if rows % 64 == 0 else rows
        for base in range(0, rows, size):
            here = pl.ds(base, size)
            jobs.append((src.at[here], narrow_v.at[here], wide_v.at[here], dst.at[here]))
    reads = [pltpu.make_async_copy(job[0], job[1], r.rsem.at[i]) for i, job in enumerate(jobs)]
    writes = [pltpu.make_async_copy(job[2], job[3], r.wsem.at[i]) for i, job in enumerate(jobs)]
    plain_in = [
        pltpu.make_async_copy(r.gtok, r.gtok_v, r.psem.at[4]),
        pltpu.make_async_copy(r.out, r.out_v, r.psem.at[5]),
    ]
    plain = [
        pltpu.make_async_copy(r.gtok_v, r.gtok_out, r.psem.at[0]),
        pltpu.make_async_copy(r.out_v, r.out_out, r.psem.at[1]),
    ]
    for copy in plain_in + reads:
        copy.start()
    for first, second in zip(plain_in, plain, strict=True):
        first.wait()
        second.start()
    for i in range(2):
        r.gain_v[i] = r.gains[i]
    plain += [pltpu.make_async_copy(r.gain_v.at[i], dst, r.psem.at[2 + i]) for i, dst in enumerate((r.gain0, r.gain1))]
    for copy in plain[2:]:
        copy.start()
    for job, read, write in zip(jobs, reads, writes, strict=True):
        read.wait()
        narrow, wide = job[1], job[2]
        tile = math.gcd(narrow.shape[0], 64)

        @pl.loop(0, narrow.shape[0] // tile)
        def _(i):
            wide[part(i, tile), :] = narrow[part(i, tile), :].astype(F32)

        write.start()
    for copy in writes + plain:
        copy.wait()


def widen(done, hidden):
    keys = [key for key in done if isinstance(key, tuple)]
    rows, width = done["out"].shape
    sds = jax.ShapeDtypeStruct
    high = {key: hidden if key[0] == "f" else width for key in keys}
    names, ins, specs = [], [], []
    for key in keys:
        names.append(("s", key))
        ins.append(done[key])
        specs.append(ANY)
    for name, spec in (("gtok", ANY), ("out", ANY), ("gains", IN_VMEM)):
        names.append(name)
        ins.append(done["out_gain"] if name == "gains" else done[name])
        specs.append(spec)
    outs = {("d", key): sds((high[key], width), F32) for key in keys}
    outs["gtok_out"] = sds((rows, width), F32)
    outs["out_out"] = sds((rows, width), BF16)
    outs["gain0"] = sds((width,), F32)
    outs["gain1"] = sds((width,), F32)
    dma = pltpu.SemaphoreType.DMA
    scratch = {("w", key): pltpu.VMEM((high[key], width), F32) for key in keys}
    scratch.update({("n", key): pltpu.VMEM((high[key], width), BF16) for key in keys})
    scratch.update(gain_v=pltpu.VMEM((2, width), F32), rsem=dma((32,)), wsem=dma((32,)), psem=dma((6,)))
    scratch.update(gtok_v=pltpu.VMEM((rows, width), F32), out_v=pltpu.VMEM((rows, width), BF16))
    names += list(outs) + list(scratch)
    results = pl.pallas_call(
        lambda *refs: widen_body(Refs(names, refs)),
        name="widen",
        out_shape=list(outs.values()),
        in_specs=specs,
        out_specs=[ANY] * len(outs),
        scratch_shapes=list(scratch.values()),
        compiler_params=pltpu.CompilerParams(vmem_limit_bytes=VMEM_BYTES),
    )(*ins)
    return dict(zip(outs, results, strict=True))


def body(
    tokens,
    cotangent,
    lengths,
    decay_rate,
    attn_gain,
    w_query,
    w_key,
    w_value,
    w_gate,
    w_out,
    ffn_gain,
    w_left,
    w_right,
    w_down,
):
    wide = lax.axis_size("wide")
    heads = decay_rate.shape[0]
    hidden = w_down.shape[0]
    shared = dict(
        lens=lengths,
        rate_s=decay_rate,
        rate_row=decay_rate[None],
        fgain=ffn_gain[None],
        again=attn_gain[None],
        wq=w_query,
        wk=w_key,
        wv=w_value,
        wg=w_gate,
        wo=w_out,
        tokens=tokens[0],
        cot=cotangent[0],
    )
    first = forward_call(wide, heads, EPS, shared)
    gated = dict(wl=w_left.T, wr=w_right.T, wd=w_down)
    done = main_call(wide, heads, EPS, {**shared, **first, **gated})
    last = widen(done, hidden)
    g_o, g_g, g_q, g_k, g_v = [last["d", ("a", i)] for i in range(5)]
    g_d, g_l, g_r = [last["d", ("f", i)] for i in range(3)]
    return (
        last["out_out"][None],
        last["gtok_out"][None],
        g_q,
        g_k,
        g_v,
        g_g,
        g_o,
        last["gain0"],
        last["gain1"],
        g_l.T,
        g_r.T,
        g_d,
    )


def solution(mesh):
    placed = (
        P("narrow", "wide", None),
        P("narrow", "wide", None),
        P("narrow", None),
        P(),
        P(),
        P(),
        P(),
        P(),
        P(),
        P(),
        P(),
        P(None, "narrow"),
        P(None, "narrow"),
        P("narrow", None),
    )
    return jax.shard_map(
        body,
        mesh=mesh,
        in_specs=placed,
        out_specs=(
            P("narrow", "wide", None),
            P("narrow", "wide", None),
            P(),
            P(),
            P(),
            P(),
            P(),
            P(),
            P(),
            P(None, "narrow"),
            P(None, "narrow"),
            P("narrow", None),
        ),
        check_vma=False,
    )
```

```python
import math

import jax
import jax.numpy as jnp
from jax import lax
from jax.experimental import pallas as pl
from jax.experimental.pallas import tpu as pltpu
from jax.sharding import PartitionSpec as P

EPS = 1e-06

MESH = pl.DeviceIdType.MESH
F32 = jnp.float32
BF16 = jnp.bfloat16
VMEM_BYTES = 63 * 1024 * 1024
ANY = pl.BlockSpec(memory_space=pl.ANY)
IN_VMEM = pl.BlockSpec(memory_space=pltpu.VMEM)
IN_SMEM = pl.BlockSpec(memory_space=pltpu.SMEM)


class Refs:
    def __init__(self, names, refs):
        self.recv, self.out_a, self.out_f = {}, {}, {}
        self.src, self.dst, self.wide_v, self.narrow_v = {}, {}, {}, {}
        groups = {"r": self.recv, "a": self.out_a, "f": self.out_f}
        groups.update(s=self.src, d=self.dst, w=self.wide_v, n=self.narrow_v)
        for name, ref in zip(names, refs, strict=True):
            if isinstance(name, str):
                setattr(self, name, ref)
            else:
                groups[name[0]][name[1:] if len(name) > 2 else name[1]] = ref


def call_kernel(body, name, number, ins, outs, scratch, cost):
    names = list(ins) + list(outs) + list(scratch)

    def kernel(*refs):
        body(Refs(names, refs))

    results = pl.pallas_call(
        kernel,
        name=name,
        out_shape=list(outs.values()),
        in_specs=[spec for _, spec in ins.values()],
        out_specs=[ANY] * len(outs),
        scratch_shapes=list(scratch.values()),
        cost_estimate=pl.CostEstimate(flops=cost, bytes_accessed=cost // 500, transcendentals=0),
        compiler_params=pltpu.CompilerParams(
            collective_id=number, has_side_effects=True, vmem_limit_bytes=VMEM_BYTES
        ),
    )(*[array for array, _ in ins.values()])
    return dict(zip(outs, results, strict=True))


def nn(left, right):
    return lax.dot_general(left, right, (((1,), (0,)), ((), ())), preferred_element_type=F32)


def nt(left, right):
    return lax.dot_general(left, right, (((1,), (1,)), ((), ())), preferred_element_type=F32)


def tn(left, right):
    return lax.dot_general(left, right, (((0,), (0,)), ((), ())), preferred_element_type=F32)


def part(index, size):
    return pl.ds(pl.multiple_of(index * size, size), size)


def round_up(number, step):
    return -(-number // step) * step


class Place:
    def __init__(self, wide):
        self.wide = wide
        self.w = lax.axis_index("wide")
        self.n = lax.axis_index("narrow")
        self.core = lax.rem(self.n, 2)
        self.xh = lax.div(self.n, 2)
        self.flip_core = (self.w, self.n + 1 - 2 * self.core)
        self.flip_x = (self.w, self.n + 2 - 4 * self.xh)
        self.bits = tuple(range(wide.bit_length() - 1))

    def bit(self, dim):
        return self.xh if dim == X else lax.rem(lax.div(self.w, 2**dim), 2)

    def partner(self, dim):
        if dim == X:
            return self.flip_x
        return (self.w + (1 - 2 * self.bit(dim)) * 2**dim, self.n)

    def on_wide(self, w):
        return (w, self.n)


def greet(partners, place, whole_wide):
    barrier = pltpu.get_barrier_semaphore()
    for partner in partners:
        pl.semaphore_signal(barrier, inc=1, device_id=partner, device_id_type=MESH)
    count = len(partners)
    if whole_wide:

        def one(step, carry):
            pl.semaphore_signal(
                barrier,
                inc=1,
                device_id=place.on_wide(lax.rem(place.w + step, place.wide)),
                device_id_type=MESH,
            )
            return carry

        lax.fori_loop(1, place.wide, one, 0)
        count += place.wide - 1
    pl.semaphore_wait(barrier, count)


def remote(src, dst, send, recv, device):
    return pltpu.make_async_remote_copy(
        src_ref=src, dst_ref=dst, send_sem=send, recv_sem=recv, device_id=device, device_id_type=MESH
    )


def segment_ends(lens):
    ends = []
    total = jnp.int32(0)
    for slot in range(lens.shape[1]):
        total = total + lens[0, slot]
        ends.append(total)
    return ends


def count_ends(ends, spots):
    total = jnp.zeros_like(spots)
    for end in ends:
        total = total + jnp.where(spots >= end, 1, 0)
    return total


def segment_setup(place, ends, rate_row, rows, gate_ref, keep_ref, reach_ref, later_first):
    anchor = place.w * rows
    col_local = lax.broadcasted_iota(jnp.int32, (rows, 1), 0)
    row_local = lax.broadcasted_iota(jnp.int32, (1, rows), 1)
    col_seg = count_ends(ends, col_local + anchor)
    row_seg = count_ends(ends, row_local + anchor)
    before = jnp.int32(0)
    last = jnp.int32(0)
    for end in ends:
        before = before + jnp.where(anchor - 1 >= end, 1, 0)
        last = last + jnp.where(anchor + rows - 1 >= end, 1, 0)
    before = jnp.where(place.w > 0, before, -1)
    col_live = (col_local + anchor) < ends[-1]
    row_live = (row_local + anchor) < ends[-1]
    rates = rate_row[...]
    steps = col_local.astype(F32)
    gate_ref[...] = jnp.exp(-(steps + 1.0) * rates) * jnp.where(
        (col_seg == before) & col_live, 1.0, 0.0
    )
    keep_ref[...] = jnp.exp(-(rows - 1.0 - steps) * rates) * jnp.where(
        (col_seg == last) & col_live, 1.0, 0.0
    )
    gap = col_local - row_local if later_first else row_local - col_local
    reaches = (gap >= 0) & (col_seg == row_seg) & row_live & col_live
    reach_ref[...] = jnp.where(reaches, gap.astype(F32), -1.0)


def decay_of(reach, rate):
    return jnp.where(reach >= 0.0, jnp.exp(-rate * reach), 0.0)


def scatter_states(place, local, arrived, sends, recvs, chunk):
    def one(step, carry):
        target = lax.rem(place.w + step, place.wide)
        remote(
            local.at[part(target, chunk)],
            arrived.at[place.w],
            sends.at[target],
            recvs.at[place.w],
            place.on_wide(target),
        ).start()
        return carry

    lax.fori_loop(1, place.wide, one, 0)
    arrived[place.w] = local[part(place.w, chunk), :]


def wait_states(place, local, arrived, sends, recvs, chunk):
    def one(step, carry):
        source = lax.rem(place.w + step, place.wide)
        copy = remote(
            local.at[part(source, chunk)],
            arrived.at[source],
            sends.at[source],
            recvs.at[source],
            place.on_wide(source),
        )
        copy.wait_recv()
        copy.wait_send()
        return carry

    lax.fori_loop(1, place.wide, one, 0)


def join_states(place, ends, rate, rows, arrived, joined, backward):
    shape = arrived.shape[1:]
    fade = jnp.exp(jnp.full((1, shape[1]), -1.0 * rows, F32) * rate)

    def one(step, state):
        block = place.wide - 1 - step if backward else step
        joined[block] = state.astype(BF16)
        cuts = jnp.int32(0)
        for end in ends:
            inside = (end >= block * rows) & (end <= block * rows + rows - 1)
            cuts = cuts + jnp.where(inside, 1, 0)
        flag = jnp.where((cuts == 0) & (block > 0), 1.0, 0.0)
        return (fade * flag) * state + arrived[block].astype(F32)

    lax.fori_loop(0, place.wide, one, jnp.zeros(shape, F32))


def return_states(place, joined, entering, sends, recvs, chunk):
    def one(step, carry):
        target = lax.rem(place.w + step, place.wide)
        remote(
            joined.at[target],
            entering.at[part(place.w, chunk)],
            sends.at[target],
            recvs.at[place.w],
            place.on_wide(target),
        ).start()
        return carry

    lax.fori_loop(1, place.wide, one, 0)
    entering[part(place.w, chunk), :] = joined[place.w]


def wait_returned(place, joined, entering, sends, recvs, chunk):
    def one(step, carry):
        source = lax.rem(place.w + step, place.wide)
        copy = remote(
            joined.at[source],
            entering.at[part(source, chunk)],
            sends.at[source],
            recvs.at[source],
            place.on_wide(source),
        )
        copy.wait_recv()
        copy.wait_send()
        return carry

    lax.fori_loop(1, place.wide, one, 0)


class Unit:
    def __init__(self, place, dims, acc, out, shift, recvs, sems, is_core, by_columns, first=0):
        self.place, self.dims, self.acc, self.out, self.shift = place, dims, acc, out, shift
        self.recvs, self.sems, self.is_core = recvs, sems, is_core
        self.first, self.stage = first, None
        self.count = 2 * len(dims) + is_core
        self.keep, self.give = [], []
        (rows, cols), row, col = acc.shape, 0, 0
        self.whole = (row, rows, col, cols)
        for dim in dims:
            bit = place.bit(dim)
            if dim == by_columns:
                cols //= 2
                self.keep.append((row, rows, col + bit * cols, cols))
                self.give.append((row, rows, col + (1 - bit) * cols, cols))
            else:
                rows //= 2
                self.keep.append((row + bit * rows, rows, col, cols))
                self.give.append((row + (1 - bit) * rows, rows, col, cols))
            row, rows, col, cols = self.keep[-1]

    def at(self, ref, region, shift=0):
        row, rows, col, cols = region
        down = pl.ds(pl.multiple_of(row, rows), rows)
        return ref.at[down, pl.ds(pl.multiple_of(col + shift, cols), cols)]

    def copy(self, stage):
        many = len(self.dims)
        send, recv = self.sems.at[2 * stage], self.sems.at[2 * stage + 1]
        if stage < many:
            src = self.at(self.acc, self.give[stage])
            return remote(src, self.recvs[stage], send, recv, self.place.partner(self.dims[stage]))
        if stage == 2 * many:
            region = self.at(self.out, self.whole, self.shift)
            return remote(region, region, send, recv, self.place.flip_core)
        step = 2 * many - 1 - stage
        dst = self.at(self.out, self.keep[step], self.shift)
        src = self.at(self.acc, self.keep[step]) if stage == many else dst
        return remote(src, dst, send, recv, self.place.partner(self.dims[step]))

    def local(self):
        return pltpu.make_async_copy(
            self.at(self.acc, self.keep[-1]),
            self.at(self.out, self.keep[-1], self.shift),
            self.sems.at[2 * self.count],
        )

    def take(self, stage):
        many = len(self.dims)
        self.copy(stage).wait_recv()
        if stage < many:
            row, rows, col, cols = self.keep[stage]
            add_into(self.acc, row, pl.ds(pl.multiple_of(col, cols), cols), self.recvs[stage])
        elif stage == many:
            self.local().wait()

    def advance(self):
        if self.stage is None:
            self.stage = self.first
        elif self.stage < self.count:
            self.take(self.stage)
            self.stage += 1
        if self.stage < self.count:
            self.copy(self.stage).start()
            if self.stage == len(self.dims):
                self.local().start()

    def close(self):
        while self.stage < self.count:
            self.advance()
        for stage in range(self.first, self.count):
            self.copy(stage).wait_send()


def add_into(acc, base, cols, other):
    rows = other.shape[0]
    tile = math.gcd(rows, 128)

    @pl.loop(0, rows // tile)
    def _(i):
        here = pl.ds(pl.multiple_of(base + i * tile, tile), tile)
        acc[here, cols] = acc[here, cols] + other[part(i, tile), :]


PIECES = 4


Y, A, B, X = 0, 1, 2, 9
D0, D1, L0, L1, R0, R1, O, G, Q, K, V = range(11)
S1, S2, S3, S5, S6, WO, WG, WQ, WK, WV, INSIDE, JOIN, OUT, OUTX, GAIN, WD, WL, WR, OUTFAR, OUTSUM = range(20, 40)
DIMS = {
    D0: (A, Y, B),
    D1: (Y, A, B),
    L0: (Y, A, B),
    L1: (A, B, Y),
    R0: (Y, A, B),
    R1: (Y, A, B),
    O: (X, Y, A, B),
    G: (X, Y, A, B),
    Q: (X, Y, A, B),
    K: (Y, X, A, B),
    V: (X, Y, A, B),
}
ORDER = (
    WD, D1, D0, OUTFAR, OUTFAR, OUTFAR, OUTSUM, WL, L0, L1, WR, R0, R1, D1, S1, S2, L0, S3, WO, WG, D1,
    INSIDE, INSIDE, L0, R0, INSIDE, INSIDE, D1, D0, R1, O, JOIN, INSIDE, L0, INSIDE, INSIDE, INSIDE, WQ, D1,
    R0, O, G, S5, L0, WK, WV, R0, S6, O, G, Q, S6, GAIN, R0, O, L0, G, K, GAIN, L1, O, Q, G, OUTX, GAIN, R0,
    O, L0, K, Q, GAIN, G, K, Q, R0, V, GAIN, G, D0, O, Q, K, GAIN, OUT, V, D1, Q, D0, K, V, G, R1, O, V, D1,
    O, R1, L1, D0, V, K, Q, G, L1, R1, V, D0, G, K, L1, V, D0, Q, R1, Q, L1, K, K, V, R1, L1, V,
)


def tall_of(wide, hidden):
    return (wide // 2) * round_up(-(-hidden // (wide // 2)), 16)


def dims_of(name, wide):
    return DIMS[name] + tuple(range(3, wide.bit_length() - 1))


def arrivals(name, wide, rows, cols):
    shapes = []
    for dim in dims_of(name, wide):
        if name < O and dim == Y:
            cols //= 2
        else:
            rows //= 2
        shapes.append((rows, cols))
    return shapes


def main_body(wide, heads, eps, r):
    p = Place(wide)
    rows, width = r.tokens.shape
    hidden = r.wl.shape[0]
    tall = tall_of(wide, hidden)
    size = rows // PIECES
    group = 256
    head = width // heads
    half = width // 2
    tile = 128
    chunk = width // wide
    mine = part(p.core, half)
    turn = [0, 0, 0, 1]
    theirs = part(1 - p.core, half)

    greet([p.flip_core, p.flip_x], p, True)

    def rows_of(ref, i):
        return ref.at[pl.ds(i * rows, rows)]

    wl_v, wr_v, wd_v = [r.wf.at[pl.ds(i * hidden, hidden)] for i in range(3)]
    wa, wc = r.wf.at[pl.ds(0, width)], r.wf.at[pl.ds(width, width)]
    wv_v, wg_v = r.X.at[pl.ds(0, width)], r.X.at[pl.ds(width, width)]
    q_v, k_v, v_v, dq_v = [rows_of(r.X, i) for i in range(4)]
    cot_v, dk_v, mix_v, n1_v = [rows_of(r.G, i) for i in range(4)]
    flat_v, gate_v, gb, gg, ga_v, gq_v = r.to_core, r.own_core, r.from_core, r.to_x, r.own_from, r.from_x
    gn2_v, hid_v, out_v, gv_v = r.own, r.keep, dk_v, r.o_own_from
    accs = [
        buf.at[pl.ds((i % 2) * width, width), pl.ds(0, half)]
        for i, buf in enumerate((r.gl, r.gl, r.gr, r.gr, r.prod))
    ]

    u = {}
    for name in range(D0, V + 1):
        first = 0
        recvs = [r.recv.get((name, step)) for step in range(len(dims_of(name, wide)))]
        if name < O:
            which, cut = divmod(name - D0, 2)
            acc, out, shift = r.p_v.at[pl.ds(which * tall, tall), pl.ds(cut * half, half)], r.out_f[which], cut * half
        else:
            acc, out, shift = accs[name - O], r.out_a[name - O], p.core * half
        u[name] = Unit(
            p,
            dims_of(name, wide),
            acc,
            out,
            shift,
            recvs,
            r.usem.at[name - D0],
            name >= O,
            Y if name < O else None,
            first,
        )

    loads, landed = {}, set()

    def load(key, src, dst):
        loads[key] = pltpu.make_async_copy(src, dst, r.lsem.at[len(loads)])
        loads[key].start()

    def need(*keys):
        for key in keys:
            if key not in landed:
                loads[key].wait()
                landed.add(key)

    def spot(c, second):
        return pl.ds(2 * rows + (2 * c + second) * size, size)

    def remotes(row, src_of, dst_of, device):
        return [
            remote(src_of(c), dst_of(c), r.xsem.at[row, c], r.xsem.at[row + 1, c], device)
            for c in range(PIECES)
        ]

    def piece(ref):
        return lambda c: ref.at[pl.ds(c * size, size)]

    gather = remotes(0, piece(r.X), lambda c: r.X.at[spot(c, 0)], p.flip_x)
    onward = remotes(2, lambda c: r.X.at[spot(c, 0)], lambda c: r.X.at[spot(c, 1)], p.flip_core)
    across = remote(r.X.at[pl.ds(0, rows)], r.X.at[pl.ds(rows, rows)], r.xsem.at[16, 0], r.xsem.at[16, 1], p.flip_core)
    back_core = remotes(4, piece(r.to_core), piece(r.from_core), p.flip_core)
    back_own = remotes(6, piece(r.own_core), piece(r.own_from), p.flip_core)
    back_x = remotes(8, piece(r.to_x), piece(r.from_x), p.flip_x)
    out_core = remotes(10, piece(r.to_core), piece(r.o_from_core), p.flip_core)
    out_own = remotes(12, piece(r.own_core), piece(r.o_own_from), p.flip_core)

    tok_a, n1_a, q_a, k_a, v_a = r.to_core, r.from_core, r.own_core, r.own_from, r.to_x
    dq_a, dk_a, gate_a, flat_a, mix_a = r.from_x, r.o_sum, r.o_x, r.o_from_core, r.o_own_from
    raw_f, hid_a, n2_a = r.own, r.keep, r.X.at[pl.ds(0, rows)]
    wk_a, wv_a = r.wf.at[pl.ds(0, width)], r.wf.at[pl.ds(width, width)]
    wq_a, wg_a = r.p_v.at[pl.ds(0, width)], r.p_v.at[pl.ds(width, width)]
    gather_g = remotes(18, piece(r.cot), lambda c: r.G.at[spot(c, 0)], p.flip_x)
    onward_g = remotes(20, lambda c: r.G.at[spot(c, 0)], lambda c: r.G.at[spot(c, 1)], p.flip_core)
    across_g = remote(r.cot, r.G.at[pl.ds(rows, rows)], r.xsem.at[17, 0], r.xsem.at[17, 1], p.flip_core)
    for copy in gather_g:
        copy.start()
    load("a_tokens", r.tokens, tok_a)
    load("a_wk", r.wk, wk_a)
    load("a_wv", r.wv, wv_a)
    load("a_wq", r.wq, wq_a)
    load("a_wg", r.wg, wg_a)
    load("g", r.cot, r.G.at[pl.ds(0, rows)])
    across_g.start()
    ends = segment_ends(r.lens)
    stores_a = []

    def store(src, dst):
        copy = pltpu.make_async_copy(src, dst, r.stsem.at[len(stores_a)])
        copy.start()
        stores_a.append(copy)

    def pass_on(c):
        gather_g[c].wait_recv()
        onward_g[c].start()

    segment_setup(p, ends, r.rate_row, rows, r.gate_in, r.keep_out, r.reach, True)
    need("a_tokens")

    @pl.loop(0, rows // tile)
    def _(i):
        here = part(i, tile)
        tok = tok_a[here, :].astype(F32)
        scale = lax.rsqrt(jnp.mean(tok * tok, axis=-1, keepdims=True) + eps)
        n1_a[here, :] = (tok * scale * r.again[...]).astype(BF16)

    store(n1_a, r.n1)

    def silu_rows(weight, act, slope):
        @pl.loop(0, rows // 256)
        def _(i):
            here = part(i, 256)
            pre = nn(n1_a[here, :], weight[...])
            gate = lax.logistic(pre)
            act[here, :] = (pre * gate).astype(BF16)
            slope[here, :] = (gate * (1.0 + pre * (1.0 - gate))).astype(BF16)

    def plain_rows(weight, dst):
        @pl.loop(0, rows // 256)
        def _(i):
            here = part(i, 256)
            dst[here, :] = nn(n1_a[here, :], weight[...]).astype(BF16)

    need("a_wk")
    silu_rows(wk_a, k_a, dk_a)
    need("a_wv")
    plain_rows(wv_a, v_a)
    load("wl", r.wl, wl_v)
    load("wr", r.wr, wr_v)
    load("wd", r.wd, wd_v)
    for h in range(heads):
        cols = slice(h * head, (h + 1) * head)
        kept = (k_a[:, cols].astype(F32) * r.keep_out[:, h : h + 1]).astype(BF16)
        r.state_a[pl.ds(h * head, head), :] = tn(kept, v_a[:, cols]).astype(BF16)
    scatter_states(p, r.state_a, r.arrived, r.ssem.at[4], r.ssem.at[5], chunk)
    store(k_a, r.k)
    store(dk_a, r.dk)
    store(v_a, r.v)
    need("a_wq")
    silu_rows(wq_a, q_a, dq_a)
    load("a_wo", r.wo, wq_a)
    store(q_a, r.q)
    store(dq_a, r.dq)

    def inside_forward(h, carry):
        cols = part(h, head)
        weight = decay_of(r.reach[...], r.rate_s[h])
        probs = (nt(q_a[:, cols], k_a[:, cols]) * weight).astype(BF16)
        raw_f[:, cols] = nn(probs, v_a[:, cols])
        return carry

    lax.fori_loop(0, heads // 2, inside_forward, 0)
    pass_on(0)
    wait_states(p, r.state_a, r.arrived, r.ssem.at[4], r.ssem.at[5], chunk)
    join_states(p, ends, r.rate_s[lax.div(p.w * chunk, head)], rows, r.arrived, r.joined, False)
    return_states(p, r.joined, r.state_b, r.ssem.at[6], r.ssem.at[7], chunk)
    need("a_wg")
    plain_rows(wg_a, gate_a)
    store(gate_a, r.gate)
    lax.fori_loop(heads // 2, heads, inside_forward, 0)
    pass_on(1)
    wait_returned(p, r.joined, r.state_b, r.ssem.at[6], r.ssem.at[7], chunk)
    store(r.state_b, r.sin)
    for h in range(heads):
        cols = slice(h * head, (h + 1) * head)
        state = r.state_b[pl.ds(h * head, head), :]
        raw = raw_f[:, cols] + nn(q_a[:, cols], state) * r.gate_in[:, h : h + 1]
        scale = lax.rsqrt(jnp.mean(raw * raw, axis=-1, keepdims=True) + eps)
        unit = raw * scale
        r.ko_v[:, h : h + 1] = scale
        flat_a[:, cols] = unit.astype(BF16)
        mix_a[:, cols] = (unit * gate_a[:, cols].astype(F32)).astype(BF16)
    for copy in stores_a:
        copy.wait()
    late = len(stores_a)
    store(r.ko_v, r.ko)
    store(flat_a, r.flat)
    store(mix_a, r.mixed)
    need("a_wo")

    for i in range(rows // group):
        here = pl.ds(i * group, group)
        hid = tok_a[here, :].astype(F32) + nn(mix_a[here, :], wq_a[...])
        scale = lax.rsqrt(jnp.mean(hid * hid, axis=-1, keepdims=True) + eps)
        hid_a[here, :] = hid
        n2_a[here, :] = (hid * scale * r.fgain[...]).astype(BF16)
        for c in range(i * group // size, (i + 1) * group // size):
            gather[c].start()

    store(hid_a, r.hidden)
    for copy in stores_a[late:]:
        copy.wait()
    across.start()
    for c in range(2, PIECES):
        pass_on(c)

    def act(here):
        x = r.X[here, :]
        left = nt(x, wl_v[...])
        right = nt(x, wr_v[...])
        r.prod[here, :] = (left * right).astype(BF16)
        up = nt(r.G[here, :], wd_v[...])
        r.gl[here, :] = (up * right).astype(BF16)
        r.gr[here, :] = (up * left).astype(BF16)
        return nn(r.gl[here, :], wl_v[...]) + nn(r.gr[here, :], wr_v[...])

    def out_part(here):
        return nn(r.prod[here, :], wd_v[...])

    need("wl", "wr", "wd", "g")

    @pl.loop(0, rows // group)
    def _(i):
        r.own[part(i, group), :] = act(part(i, group))

    across.wait_recv()
    across_g.wait_recv()

    @pl.loop(0, rows // group)
    def _(i):
        r.own_core[part(i, group), :] = act(pl.ds(pl.multiple_of(rows + i * group, group), group)).astype(BF16)

    for copy in back_own:
        copy.start()
    gather[0].wait_recv()
    onward[0].start()

    def out_own_rows(i):
        r.o_sum[part(i, group), :] = out_part(part(i, group)).astype(BF16)

    def out_core_rows(i):
        if i == 0:
            for copy in back_own:
                copy.wait_send()
        r.own_core[part(i, group), :] = out_part(pl.ds(rows + i * group, group)).astype(BF16)

    def far(c):
        here = pl.ds(2 * rows + 2 * c * size, 2 * size)
        got = act(here)
        r.keep[pl.ds(c * size, size), :] = got[:size]
        r.to_core[pl.ds(c * size, size), :] = got[size:].astype(BF16)
        back_core[c].start()

    def far_send(c):
        back_core[c].wait_recv()
        here = pl.ds(c * size, size)
        r.to_x[here, :] = (r.keep[here, :] + r.from_core[here, :].astype(F32)).astype(BF16)
        back_x[c].start()

    fill = [
        lambda: out_own_rows(0),
        lambda: out_own_rows(1),
        lambda: out_core_rows(0),
        lambda: out_core_rows(1),
    ]
    for c in range(PIECES):
        fill[c]()
        onward[c].wait_recv()
        onward_g[c].wait_recv()
        far(c)
        if c + 1 < PIECES:
            if c:
                far_send(c - 1)
            gather[c + 1].wait_recv()
            onward[c + 1].start()
    for copy in out_own:
        copy.start()
    far_send(PIECES - 2)

    def out_far(c):
        got = out_part(pl.ds(2 * rows + 2 * c * size, 2 * size)).astype(BF16)
        here = pl.ds(c * size, size)
        r.o_x[here, :] = got[:size]
        back_core[c].wait_send()
        r.to_core[here, :] = got[size:]
        out_core[c].start()

    out_far(0)
    far_send(PIECES - 1)
    load("hidden", r.hidden, hid_v)
    load("wo", r.wo, wa)
    load("ko", r.ko, r.ko_v)
    load("sin", r.sin, r.sin_v)
    out_x = remote(r.o_x, r.out_rx, r.osem.at[2], r.osem.at[3], p.flip_x)
    to_sib = [
        remote(r.mixed, r.mix_sib, r.csem.at[0], r.csem.at[1], p.flip_core),
        remote(r.n1, r.n1_sib, r.csem.at[2], r.csem.at[3], p.flip_core),
    ]
    for copy in to_sib:
        copy.start()

    def out_far_next():
        out_far(turn[3])
        turn[3] += 1

    def out_sums():
        for c in range(PIECES):
            out_core[c].wait_recv()
            out_own[c].wait_recv()
            here = pl.ds(c * size, size)
            r.o_x[here, :] = r.o_x[here, :] + r.o_from_core[here, :]
            r.o_sum[here, :] = r.o_sum[here, :] + r.o_own_from[here, :]
        for copy in out_core + out_own:
            copy.wait_send()
        load("flat", r.flat, flat_v)
        load("gate", r.gate, gate_v)
        load("wk", r.wk, wc)

    def weight(which, left, right):
        cut = 384 if hidden > 384 else hidden
        for base, extent in ((0, cut), (cut, hidden - cut)):
            if extent:
                here = pl.ds(base, extent)
                r.p_v[pl.ds(which * tall + base, extent), :] = tn(left[:, here], right[...]).astype(BF16)

    def weight_last():
        weight(2, r.gr, r.X)
        for copy in onward + onward_g + gather + [across]:
            copy.wait_send()
        load("q", r.q, q_v)
        load("mixed", r.mixed, mix_v)
        load("n1", r.n1, n1_v)
        load("k", r.k, k_v)
        load("v", r.v, v_v)
        load("dq", r.dq, dq_v)
        load("dk", r.dk, dk_v)

    halves = {}

    def send_half(key, src):
        slot = key - O
        halves[key] = remote(
            src.at[:, theirs], r.sib.at[slot], r.csem.at[4 + 2 * slot], r.csem.at[5 + 2 * slot], p.flip_core
        )
        halves[key].start()

    def fold(x):
        return jnp.sum(x.reshape(x.shape[0] // 8, 8, x.shape[1]), axis=0)

    def second_norm():
        r.gsum[...] = jnp.zeros_like(r.gsum)
        for c in range(PIECES):
            back_own[c].wait_recv()
            back_x[c].wait_recv()
        need("hidden")

        @pl.loop(0, rows // tile)
        def _(i):
            here = part(i, tile)
            hid = hid_v[here, :]
            scale = lax.rsqrt(jnp.mean(hid * hid, axis=-1, keepdims=True) + eps)
            unit = hid * scale
            up = gn2_v[here, :] + r.own_from[here, :].astype(F32) + r.from_x[here, :].astype(F32)
            r.gsum[1] += fold(up * unit)
            up = up * r.fgain[...]
            down = scale * (up - unit * jnp.mean(up * unit, axis=-1, keepdims=True))
            down = down + cot_v[here, :].astype(F32)
            hid_v[here, :] = down
            gb[here, :] = down.astype(BF16)

        load("tok", r.tokens, cot_v)
        send_half(O, gb)

    def gates():
        for copy in back_x:
            copy.wait_send()
        need("wo", "flat", "gate", "ko")

        @pl.loop(0, rows // 256)
        def _(i):
            here = part(i, 256)
            gm = nt(gb[here, :], wa[...])
            flat = flat_v[here, :].astype(F32)
            gg[here, :] = (gm * flat).astype(BF16)
            gm = gm * gate_v[here, :].astype(F32)
            ko = r.ko_v[here, :]
            for h in range(heads):
                cols = slice(h * head, (h + 1) * head)
                up, unit = gm[:, cols], flat[:, cols]
                mean = jnp.mean(up * unit, axis=-1, keepdims=True)
                ga_v[here, cols] = (ko[:, h : h + 1] * (up - unit * mean)).astype(BF16)

        send_half(G, gg)
        load("wq", r.wq, wa)

    def states():
        segment_setup(p, ends, r.rate_row, rows, r.gate_in, r.keep_out, r.reach, False)
        need("q")
        for h in range(heads):
            cols = slice(h * head, (h + 1) * head)
            gated = (q_v[:, cols].astype(F32) * r.gate_in[:, h : h + 1]).astype(BF16)
            r.state_a[pl.ds(h * head, head), :] = tn(gated, ga_v[:, cols]).astype(BF16)
        scatter_states(p, r.state_a, r.arrived, r.ssem.at[0], r.ssem.at[1], chunk)

    def weight_unit(name, left, own):
        acc = accs[name - O]
        other = r.sib.at[name - O]
        halves[name].wait_recv()

        @pl.loop(0, width // 512)
        def _(i):
            here = part(i, 512)
            acc[here, :] = (
                tn(left[0][:, here], own[:, mine]) + tn(left[1][:, here], other[...])
            ).astype(BF16)

        u[name].advance()

    def weight_o():
        need("mixed")
        to_sib[0].wait_recv()
        weight_unit(O, (mix_v, r.mix_sib), gb)

    def weight_g():
        need("n1")
        to_sib[1].wait_recv()
        weight_unit(G, (n1_v, r.n1_sib), gg)


    def inside():
        need("k", "v", "sin", "dq", "dk")
        first = turn[0]
        turn[0] += heads // 8

        def one(h, carry):
            cols = part(h, head)
            q, k, v, ga = q_v[:, cols], k_v[:, cols], v_v[:, cols], ga_v[:, cols]
            weight = decay_of(r.reach[...], r.rate_s[h])
            probs = (nt(k, q) * weight).astype(BF16)
            gv_v[:, cols] = nn(probs, ga).astype(BF16)
            scores = (nt(v, ga) * weight).astype(BF16)
            gn2_v[:, cols] = nn(scores, q)
            pick = lax.broadcasted_iota(jnp.int32, (1, heads), 1) == h
            gate = jnp.sum(jnp.where(pick, r.gate_in[...], 0.0), axis=1, keepdims=True)
            gq = tn(scores, k) + nt(ga, r.sin_v[cols, :]) * gate
            gq_v[:, cols] = (gq * dq_v[:, cols].astype(F32)).astype(BF16)
            return carry

        lax.fori_loop(first, turn[0], one, 0)
        if turn[0] == heads:
            send_half(Q, gq_v)

    def join():
        wait_states(p, r.state_a, r.arrived, r.ssem.at[0], r.ssem.at[1], chunk)
        rate = r.rate_s[lax.div(p.w * chunk, head)]
        join_states(p, ends, rate, rows, r.arrived, r.joined, True)
        return_states(p, r.joined, r.state_b, r.ssem.at[2], r.ssem.at[3], chunk)

    def with_states():
        wait_returned(p, r.joined, r.state_b, r.ssem.at[2], r.ssem.at[3], chunk)
        for h in range(heads):
            cols = slice(h * head, (h + 1) * head)
            state = r.state_b[pl.ds(h * head, head), :]
            keep = r.keep_out[:, h : h + 1]
            gk = gn2_v[:, cols] + nt(v_v[:, cols], state) * keep
            flat_v[:, cols] = (gk * dk_v[:, cols].astype(F32)).astype(BF16)
            gv = gv_v[:, cols].astype(F32) + nn(k_v[:, cols], state) * keep
            gate_v[:, cols] = gv.astype(BF16)
        send_half(K, flat_v)
        send_half(V, gate_v)
        load("hidden_again", r.hidden, gn2_v)
        load("wv", r.wv, wv_v)
        load("wg", r.wg, wg_v)

    def first_norm():
        need("wq", "wk", "wv", "wg", "tok")
        size = rows // 2
        here = pl.ds(turn[1] * size, size)
        turn[1] += 1
        up = (
            nt(gq_v[here, :], wa[...])
            + nt(flat_v[here, :], wc[...])
            + nt(gate_v[here, :], wv_v[...])
            + nt(gg[here, :], wg_v[...])
        )
        tok = cot_v[here, :].astype(F32)
        scale = lax.rsqrt(jnp.mean(tok * tok, axis=-1, keepdims=True) + eps)
        unit = tok * scale
        r.gsum[0] += fold(up * unit)
        up = up * r.again[...]
        down = scale * (up - unit * jnp.mean(up * unit, axis=-1, keepdims=True))
        hid_v[here, :] += down
        if turn[1] == 2:
            stores["gtok"].start()
            r.gains[0] = jnp.zeros_like(r.gains[0])
            for row in range(2):
                r.gains[0, pl.ds(row, 1), :] = jnp.sum(r.gsum[row], axis=0, keepdims=True)

    stores = {
        "gtok": pltpu.make_async_copy(hid_v, r.gtok, r.osem.at[0]),
        "gain": pltpu.make_async_copy(r.gains.at[2 + len(p.bits)], r.out_gain, r.osem.at[1]),
        "out": pltpu.make_async_copy(out_v, r.out, r.osem.at[4]),
    }

    def output():
        out_x.wait_recv()
        need("hidden_again")

        @pl.loop(0, rows // tile)
        def _(i):
            here = part(i, tile)
            total = r.o_sum[here, :].astype(F32) + r.out_rx[here, :].astype(F32)
            out_v[here, :] = (gn2_v[here, :] + total).astype(BF16)

        stores["out"].start()

    gain_to = [p.flip_core, p.flip_x] + [p.partner(bit) for bit in p.bits]
    many = len(gain_to)

    def gain_copy(step):
        return remote(
            r.gains.at[step], r.grecv.at[step], r.gsem.at[2 * step], r.gsem.at[2 * step + 1], gain_to[step]
        )

    def gain():
        step = turn[2]
        turn[2] += 1
        if step:
            gain_copy(step - 1).wait_recv()
            r.gains[step] = r.gains[step - 1] + r.grecv[step - 1]
        if step < many:
            gain_copy(step).start()
        else:
            stores["gain"].start()

    steps = {
        S1: second_norm,
        S2: gates,
        S3: states,
        WO: weight_o,
        WG: weight_g,
        WQ: lambda: weight_unit(Q, (n1_v, r.n1_sib), gq_v),
        WK: lambda: weight_unit(K, (n1_v, r.n1_sib), flat_v),
        WV: lambda: weight_unit(V, (n1_v, r.n1_sib), gate_v),
        INSIDE: inside,
        JOIN: join,
        S5: with_states,
        S6: first_norm,
        OUT: output,
        OUTX: out_x.start,
        WD: lambda: weight(0, r.prod, r.G),
        WL: lambda: weight(1, r.gl, r.X),
        WR: weight_last,
        OUTFAR: out_far_next,
        OUTSUM: out_sums,
        GAIN: gain,
    }
    for step in ORDER:
        if step in u:
            u[step].advance()
        else:
            steps[step]()
    while turn[2] <= many:
        gain()
    for one in u.values():
        one.close()
    for copy in stores.values():
        copy.wait()
    out_x.wait_send()
    for copy in to_sib + gather_g + [across_g]:
        copy.wait_send()
    for copy in halves.values():
        copy.wait_send()
    for step in range(many):
        gain_copy(step).wait_send()


def main_call(wide, heads, eps, arrays):
    rows, width = arrays["tokens"].shape
    hidden = arrays["wl"].shape[0]
    half = width // 2
    bits = wide.bit_length() - 1
    tall = tall_of(wide, hidden)
    specs = {"lens": IN_SMEM, "rate_s": IN_SMEM, "rate_row": IN_VMEM, "fgain": IN_VMEM, "again": IN_VMEM}
    ins = {nm: (a, specs.get(nm, ANY)) for nm, a in arrays.items()}
    sds = jax.ShapeDtypeStruct
    outs = {("a", i): sds((width, width), BF16) for i in range(5)}
    outs.update({("f", i): sds((tall, width), BF16) for i in range(3)})
    outs["out"] = sds((rows, width), BF16)
    outs["gtok"] = sds((rows, width), F32)
    outs["out_gain"] = sds((8, width), F32)
    outs.update({nm: sds((rows, width), BF16) for nm in ("n1", "q", "k", "v", "dq", "dk", "gate", "flat", "mixed")})
    outs["ko"] = sds((rows, heads), F32)
    outs["hidden"] = sds((rows, width), F32)
    outs["sin"] = sds((width, width // heads), BF16)
    VM = pltpu.VMEM
    dma = pltpu.SemaphoreType.DMA
    few = ("to_core", "from_core", "own_core", "own_from", "to_x", "from_x")
    few += ("o_sum", "o_x", "o_from_core", "o_own_from", "out_rx", "mix_sib", "n1_sib")
    scratch = {nm: VM((rows, width), BF16) for nm in few}
    scratch.update({nm: VM((rows, width), F32) for nm in ("own", "keep")})
    scratch.update({nm: VM((4 * rows, hidden), BF16) for nm in ("prod", "gl", "gr")})
    scratch.update({nm: VM((4 * rows, width), BF16) for nm in ("X", "G")})
    scratch.update({nm: VM((rows, heads), F32) for nm in ("ko_v", "gate_in", "keep_out")})
    scratch.update({nm: VM((width, width // heads), BF16) for nm in ("sin_v", "state_a", "state_b")})
    scratch.update({nm: VM((wide, width // wide, width // heads), BF16) for nm in ("arrived", "joined")})
    scratch.update(
        wf=VM((3 * hidden, width), BF16),
        p_v=VM((3 * tall, width), BF16),
        sib=VM((5, rows, half), BF16),
        reach=VM((rows, rows), F32),
        gsum=VM((2, 8, width), F32),
        gains=VM((3 + bits, 8, width), F32),
        grecv=VM((2 + bits, 8, width), F32),
        lsem=dma((40,)),
        csem=dma((14,)),
        ssem=dma((8, wide)),
        stsem=dma((16,)),
        xsem=dma((22, PIECES)),
        usem=dma((11, 4 * (bits + 1) + 4)),
        gsem=dma((4 + 2 * bits,)),
        osem=dma((5,)),
    )
    for name in range(D0, V + 1):
        for step, shape in enumerate(arrivals(name, wide, tall if name < O else width, half)):
            scratch["r", name, step] = VM(shape, BF16)
    return call_kernel(lambda r: main_body(wide, heads, eps, r), "whole_block", 3, ins, outs, scratch, 48 * 10**9)


def widen_body(r):
    jobs = []
    for key, src in r.src.items():
        dst, wide_v, narrow_v = r.dst[key], r.wide_v[key], r.narrow_v[key]
        rows = dst.shape[0]
        size = rows // 4 if rows % 64 == 0 else rows
        for base in range(0, rows, size):
            here = pl.ds(base, size)
            jobs.append((src.at[here], narrow_v.at[here], wide_v.at[here], dst.at[here]))
    reads = [pltpu.make_async_copy(job[0], job[1], r.rsem.at[i]) for i, job in enumerate(jobs)]
    writes = [pltpu.make_async_copy(job[2], job[3], r.wsem.at[i]) for i, job in enumerate(jobs)]
    plain_in = [
        pltpu.make_async_copy(r.gtok, r.gtok_v, r.psem.at[4]),
        pltpu.make_async_copy(r.out, r.out_v, r.psem.at[5]),
    ]
    plain = [
        pltpu.make_async_copy(r.gtok_v, r.gtok_out, r.psem.at[0]),
        pltpu.make_async_copy(r.out_v, r.out_out, r.psem.at[1]),
    ]
    for copy in plain_in + reads:
        copy.start()
    for first, second in zip(plain_in, plain, strict=True):
        first.wait()
        second.start()
    for i in range(2):
        r.gain_v[i] = r.gains[i]
    plain += [pltpu.make_async_copy(r.gain_v.at[i], dst, r.psem.at[2 + i]) for i, dst in enumerate((r.gain0, r.gain1))]
    for copy in plain[2:]:
        copy.start()
    for job, read, write in zip(jobs, reads, writes, strict=True):
        read.wait()
        narrow, wide = job[1], job[2]
        tile = math.gcd(narrow.shape[0], 64)

        @pl.loop(0, narrow.shape[0] // tile)
        def _(i):
            wide[part(i, tile), :] = narrow[part(i, tile), :].astype(F32)

        write.start()
    for copy in writes + plain:
        copy.wait()


def widen(done, hidden):
    keys = [key for key in done if isinstance(key, tuple)]
    rows, width = done["out"].shape
    sds = jax.ShapeDtypeStruct
    high = {key: hidden if key[0] == "f" else width for key in keys}
    names, ins, specs = [], [], []
    for key in keys:
        names.append(("s", key))
        ins.append(done[key])
        specs.append(ANY)
    for name, spec in (("gtok", ANY), ("out", ANY), ("gains", IN_VMEM)):
        names.append(name)
        ins.append(done["out_gain"] if name == "gains" else done[name])
        specs.append(spec)
    outs = {("d", key): sds((high[key], width), F32) for key in keys}
    outs["gtok_out"] = sds((rows, width), F32)
    outs["out_out"] = sds((rows, width), BF16)
    outs["gain0"] = sds((width,), F32)
    outs["gain1"] = sds((width,), F32)
    dma = pltpu.SemaphoreType.DMA
    scratch = {("w", key): pltpu.VMEM((high[key], width), F32) for key in keys}
    scratch.update({("n", key): pltpu.VMEM((high[key], width), BF16) for key in keys})
    scratch.update(gain_v=pltpu.VMEM((2, width), F32), rsem=dma((32,)), wsem=dma((32,)), psem=dma((6,)))
    scratch.update(gtok_v=pltpu.VMEM((rows, width), F32), out_v=pltpu.VMEM((rows, width), BF16))
    names += list(outs) + list(scratch)
    results = pl.pallas_call(
        lambda *refs: widen_body(Refs(names, refs)),
        name="widen",
        out_shape=list(outs.values()),
        in_specs=specs,
        out_specs=[ANY] * len(outs),
        scratch_shapes=list(scratch.values()),
        compiler_params=pltpu.CompilerParams(vmem_limit_bytes=VMEM_BYTES),
    )(*ins)
    return dict(zip(outs, results, strict=True))


def body(
    tokens,
    cotangent,
    lengths,
    decay_rate,
    attn_gain,
    w_query,
    w_key,
    w_value,
    w_gate,
    w_out,
    ffn_gain,
    w_left,
    w_right,
    w_down,
):
    wide = lax.axis_size("wide")
    heads = decay_rate.shape[0]
    hidden = w_down.shape[0]
    shared = dict(
        lens=lengths,
        rate_s=decay_rate,
        rate_row=decay_rate[None],
        fgain=ffn_gain[None],
        again=attn_gain[None],
        wq=w_query,
        wk=w_key,
        wv=w_value,
        wg=w_gate,
        wo=w_out,
        tokens=tokens[0],
        cot=cotangent[0],
    )
    gated = dict(wl=w_left.T, wr=w_right.T, wd=w_down)
    done = main_call(wide, heads, EPS, {**shared, **gated})
    last = widen(done, hidden)
    g_o, g_g, g_q, g_k, g_v = [last["d", ("a", i)] for i in range(5)]
    g_d, g_l, g_r = [last["d", ("f", i)] for i in range(3)]
    return (
        last["out_out"][None],
        last["gtok_out"][None],
        g_q,
        g_k,
        g_v,
        g_g,
        g_o,
        last["gain0"],
        last["gain1"],
        g_l.T,
        g_r.T,
        g_d,
    )


def solution(mesh):
    placed = (
        P("narrow", "wide", None),
        P("narrow", "wide", None),
        P("narrow", None),
        P(),
        P(),
        P(),
        P(),
        P(),
        P(),
        P(),
        P(),
        P(None, "narrow"),
        P(None, "narrow"),
        P("narrow", None),
    )
    return jax.shard_map(
        body,
        mesh=mesh,
        in_specs=placed,
        out_specs=(
            P("narrow", "wide", None),
            P("narrow", "wide", None),
            P(),
            P(),
            P(),
            P(),
            P(),
            P(),
            P(),
            P(None, "narrow"),
            P(None, "narrow"),
            P("narrow", None),
        ),
        check_vma=False,
    )
```

```python
import math

import jax
import jax.numpy as jnp
from jax import lax
from jax.experimental import pallas as pl
from jax.experimental.pallas import tpu as pltpu
from jax.sharding import PartitionSpec as P

EPS = 1e-06

MESH = pl.DeviceIdType.MESH
F32 = jnp.float32
BF16 = jnp.bfloat16
VMEM_BYTES = 63 * 1024 * 1024
ANY = pl.BlockSpec(memory_space=pl.ANY)
IN_VMEM = pl.BlockSpec(memory_space=pltpu.VMEM)
IN_SMEM = pl.BlockSpec(memory_space=pltpu.SMEM)


class Refs:
    def __init__(self, names, refs):
        self.recv, self.out_a, self.out_f = {}, {}, {}
        self.src, self.dst, self.wide_v, self.narrow_v = {}, {}, {}, {}
        groups = {"r": self.recv, "a": self.out_a, "f": self.out_f}
        groups.update(s=self.src, d=self.dst, w=self.wide_v, n=self.narrow_v)
        for name, ref in zip(names, refs, strict=True):
            if isinstance(name, str):
                setattr(self, name, ref)
            else:
                groups[name[0]][name[1:] if len(name) > 2 else name[1]] = ref


def call_kernel(body, name, number, ins, outs, scratch, cost):
    names = list(ins) + list(outs) + list(scratch)

    def kernel(*refs):
        body(Refs(names, refs))

    results = pl.pallas_call(
        kernel,
        name=name,
        out_shape=list(outs.values()),
        in_specs=[spec for _, spec in ins.values()],
        out_specs=[ANY] * len(outs),
        scratch_shapes=list(scratch.values()),
        cost_estimate=pl.CostEstimate(flops=cost, bytes_accessed=cost // 500, transcendentals=0),
        compiler_params=pltpu.CompilerParams(
            collective_id=number, has_side_effects=True, vmem_limit_bytes=VMEM_BYTES
        ),
    )(*[array for array, _ in ins.values()])
    return dict(zip(outs, results, strict=True))


def nn(left, right):
    return lax.dot_general(left, right, (((1,), (0,)), ((), ())), preferred_element_type=F32)


def nt(left, right):
    return lax.dot_general(left, right, (((1,), (1,)), ((), ())), preferred_element_type=F32)


def tn(left, right):
    return lax.dot_general(left, right, (((0,), (0,)), ((), ())), preferred_element_type=F32)


def part(index, size):
    return pl.ds(pl.multiple_of(index * size, size), size)


def round_up(number, step):
    return -(-number // step) * step


class Place:
    def __init__(self, wide):
        self.wide = wide
        self.w = lax.axis_index("wide")
        self.n = lax.axis_index("narrow")
        self.core = lax.rem(self.n, 2)
        self.xh = lax.div(self.n, 2)
        self.flip_core = (self.w, self.n + 1 - 2 * self.core)
        self.flip_x = (self.w, self.n + 2 - 4 * self.xh)
        self.bits = tuple(range(wide.bit_length() - 1))

    def bit(self, dim):
        return self.xh if dim == X else lax.rem(lax.div(self.w, 2**dim), 2)

    def partner(self, dim):
        if dim == X:
            return self.flip_x
        return (self.w + (1 - 2 * self.bit(dim)) * 2**dim, self.n)

    def on_wide(self, w):
        return (w, self.n)


def greet(partners, place, whole_wide):
    barrier = pltpu.get_barrier_semaphore()
    for partner in partners:
        pl.semaphore_signal(barrier, inc=1, device_id=partner, device_id_type=MESH)
    count = len(partners)
    if whole_wide:

        def one(step, carry):
            pl.semaphore_signal(
                barrier,
                inc=1,
                device_id=place.on_wide(lax.rem(place.w + step, place.wide)),
                device_id_type=MESH,
            )
            return carry

        lax.fori_loop(1, place.wide, one, 0)
        count += place.wide - 1
    pl.semaphore_wait(barrier, count)


def remote(src, dst, send, recv, device):
    return pltpu.make_async_remote_copy(
        src_ref=src, dst_ref=dst, send_sem=send, recv_sem=recv, device_id=device, device_id_type=MESH
    )


def segment_ends(lens):
    ends = []
    total = jnp.int32(0)
    for slot in range(lens.shape[1]):
        total = total + lens[0, slot]
        ends.append(total)
    return ends


def count_ends(ends, spots):
    total = jnp.zeros_like(spots)
    for end in ends:
        total = total + jnp.where(spots >= end, 1, 0)
    return total


def segment_setup(place, ends, rate_row, rows, gate_ref, keep_ref, reach_ref, later_first):
    anchor = place.w * rows
    col_local = lax.broadcasted_iota(jnp.int32, (rows, 1), 0)
    row_local = lax.broadcasted_iota(jnp.int32, (1, rows), 1)
    col_seg = count_ends(ends, col_local + anchor)
    row_seg = count_ends(ends, row_local + anchor)
    before = jnp.int32(0)
    last = jnp.int32(0)
    for end in ends:
        before = before + jnp.where(anchor - 1 >= end, 1, 0)
        last = last + jnp.where(anchor + rows - 1 >= end, 1, 0)
    before = jnp.where(place.w > 0, before, -1)
    col_live = (col_local + anchor) < ends[-1]
    row_live = (row_local + anchor) < ends[-1]
    rates = rate_row[...]
    steps = col_local.astype(F32)
    gate_ref[...] = jnp.exp(-(steps + 1.0) * rates) * jnp.where(
        (col_seg == before) & col_live, 1.0, 0.0
    )
    keep_ref[...] = jnp.exp(-(rows - 1.0 - steps) * rates) * jnp.where(
        (col_seg == last) & col_live, 1.0, 0.0
    )
    gap = col_local - row_local if later_first else row_local - col_local
    reaches = (gap >= 0) & (col_seg == row_seg) & row_live & col_live
    reach_ref[...] = jnp.where(reaches, gap.astype(F32), -1.0)


def decay_of(reach, rate):
    return jnp.where(reach >= 0.0, jnp.exp(-rate * reach), 0.0)


def scatter_states(place, local, arrived, sends, recvs, chunk):
    def one(step, carry):
        target = lax.rem(place.w + step, place.wide)
        remote(
            local.at[part(target, chunk)],
            arrived.at[place.w],
            sends.at[target],
            recvs.at[place.w],
            place.on_wide(target),
        ).start()
        return carry

    lax.fori_loop(1, place.wide, one, 0)
    arrived[place.w] = local[part(place.w, chunk), :]


def wait_states(place, local, arrived, sends, recvs, chunk):
    def one(step, carry):
        source = lax.rem(place.w + step, place.wide)
        copy = remote(
            local.at[part(source, chunk)],
            arrived.at[source],
            sends.at[source],
            recvs.at[source],
            place.on_wide(source),
        )
        copy.wait_recv()
        copy.wait_send()
        return carry

    lax.fori_loop(1, place.wide, one, 0)


def join_states(place, ends, rate, rows, arrived, joined, backward):
    shape = arrived.shape[1:]
    fade = jnp.exp(jnp.full((1, shape[1]), -1.0 * rows, F32) * rate)

    def one(step, state):
        block = place.wide - 1 - step if backward else step
        joined[block] = state.astype(BF16)
        cuts = jnp.int32(0)
        for end in ends:
            inside = (end >= block * rows) & (end <= block * rows + rows - 1)
            cuts = cuts + jnp.where(inside, 1, 0)
        flag = jnp.where((cuts == 0) & (block > 0), 1.0, 0.0)
        return (fade * flag) * state + arrived[block].astype(F32)

    lax.fori_loop(0, place.wide, one, jnp.zeros(shape, F32))


def return_states(place, joined, entering, sends, recvs, chunk):
    def one(step, carry):
        target = lax.rem(place.w + step, place.wide)
        remote(
            joined.at[target],
            entering.at[part(place.w, chunk)],
            sends.at[target],
            recvs.at[place.w],
            place.on_wide(target),
        ).start()
        return carry

    lax.fori_loop(1, place.wide, one, 0)
    entering[part(place.w, chunk), :] = joined[place.w]


def wait_returned(place, joined, entering, sends, recvs, chunk):
    def one(step, carry):
        source = lax.rem(place.w + step, place.wide)
        copy = remote(
            joined.at[source],
            entering.at[part(source, chunk)],
            sends.at[source],
            recvs.at[source],
            place.on_wide(source),
        )
        copy.wait_recv()
        copy.wait_send()
        return carry

    lax.fori_loop(1, place.wide, one, 0)


class Unit:
    def __init__(self, place, dims, acc, out, shift, recvs, sems, is_core, by_columns, first=0):
        self.place, self.dims, self.acc, self.out, self.shift = place, dims, acc, out, shift
        self.recvs, self.sems, self.is_core = recvs, sems, is_core
        self.first, self.stage = first, None
        self.count = 2 * len(dims) + is_core
        self.keep, self.give = [], []
        (rows, cols), row, col = acc.shape, 0, 0
        self.whole = (row, rows, col, cols)
        for dim in dims:
            bit = place.bit(dim)
            if dim == by_columns:
                cols //= 2
                self.keep.append((row, rows, col + bit * cols, cols))
                self.give.append((row, rows, col + (1 - bit) * cols, cols))
            else:
                rows //= 2
                self.keep.append((row + bit * rows, rows, col, cols))
                self.give.append((row + (1 - bit) * rows, rows, col, cols))
            row, rows, col, cols = self.keep[-1]

    def at(self, ref, region, shift=0):
        row, rows, col, cols = region
        down = pl.ds(pl.multiple_of(row, rows), rows)
        return ref.at[down, pl.ds(pl.multiple_of(col + shift, cols), cols)]

    def copy(self, stage):
        many = len(self.dims)
        send, recv = self.sems.at[2 * stage], self.sems.at[2 * stage + 1]
        if stage < many:
            src = self.at(self.acc, self.give[stage])
            return remote(src, self.recvs[stage], send, recv, self.place.partner(self.dims[stage]))
        if stage == 2 * many:
            region = self.at(self.out, self.whole, self.shift)
            return remote(region, region, send, recv, self.place.flip_core)
        step = 2 * many - 1 - stage
        dst = self.at(self.out, self.keep[step], self.shift)
        src = self.at(self.acc, self.keep[step]) if stage == many else dst
        return remote(src, dst, send, recv, self.place.partner(self.dims[step]))

    def local(self):
        return pltpu.make_async_copy(
            self.at(self.acc, self.keep[-1]),
            self.at(self.out, self.keep[-1], self.shift),
            self.sems.at[2 * self.count],
        )

    def take(self, stage):
        many = len(self.dims)
        self.copy(stage).wait_recv()
        if stage < many:
            row, rows, col, cols = self.keep[stage]
            add_into(self.acc, row, pl.ds(pl.multiple_of(col, cols), cols), self.recvs[stage])
        elif stage == many:
            self.local().wait()

    def advance(self):
        if self.stage is None:
            self.stage = self.first
        elif self.stage < self.count:
            self.take(self.stage)
            self.stage += 1
        if self.stage < self.count:
            self.copy(self.stage).start()
            if self.stage == len(self.dims):
                self.local().start()

    def close(self):
        while self.stage < self.count:
            self.advance()
        for stage in range(self.first, self.count):
            self.copy(stage).wait_send()


def add_into(acc, base, cols, other):
    rows = other.shape[0]
    tile = math.gcd(rows, 128)

    @pl.loop(0, rows // tile)
    def _(i):
        here = pl.ds(pl.multiple_of(base + i * tile, tile), tile)
        acc[here, cols] = acc[here, cols] + other[part(i, tile), :]


PIECES = 4


Y, A, B, X = 0, 1, 2, 9
D0, D1, L0, L1, R0, R1, O, G, Q, K, V = range(11)
S1, S2, S3, S5, S6, WO, WG, WQ, WK, WV, INSIDE, JOIN, OUT, OUTX, GAIN, WD, WL, WR, OUTFAR, OUTSUM = range(20, 40)
DIMS = {
    D0: (Y, B, A),
    D1: (A, Y, B),
    L0: (A, Y, B),
    L1: (Y, A, B),
    R0: (Y, A, B),
    R1: (Y, A, B),
    O: (X, Y, A, B),
    G: (X, A, Y, B),
    Q: (X, Y, A, B),
    K: (Y, X, A, B),
    V: (X, Y, A, B),
}
ORDER = (
    WD, D0, D1, OUTFAR, OUTFAR, OUTFAR, OUTSUM, WL, L0, L1, WR, D0, R0, S1, S2, S3, WO, WG, D0, R1, INSIDE,
    INSIDE, L1, INSIDE, INSIDE, D0, JOIN, INSIDE, INSIDE, INSIDE, INSIDE, WQ, D0, O, R1, S5, WK, R0, WV, R1,
    O, S6, G, D0, S6, GAIN, R1, O, Q, G, R0, GAIN, R1, O, D0, K, R0, GAIN, R1, Q, O, OUTX, G, GAIN, K, V, Q,
    O, G, GAIN, R1, R0, K, G, Q, GAIN, V, K, L0, O, Q, V, G, R0, OUT, V, Q, K, G, R0, L0, V, O, D1, L1, O, V,
    L0, K, D1, G, Q, L0, L1, G, K, D1, L0, V, L1, D1, Q, L0, K, Q, L1, D1, K, V, V, L1, D1,
)


def tall_of(wide, hidden):
    return (wide // 2) * round_up(-(-hidden // (wide // 2)), 16)


def dims_of(name, wide):
    return DIMS[name] + tuple(range(3, wide.bit_length() - 1))


def arrivals(name, wide, rows, cols):
    shapes = []
    for dim in dims_of(name, wide):
        if name < O and dim == Y:
            cols //= 2
        else:
            rows //= 2
        shapes.append((rows, cols))
    return shapes


def main_body(wide, heads, eps, r):
    p = Place(wide)
    rows, width = r.tokens.shape
    hidden = r.wl.shape[0]
    tall = tall_of(wide, hidden)
    size = rows // PIECES
    group = 256
    head = width // heads
    half = width // 2
    tile = 128
    chunk = width // wide
    mine = part(p.core, half)
    turn = [0, 0, 0, 1]
    theirs = part(1 - p.core, half)

    greet([p.flip_core, p.flip_x], p, True)

    def rows_of(ref, i):
        return ref.at[pl.ds(i * rows, rows)]

    wl_v, wr_v, wd_v = [r.wf.at[pl.ds(i * hidden, hidden)] for i in range(3)]
    wa, wc = r.wf.at[pl.ds(0, width)], r.wf.at[pl.ds(width, width)]
    wv_v, wg_v = r.X.at[pl.ds(0, width)], r.X.at[pl.ds(width, width)]
    q_v, k_v, v_v, dq_v = [rows_of(r.X, i) for i in range(4)]
    cot_v, dk_v, mix_v, n1_v = [rows_of(r.G, i) for i in range(4)]
    flat_v, gate_v, gb, gg, ga_v, gq_v = r.to_core, r.own_core, r.from_core, r.to_x, r.own_from, r.from_x
    gn2_v, hid_v, out_v, gv_v = r.own, r.keep, dk_v, r.o_own_from
    accs = [
        buf.at[pl.ds((i % 2) * width, width), pl.ds(0, half)]
        for i, buf in enumerate((r.gl, r.gl, r.gr, r.gr, r.prod))
    ]

    u = {}
    for name in range(D0, V + 1):
        first = 0
        recvs = [r.recv.get((name, step)) for step in range(len(dims_of(name, wide)))]
        if name < O:
            which, cut = divmod(name - D0, 2)
            acc, out, shift = r.p_v.at[pl.ds(which * tall, tall), pl.ds(cut * half, half)], r.out_f[which], cut * half
        else:
            acc, out, shift = accs[name - O], r.out_a[name - O], p.core * half
        u[name] = Unit(
            p,
            dims_of(name, wide),
            acc,
            out,
            shift,
            recvs,
            r.usem.at[name - D0],
            name >= O,
            Y if name < O else None,
            first,
        )

    loads, landed = {}, set()

    def load(key, src, dst):
        loads[key] = pltpu.make_async_copy(src, dst, r.lsem.at[len(loads)])
        loads[key].start()

    def need(*keys):
        for key in keys:
            if key not in landed:
                loads[key].wait()
                landed.add(key)

    def spot(c, second):
        return pl.ds(2 * rows + (2 * c + second) * size, size)

    def remotes(row, src_of, dst_of, device):
        return [
            remote(src_of(c), dst_of(c), r.xsem.at[row, c], r.xsem.at[row + 1, c], device)
            for c in range(PIECES)
        ]

    def piece(ref):
        return lambda c: ref.at[pl.ds(c * size, size)]

    gather = remotes(0, piece(r.X), lambda c: r.X.at[spot(c, 0)], p.flip_x)
    onward = remotes(2, lambda c: r.X.at[spot(c, 0)], lambda c: r.X.at[spot(c, 1)], p.flip_core)
    across = remote(r.X.at[pl.ds(0, rows)], r.X.at[pl.ds(rows, rows)], r.xsem.at[16, 0], r.xsem.at[16, 1], p.flip_core)
    back_core = remotes(4, piece(r.to_core), piece(r.from_core), p.flip_core)
    back_own = remotes(6, piece(r.own_core), piece(r.own_from), p.flip_core)
    back_x = remotes(8, piece(r.to_x), piece(r.from_x), p.flip_x)
    out_core = remotes(10, piece(r.to_core), piece(r.o_from_core), p.flip_core)
    out_own = remotes(12, piece(r.own_core), piece(r.o_own_from), p.flip_core)

    tok_a, n1_a, q_a, k_a, v_a = r.to_core, r.from_core, r.own_core, r.own_from, r.to_x
    dq_a, dk_a, gate_a, flat_a, mix_a = r.from_x, r.o_sum, r.o_x, r.o_from_core, r.o_own_from
    raw_f, hid_a, n2_a = r.own, r.keep, r.X.at[pl.ds(0, rows)]
    wk_a, wv_a = r.wf.at[pl.ds(0, width)], r.wf.at[pl.ds(width, width)]
    wq_a, wg_a = r.p_v.at[pl.ds(0, width)], r.p_v.at[pl.ds(width, width)]
    gather_g = remotes(18, piece(r.cot), lambda c: r.G.at[spot(c, 0)], p.flip_x)
    onward_g = remotes(20, lambda c: r.G.at[spot(c, 0)], lambda c: r.G.at[spot(c, 1)], p.flip_core)
    across_g = remote(r.cot, r.G.at[pl.ds(rows, rows)], r.xsem.at[17, 0], r.xsem.at[17, 1], p.flip_core)
    for copy in gather_g:
        copy.start()
    load("a_tokens", r.tokens, tok_a)
    load("a_wk", r.wk, wk_a)
    load("a_wv", r.wv, wv_a)
    load("a_wq", r.wq, wq_a)
    load("a_wg", r.wg, wg_a)
    load("g", r.cot, r.G.at[pl.ds(0, rows)])
    across_g.start()
    ends = segment_ends(r.lens)
    stores_a = []

    def store(src, dst):
        copy = pltpu.make_async_copy(src, dst, r.stsem.at[len(stores_a)])
        copy.start()
        stores_a.append(copy)

    def pass_on(c):
        gather_g[c].wait_recv()
        onward_g[c].start()

    segment_setup(p, ends, r.rate_row, rows, r.gate_in, r.keep_out, r.reach, True)
    need("a_tokens")

    @pl.loop(0, rows // tile)
    def _(i):
        here = part(i, tile)
        tok = tok_a[here, :].astype(F32)
        scale = lax.rsqrt(jnp.mean(tok * tok, axis=-1, keepdims=True) + eps)
        n1_a[here, :] = (tok * scale * r.again[...]).astype(BF16)

    store(n1_a, r.n1)

    def silu_rows(weight, act, slope):
        @pl.loop(0, rows // 256)
        def _(i):
            here = part(i, 256)
            pre = nn(n1_a[here, :], weight[...])
            gate = lax.logistic(pre)
            act[here, :] = (pre * gate).astype(BF16)
            slope[here, :] = (gate * (1.0 + pre * (1.0 - gate))).astype(BF16)

    def plain_rows(weight, dst):
        @pl.loop(0, rows // 256)
        def _(i):
            here = part(i, 256)
            dst[here, :] = nn(n1_a[here, :], weight[...]).astype(BF16)

    need("a_wk")
    silu_rows(wk_a, k_a, dk_a)
    need("a_wv")
    plain_rows(wv_a, v_a)
    load("wl", r.wl, wl_v)
    load("wr", r.wr, wr_v)
    load("wd", r.wd, wd_v)
    for h in range(heads):
        cols = slice(h * head, (h + 1) * head)
        kept = (k_a[:, cols].astype(F32) * r.keep_out[:, h : h + 1]).astype(BF16)
        r.state_a[pl.ds(h * head, head), :] = tn(kept, v_a[:, cols]).astype(BF16)
    scatter_states(p, r.state_a, r.arrived, r.ssem.at[4], r.ssem.at[5], chunk)
    store(k_a, r.k)
    store(dk_a, r.dk)
    store(v_a, r.v)
    need("a_wq")
    silu_rows(wq_a, q_a, dq_a)
    load("a_wo", r.wo, wq_a)
    store(q_a, r.q)
    store(dq_a, r.dq)

    def inside_forward(h, carry):
        cols = part(h, head)
        weight = decay_of(r.reach[...], r.rate_s[h])
        probs = (nt(q_a[:, cols], k_a[:, cols]) * weight).astype(BF16)
        raw_f[:, cols] = nn(probs, v_a[:, cols])
        return carry

    lax.fori_loop(0, heads // 2, inside_forward, 0)
    pass_on(0)
    wait_states(p, r.state_a, r.arrived, r.ssem.at[4], r.ssem.at[5], chunk)
    join_states(p, ends, r.rate_s[lax.div(p.w * chunk, head)], rows, r.arrived, r.joined, False)
    return_states(p, r.joined, r.state_b, r.ssem.at[6], r.ssem.at[7], chunk)
    need("a_wg")
    plain_rows(wg_a, gate_a)
    store(gate_a, r.gate)
    lax.fori_loop(heads // 2, heads, inside_forward, 0)
    pass_on(1)
    wait_returned(p, r.joined, r.state_b, r.ssem.at[6], r.ssem.at[7], chunk)
    store(r.state_b, r.sin)
    for h in range(heads):
        cols = slice(h * head, (h + 1) * head)
        state = r.state_b[pl.ds(h * head, head), :]
        raw = raw_f[:, cols] + nn(q_a[:, cols], state) * r.gate_in[:, h : h + 1]
        scale = lax.rsqrt(jnp.mean(raw * raw, axis=-1, keepdims=True) + eps)
        unit = raw * scale
        r.ko_v[:, h : h + 1] = scale
        flat_a[:, cols] = unit.astype(BF16)
        mix_a[:, cols] = (unit * gate_a[:, cols].astype(F32)).astype(BF16)
    for copy in stores_a:
        copy.wait()
    late = len(stores_a)
    store(r.ko_v, r.ko)
    store(flat_a, r.flat)
    store(mix_a, r.mixed)
    need("a_wo")

    for i in range(rows // group):
        here = pl.ds(i * group, group)
        hid = tok_a[here, :].astype(F32) + nn(mix_a[here, :], wq_a[...])
        scale = lax.rsqrt(jnp.mean(hid * hid, axis=-1, keepdims=True) + eps)
        hid_a[here, :] = hid
        n2_a[here, :] = (hid * scale * r.fgain[...]).astype(BF16)
        for c in range(i * group // size, (i + 1) * group // size):
            gather[c].start()

    store(hid_a, r.hidden)
    for copy in stores_a[late:]:
        copy.wait()
    across.start()
    for c in range(2, PIECES):
        pass_on(c)

    def act(here):
        x = r.X[here, :]
        left = nt(x, wl_v[...])
        right = nt(x, wr_v[...])
        r.prod[here, :] = (left * right).astype(BF16)
        up = nt(r.G[here, :], wd_v[...])
        r.gl[here, :] = (up * right).astype(BF16)
        r.gr[here, :] = (up * left).astype(BF16)
        return nn(r.gl[here, :], wl_v[...]) + nn(r.gr[here, :], wr_v[...])

    def out_part(here):
        return nn(r.prod[here, :], wd_v[...])

    need("wl", "wr", "wd", "g")

    @pl.loop(0, rows // group)
    def _(i):
        r.own[part(i, group), :] = act(part(i, group))

    across.wait_recv()
    across_g.wait_recv()

    @pl.loop(0, rows // group)
    def _(i):
        r.own_core[part(i, group), :] = act(pl.ds(pl.multiple_of(rows + i * group, group), group)).astype(BF16)

    for copy in back_own:
        copy.start()
    gather[0].wait_recv()
    onward[0].start()

    def out_own_rows(i):
        r.o_sum[part(i, group), :] = out_part(part(i, group)).astype(BF16)

    def out_core_rows(i):
        if i == 0:
            for copy in back_own:
                copy.wait_send()
        r.own_core[part(i, group), :] = out_part(pl.ds(rows + i * group, group)).astype(BF16)

    def far(c):
        here = pl.ds(2 * rows + 2 * c * size, 2 * size)
        got = act(here)
        r.keep[pl.ds(c * size, size), :] = got[:size]
        r.to_core[pl.ds(c * size, size), :] = got[size:].astype(BF16)
        back_core[c].start()

    def far_send(c):
        back_core[c].wait_recv()
        here = pl.ds(c * size, size)
        r.to_x[here, :] = (r.keep[here, :] + r.from_core[here, :].astype(F32)).astype(BF16)
        back_x[c].start()

    fill = [
        lambda: out_own_rows(0),
        lambda: out_own_rows(1),
        lambda: out_core_rows(0),
        lambda: out_core_rows(1),
    ]
    for c in range(PIECES):
        fill[c]()
        onward[c].wait_recv()
        onward_g[c].wait_recv()
        far(c)
        if c + 1 < PIECES:
            if c:
                far_send(c - 1)
            gather[c + 1].wait_recv()
            onward[c + 1].start()
    for copy in out_own:
        copy.start()
    far_send(PIECES - 2)

    def out_far(c):
        got = out_part(pl.ds(2 * rows + 2 * c * size, 2 * size)).astype(BF16)
        here = pl.ds(c * size, size)
        r.o_x[here, :] = got[:size]
        back_core[c].wait_send()
        r.to_core[here, :] = got[size:]
        out_core[c].start()

    out_far(0)
    far_send(PIECES - 1)
    load("hidden", r.hidden, hid_v)
    load("wo", r.wo, wa)
    load("ko", r.ko, r.ko_v)
    load("sin", r.sin, r.sin_v)
    out_x = remote(r.o_x, r.out_rx, r.osem.at[2], r.osem.at[3], p.flip_x)
    to_sib = [
        remote(r.mixed, r.mix_sib, r.csem.at[0], r.csem.at[1], p.flip_core),
        remote(r.n1, r.n1_sib, r.csem.at[2], r.csem.at[3], p.flip_core),
    ]
    for copy in to_sib:
        copy.start()

    def out_far_next():
        out_far(turn[3])
        turn[3] += 1

    def out_sums():
        for c in range(PIECES):
            out_core[c].wait_recv()
            out_own[c].wait_recv()
            here = pl.ds(c * size, size)
            r.o_x[here, :] = r.o_x[here, :] + r.o_from_core[here, :]
            r.o_sum[here, :] = r.o_sum[here, :] + r.o_own_from[here, :]
        for copy in out_core + out_own:
            copy.wait_send()
        load("flat", r.flat, flat_v)
        load("gate", r.gate, gate_v)
        load("wk", r.wk, wc)

    def weight(which, left, right):
        cut = 384 if hidden > 384 else hidden
        for base, extent in ((0, cut), (cut, hidden - cut)):
            if extent:
                here = pl.ds(base, extent)
                r.p_v[pl.ds(which * tall + base, extent), :] = tn(left[:, here], right[...]).astype(BF16)

    def weight_last():
        weight(2, r.gr, r.X)
        for copy in onward + onward_g + gather + [across]:
            copy.wait_send()
        load("q", r.q, q_v)
        load("mixed", r.mixed, mix_v)
        load("n1", r.n1, n1_v)
        load("k", r.k, k_v)
        load("v", r.v, v_v)
        load("dq", r.dq, dq_v)
        load("dk", r.dk, dk_v)

    halves = {}

    def send_half(key, src):
        slot = key - O
        halves[key] = remote(
            src.at[:, theirs], r.sib.at[slot], r.csem.at[4 + 2 * slot], r.csem.at[5 + 2 * slot], p.flip_core
        )
        halves[key].start()

    def fold(x):
        return jnp.sum(x.reshape(x.shape[0] // 8, 8, x.shape[1]), axis=0)

    def second_norm():
        r.gsum[...] = jnp.zeros_like(r.gsum)
        for c in range(PIECES):
            back_own[c].wait_recv()
            back_x[c].wait_recv()
        need("hidden")

        @pl.loop(0, rows // tile)
        def _(i):
            here = part(i, tile)
            hid = hid_v[here, :]
            scale = lax.rsqrt(jnp.mean(hid * hid, axis=-1, keepdims=True) + eps)
            unit = hid * scale
            up = gn2_v[here, :] + r.own_from[here, :].astype(F32) + r.from_x[here, :].astype(F32)
            r.gsum[1] += fold(up * unit)
            up = up * r.fgain[...]
            down = scale * (up - unit * jnp.mean(up * unit, axis=-1, keepdims=True))
            down = down + cot_v[here, :].astype(F32)
            hid_v[here, :] = down
            gb[here, :] = down.astype(BF16)

        load("tok", r.tokens, cot_v)
        send_half(O, gb)

    def gates():
        for copy in back_x:
            copy.wait_send()
        need("wo", "flat", "gate", "ko")

        @pl.loop(0, rows // 256)
        def _(i):
            here = part(i, 256)
            gm = nt(gb[here, :], wa[...])
            flat = flat_v[here, :].astype(F32)
            gg[here, :] = (gm * flat).astype(BF16)
            gm = gm * gate_v[here, :].astype(F32)
            ko = r.ko_v[here, :]
            for h in range(heads):
                cols = slice(h * head, (h + 1) * head)
                up, unit = gm[:, cols], flat[:, cols]
                mean = jnp.mean(up * unit, axis=-1, keepdims=True)
                ga_v[here, cols] = (ko[:, h : h + 1] * (up - unit * mean)).astype(BF16)

        send_half(G, gg)
        load("wq", r.wq, wa)

    def states():
        segment_setup(p, ends, r.rate_row, rows, r.gate_in, r.keep_out, r.reach, False)
        need("q")
        for h in range(heads):
            cols = slice(h * head, (h + 1) * head)
            gated = (q_v[:, cols].astype(F32) * r.gate_in[:, h : h + 1]).astype(BF16)
            r.state_a[pl.ds(h * head, head), :] = tn(gated, ga_v[:, cols]).astype(BF16)
        scatter_states(p, r.state_a, r.arrived, r.ssem.at[0], r.ssem.at[1], chunk)

    def weight_unit(name, left, own):
        acc = accs[name - O]
        other = r.sib.at[name - O]
        halves[name].wait_recv()

        @pl.loop(0, width // 512)
        def _(i):
            here = part(i, 512)
            acc[here, :] = (
                tn(left[0][:, here], own[:, mine]) + tn(left[1][:, here], other[...])
            ).astype(BF16)

        u[name].advance()

    def weight_o():
        need("mixed")
        to_sib[0].wait_recv()
        weight_unit(O, (mix_v, r.mix_sib), gb)

    def weight_g():
        need("n1")
        to_sib[1].wait_recv()
        weight_unit(G, (n1_v, r.n1_sib), gg)


    def inside():
        need("k", "v", "sin", "dq", "dk")
        first = turn[0]
        turn[0] += heads // 8

        def one(h, carry):
            cols = part(h, head)
            q, k, v, ga = q_v[:, cols], k_v[:, cols], v_v[:, cols], ga_v[:, cols]
            weight = decay_of(r.reach[...], r.rate_s[h])
            probs = (nt(k, q) * weight).astype(BF16)
            gv_v[:, cols] = nn(probs, ga).astype(BF16)
            scores = (nt(v, ga) * weight).astype(BF16)
            gn2_v[:, cols] = nn(scores, q)
            pick = lax.broadcasted_iota(jnp.int32, (1, heads), 1) == h
            gate = jnp.sum(jnp.where(pick, r.gate_in[...], 0.0), axis=1, keepdims=True)
            gq = tn(scores, k) + nt(ga, r.sin_v[cols, :]) * gate
            gq_v[:, cols] = (gq * dq_v[:, cols].astype(F32)).astype(BF16)
            return carry

        lax.fori_loop(first, turn[0], one, 0)
        if turn[0] == heads:
            send_half(Q, gq_v)

    def join():
        wait_states(p, r.state_a, r.arrived, r.ssem.at[0], r.ssem.at[1], chunk)
        rate = r.rate_s[lax.div(p.w * chunk, head)]
        join_states(p, ends, rate, rows, r.arrived, r.joined, True)
        return_states(p, r.joined, r.state_b, r.ssem.at[2], r.ssem.at[3], chunk)

    def with_states():
        wait_returned(p, r.joined, r.state_b, r.ssem.at[2], r.ssem.at[3], chunk)
        for h in range(heads):
            cols = slice(h * head, (h + 1) * head)
            state = r.state_b[pl.ds(h * head, head), :]
            keep = r.keep_out[:, h : h + 1]
            gk = gn2_v[:, cols] + nt(v_v[:, cols], state) * keep
            flat_v[:, cols] = (gk * dk_v[:, cols].astype(F32)).astype(BF16)
            gv = gv_v[:, cols].astype(F32) + nn(k_v[:, cols], state) * keep
            gate_v[:, cols] = gv.astype(BF16)
        send_half(K, flat_v)
        send_half(V, gate_v)
        load("hidden_again", r.hidden, gn2_v)
        load("wv", r.wv, wv_v)
        load("wg", r.wg, wg_v)

    def first_norm():
        need("wq", "wk", "wv", "wg", "tok")
        size = rows // 2
        here = pl.ds(turn[1] * size, size)
        turn[1] += 1
        up = (
            nt(gq_v[here, :], wa[...])
            + nt(flat_v[here, :], wc[...])
            + nt(gate_v[here, :], wv_v[...])
            + nt(gg[here, :], wg_v[...])
        )
        tok = cot_v[here, :].astype(F32)
        scale = lax.rsqrt(jnp.mean(tok * tok, axis=-1, keepdims=True) + eps)
        unit = tok * scale
        r.gsum[0] += fold(up * unit)
        up = up * r.again[...]
        down = scale * (up - unit * jnp.mean(up * unit, axis=-1, keepdims=True))
        hid_v[here, :] += down
        if turn[1] == 2:
            stores["gtok"].start()
            r.gains[0] = jnp.zeros_like(r.gains[0])
            for row in range(2):
                r.gains[0, pl.ds(row, 1), :] = jnp.sum(r.gsum[row], axis=0, keepdims=True)

    stores = {
        "gtok": pltpu.make_async_copy(hid_v, r.gtok, r.osem.at[0]),
        "gain": pltpu.make_async_copy(r.gains.at[2 + len(p.bits)], r.out_gain, r.osem.at[1]),
        "out": pltpu.make_async_copy(out_v, r.out, r.osem.at[4]),
    }

    def output():
        out_x.wait_recv()
        need("hidden_again")

        @pl.loop(0, rows // tile)
        def _(i):
            here = part(i, tile)
            total = r.o_sum[here, :].astype(F32) + r.out_rx[here, :].astype(F32)
            out_v[here, :] = (gn2_v[here, :] + total).astype(BF16)

        stores["out"].start()

    gain_to = [p.flip_core, p.flip_x] + [p.partner(bit) for bit in p.bits]
    many = len(gain_to)

    def gain_copy(step):
        return remote(
            r.gains.at[step], r.grecv.at[step], r.gsem.at[2 * step], r.gsem.at[2 * step + 1], gain_to[step]
        )

    def gain():
        step = turn[2]
        turn[2] += 1
        if step:
            gain_copy(step - 1).wait_recv()
            r.gains[step] = r.gains[step - 1] + r.grecv[step - 1]
        if step < many:
            gain_copy(step).start()
        else:
            stores["gain"].start()

    steps = {
        S1: second_norm,
        S2: gates,
        S3: states,
        WO: weight_o,
        WG: weight_g,
        WQ: lambda: weight_unit(Q, (n1_v, r.n1_sib), gq_v),
        WK: lambda: weight_unit(K, (n1_v, r.n1_sib), flat_v),
        WV: lambda: weight_unit(V, (n1_v, r.n1_sib), gate_v),
        INSIDE: inside,
        JOIN: join,
        S5: with_states,
        S6: first_norm,
        OUT: output,
        OUTX: out_x.start,
        WD: lambda: weight(0, r.prod, r.G),
        WL: lambda: weight(1, r.gl, r.X),
        WR: weight_last,
        OUTFAR: out_far_next,
        OUTSUM: out_sums,
        GAIN: gain,
    }
    for step in ORDER:
        if step in u:
            u[step].advance()
        else:
            steps[step]()
    while turn[2] <= many:
        gain()
    for one in u.values():
        one.close()
    for copy in stores.values():
        copy.wait()
    out_x.wait_send()
    for copy in to_sib + gather_g + [across_g]:
        copy.wait_send()
    for copy in halves.values():
        copy.wait_send()
    for step in range(many):
        gain_copy(step).wait_send()


def main_call(wide, heads, eps, arrays):
    rows, width = arrays["tokens"].shape
    hidden = arrays["wl"].shape[0]
    half = width // 2
    bits = wide.bit_length() - 1
    tall = tall_of(wide, hidden)
    specs = {"lens": IN_SMEM, "rate_s": IN_SMEM, "rate_row": IN_VMEM, "fgain": IN_VMEM, "again": IN_VMEM}
    ins = {nm: (a, specs.get(nm, ANY)) for nm, a in arrays.items()}
    sds = jax.ShapeDtypeStruct
    outs = {("a", i): sds((width, width), BF16) for i in range(5)}
    outs.update({("f", i): sds((tall, width), BF16) for i in range(3)})
    outs["out"] = sds((rows, width), BF16)
    outs["gtok"] = sds((rows, width), F32)
    outs["out_gain"] = sds((8, width), F32)
    outs.update({nm: sds((rows, width), BF16) for nm in ("n1", "q", "k", "v", "dq", "dk", "gate", "flat", "mixed")})
    outs["ko"] = sds((rows, heads), F32)
    outs["hidden"] = sds((rows, width), F32)
    outs["sin"] = sds((width, width // heads), BF16)
    VM = pltpu.VMEM
    dma = pltpu.SemaphoreType.DMA
    few = ("to_core", "from_core", "own_core", "own_from", "to_x", "from_x")
    few += ("o_sum", "o_x", "o_from_core", "o_own_from", "out_rx", "mix_sib", "n1_sib")
    scratch = {nm: VM((rows, width), BF16) for nm in few}
    scratch.update({nm: VM((rows, width), F32) for nm in ("own", "keep")})
    scratch.update({nm: VM((4 * rows, hidden), BF16) for nm in ("prod", "gl", "gr")})
    scratch.update({nm: VM((4 * rows, width), BF16) for nm in ("X", "G")})
    scratch.update({nm: VM((rows, heads), F32) for nm in ("ko_v", "gate_in", "keep_out")})
    scratch.update({nm: VM((width, width // heads), BF16) for nm in ("sin_v", "state_a", "state_b")})
    scratch.update({nm: VM((wide, width // wide, width // heads), BF16) for nm in ("arrived", "joined")})
    scratch.update(
        wf=VM((3 * hidden, width), BF16),
        p_v=VM((3 * tall, width), BF16),
        sib=VM((5, rows, half), BF16),
        reach=VM((rows, rows), F32),
        gsum=VM((2, 8, width), F32),
        gains=VM((3 + bits, 8, width), F32),
        grecv=VM((2 + bits, 8, width), F32),
        lsem=dma((40,)),
        csem=dma((14,)),
        ssem=dma((8, wide)),
        stsem=dma((16,)),
        xsem=dma((22, PIECES)),
        usem=dma((11, 4 * (bits + 1) + 4)),
        gsem=dma((4 + 2 * bits,)),
        osem=dma((5,)),
    )
    for name in range(D0, V + 1):
        for step, shape in enumerate(arrivals(name, wide, tall if name < O else width, half)):
            scratch["r", name, step] = VM(shape, BF16)
    return call_kernel(lambda r: main_body(wide, heads, eps, r), "whole_block", 3, ins, outs, scratch, 48 * 10**9)


def widen_body(r):
    jobs = []
    for key, src in r.src.items():
        dst, wide_v, narrow_v = r.dst[key], r.wide_v[key], r.narrow_v[key]
        rows = dst.shape[0]
        size = rows // 4 if rows % 64 == 0 else rows
        for base in range(0, rows, size):
            here = pl.ds(base, size)
            jobs.append((src.at[here], narrow_v.at[here], wide_v.at[here], dst.at[here]))
    reads = [pltpu.make_async_copy(job[0], job[1], r.rsem.at[i]) for i, job in enumerate(jobs)]
    writes = [pltpu.make_async_copy(job[2], job[3], r.wsem.at[i]) for i, job in enumerate(jobs)]
    plain_in = [
        pltpu.make_async_copy(r.gtok, r.gtok_v, r.psem.at[4]),
        pltpu.make_async_copy(r.out, r.out_v, r.psem.at[5]),
    ]
    plain = [
        pltpu.make_async_copy(r.gtok_v, r.gtok_out, r.psem.at[0]),
        pltpu.make_async_copy(r.out_v, r.out_out, r.psem.at[1]),
    ]
    for copy in plain_in + reads:
        copy.start()
    for first, second in zip(plain_in, plain, strict=True):
        first.wait()
        second.start()
    for i in range(2):
        r.gain_v[i] = r.gains[i]
    plain += [pltpu.make_async_copy(r.gain_v.at[i], dst, r.psem.at[2 + i]) for i, dst in enumerate((r.gain0, r.gain1))]
    for copy in plain[2:]:
        copy.start()
    for job, read, write in zip(jobs, reads, writes, strict=True):
        read.wait()
        narrow, wide = job[1], job[2]
        tile = math.gcd(narrow.shape[0], 64)

        @pl.loop(0, narrow.shape[0] // tile)
        def _(i):
            wide[part(i, tile), :] = narrow[part(i, tile), :].astype(F32)

        write.start()
    for copy in writes + plain:
        copy.wait()


def widen(done, hidden):
    keys = [key for key in done if isinstance(key, tuple)]
    rows, width = done["out"].shape
    sds = jax.ShapeDtypeStruct
    high = {key: hidden if key[0] == "f" else width for key in keys}
    names, ins, specs = [], [], []
    for key in keys:
        names.append(("s", key))
        ins.append(done[key])
        specs.append(ANY)
    for name, spec in (("gtok", ANY), ("out", ANY), ("gains", IN_VMEM)):
        names.append(name)
        ins.append(done["out_gain"] if name == "gains" else done[name])
        specs.append(spec)
    outs = {("d", key): sds((high[key], width), F32) for key in keys}
    outs["gtok_out"] = sds((rows, width), F32)
    outs["out_out"] = sds((rows, width), BF16)
    outs["gain0"] = sds((width,), F32)
    outs["gain1"] = sds((width,), F32)
    dma = pltpu.SemaphoreType.DMA
    scratch = {("w", key): pltpu.VMEM((high[key], width), F32) for key in keys}
    scratch.update({("n", key): pltpu.VMEM((high[key], width), BF16) for key in keys})
    scratch.update(gain_v=pltpu.VMEM((2, width), F32), rsem=dma((32,)), wsem=dma((32,)), psem=dma((6,)))
    scratch.update(gtok_v=pltpu.VMEM((rows, width), F32), out_v=pltpu.VMEM((rows, width), BF16))
    names += list(outs) + list(scratch)
    results = pl.pallas_call(
        lambda *refs: widen_body(Refs(names, refs)),
        name="widen",
        out_shape=list(outs.values()),
        in_specs=specs,
        out_specs=[ANY] * len(outs),
        scratch_shapes=list(scratch.values()),
        compiler_params=pltpu.CompilerParams(vmem_limit_bytes=VMEM_BYTES),
    )(*ins)
    return dict(zip(outs, results, strict=True))


def body(
    tokens,
    cotangent,
    lengths,
    decay_rate,
    attn_gain,
    w_query,
    w_key,
    w_value,
    w_gate,
    w_out,
    ffn_gain,
    w_left,
    w_right,
    w_down,
):
    wide = lax.axis_size("wide")
    heads = decay_rate.shape[0]
    hidden = w_down.shape[0]
    shared = dict(
        lens=lengths,
        rate_s=decay_rate,
        rate_row=decay_rate[None],
        fgain=ffn_gain[None],
        again=attn_gain[None],
        wq=w_query,
        wk=w_key,
        wv=w_value,
        wg=w_gate,
        wo=w_out,
        tokens=tokens[0],
        cot=cotangent[0],
    )
    gated = dict(wl=w_left.T, wr=w_right.T, wd=w_down)
    done = main_call(wide, heads, EPS, {**shared, **gated})
    last = widen(done, hidden)
    g_o, g_g, g_q, g_k, g_v = [last["d", ("a", i)] for i in range(5)]
    g_d, g_l, g_r = [last["d", ("f", i)] for i in range(3)]
    return (
        last["out_out"][None],
        last["gtok_out"][None],
        g_q,
        g_k,
        g_v,
        g_g,
        g_o,
        last["gain0"],
        last["gain1"],
        g_l.T,
        g_r.T,
        g_d,
    )


def solution(mesh):
    placed = (
        P("narrow", "wide", None),
        P("narrow", "wide", None),
        P("narrow", None),
        P(),
        P(),
        P(),
        P(),
        P(),
        P(),
        P(),
        P(),
        P(None, "narrow"),
        P(None, "narrow"),
        P("narrow", None),
    )
    return jax.shard_map(
        body,
        mesh=mesh,
        in_specs=placed,
        out_specs=(
            P("narrow", "wide", None),
            P("narrow", "wide", None),
            P(),
            P(),
            P(),
            P(),
            P(),
            P(),
            P(),
            P(None, "narrow"),
            P(None, "narrow"),
            P("narrow", None),
        ),
        check_vma=False,
    )
```
